32 devices in a mesh: dp: 16 (over z, y, core), mp: 2 (over x).
Axes of the slice: x: 2, y: 2, z: 4, core: 2. Of those that a mesh axis runs over, the one named last changes fastest.
Arguments:
- hidden_in: bfloat16 [4096, 2048], P(('dp', 'mp')), may hold values from -6 to 6
- cotangent: bfloat16 [4096, 2048], P(('dp', 'mp')), may hold values from -6 to 6
- norm_gains: float32 [2, 2048], replicated, may hold values from 0.5 to 1.5
- qkv_weight: bfloat16 [3, 2048, 2048], P(None, 'dp', 'mp'), may hold values from -0.125 to 0.125
- qkv_bias: bfloat16 [3, 2048], replicated, may hold values from -3 to 3
- out_weight: bfloat16 [2048, 2048], P('mp', 'dp'), may hold values from -2 to 2
- router_weight: bfloat16 [2048, 16], replicated, may hold values from -0.0625 to 0.0625
- shared_gate_vec: bfloat16 [2048], replicated, may hold values from -0.125 to 0.125
- shared_gate_up: bfloat16 [2, 2048, 5632], P(None, 'dp', 'mp'), may hold values from -0.125 to 0.125
- shared_down: bfloat16 [5632, 2048], P('mp', 'dp'), may hold values from -0.109375 to 0.109375
- expert_gate_up: bfloat16 [16, 2, 2048, 1408], P('dp', None, None, 'mp'), may hold values from -0.125 to 0.125
- expert_down: bfloat16 [16, 1408, 2048], P('dp', 'mp'), may hold values from -6 to 6
- segments: int32 [4096], P('dp'), may hold values from 0 to 4095, as said below
- valid_mask: int32 [4096], P('dp'), may hold values 0 or 1
- routes: int32 [4096, 4], P('dp'), may hold values from 0 to 15, as said below
- slots: int32 [4096, 4], P('dp'), may hold values from 0 to 84, as said below
Outputs:
- output: bfloat16 [4096, 2048], P(('dp', 'mp'))
- input_grad: float32 [4096, 2048], P(('dp', 'mp'))
- grad_norm_gains: float32 [2, 2048], replicated
- grad_qkv_weight: float32 [3, 2048, 2048], P(None, 'dp', 'mp')
- grad_qkv_bias: float32 [3, 2048], replicated
- grad_out_weight: float32 [2048, 2048], P('mp', 'dp')
- grad_router_weight: float32 [2048, 16], replicated
- grad_shared_gate_vec: float32 [2048], replicated
- grad_shared_gate_up: float32 [2, 2048, 5632], P(None, 'dp', 'mp')
- grad_shared_down: float32 [5632, 2048], P('mp', 'dp')
- grad_expert_gate_up: float32 [16, 2, 2048, 1408], P('dp', None, None, 'mp')
- grad_expert_down: float32 [16, 1408, 2048], P('dp', 'mp')
- rms_residual: float32 [], replicated
- rms_attention: float32 [], replicated
- rms_moe: float32 [], replicated
The draws below stay inside these ranges and needn't reach their ends.
Inputs may be any that keep to these rules, and one draw needn't show every extreme that they name: `segments`: each document's number is the position of its first token. Numbers never fall, a new document begins at every multiple of 4096 positions, and the last token begins a document of its own. `routes`: each row names 4 different experts. Among the 256 rows of one index of dp (aligned blocks), no expert is named more than 85 times, and one expert is named exactly 85 times in every block. Within one block of 256 rows, the routes to one expert carry different slots.
All inputs are finite; a program needn't handle non-finite values. No bound on the sum of `valid_mask` on one device may be relied on, other than what follows from the above.
Results may differ from the reference program's by a relative error of at most 0.018.
Values may be sent and summed in bfloat16 or wider, within the bound.
No kernel may reach another device: no remote copies, remote signals or barrier semaphores. Data moves between devices by JAX's collectives and lax.ppermute only.
A program may use at most 448 MiB of HBM per device.

```python
import jax
import jax.numpy as jnp
from jax import lax

D = 2048
HEADS = 16
HEAD = 128
EFF = 1408
SFF = 5632
TOP = 4
SEQ = 4096
WINDOW = 1024
TOK_DP = 256
EXPERTS = 16
TOKENS = 4096
CAP = 85
N_MP = 2


def route_table(key):
    key = jax.random.fold_in(key, 71)
    blocks = TOKENS // TOK_DP
    slot_total = EXPERTS * CAP
    needed = TOK_DP * TOP
    favoured = jax.random.randint(jax.random.fold_in(key, 1), (), 0, EXPERTS)

    def one_block(block_key):
        order_key, token_key = jax.random.split(block_key)
        ordering = jax.random.permutation(order_key, slot_total).astype(jnp.int32)
        ranking = jnp.arange(slot_total, dtype=jnp.int32)
        priority = jnp.where(ordering // CAP == favoured, 0, 1) * slot_total + ranking
        chosen = jnp.sort(ordering[jnp.argsort(priority)][:needed])
        layout = chosen.reshape(TOP, TOK_DP).T
        layout = layout[jax.random.permutation(token_key, TOK_DP)]
        return (layout // CAP, layout % CAP)
    experts_of, slots_of = jax.vmap(one_block)(jax.random.split(jax.random.fold_in(key, 2), blocks))
    return (experts_of.reshape(TOKENS, TOP).astype(jnp.int32), slots_of.reshape(TOKENS, TOP).astype(jnp.int32))


def draw_routes(key, part):
    return route_table(key)[0]


def draw_slots(key, part):
    return route_table(key)[1]


def draw_segments(key, part):
    key = jax.random.fold_in(key, 13)
    position = jnp.arange(TOKENS, dtype=jnp.int32)
    starts = (jax.random.randint(key, (TOKENS,), 0, SEQ // 4) == 0) | (position % SEQ == 0) | (position == TOKENS - 1)
    first_of = jnp.where(starts, position, 0).astype(jnp.int32)
    return lax.cummax(first_of, axis=0).astype(jnp.int32)


def place_ends(values, stream_key, least, top_value):
    extent = values.shape
    spot = [jax.random.randint(jax.random.fold_in(stream_key, axis), (), 0, extent[axis]) for axis in range(len(extent))]
    values = values.at[tuple(spot)].set(least)
    longest = extent.index(max(extent))
    spot[longest] = (spot[longest] + 1) % extent[longest]
    return values.at[tuple(spot)].set(top_value)


def steps_of(key, dims, shards, smallest, high):
    def one(axis_at, blocks):
        heights = jax.random.uniform(jax.random.fold_in(jax.random.fold_in(key, 6), axis_at), (blocks,), jnp.float32, smallest / len(shards), high / len(shards))
        return jnp.repeat(jnp.exp(heights), dims[axis_at] // blocks).reshape((-1,) + (1,) * (len(dims) - axis_at - 1))

    loudness = one(*shards[0])
    for cut in shards[1:]:
        loudness = loudness * one(*cut)
    return loudness


def normal_values(stream_key, dims, scale, limit, cuts=(), kind=jnp.bfloat16):
    factor_of = steps_of(stream_key, dims, cuts, -0.22, 0.18) if cuts else 1.0
    result = jax.random.normal(stream_key, dims, jnp.float32) * scale * factor_of
    return jnp.minimum(jnp.maximum(result, -limit), limit).astype(kind)


def setup_inputs(seed: int = 0) -> dict:
    splits = jax.random.split(jax.random.key(seed), 17)
    return {
        "hidden_in": normal_values(splits[0], (TOKENS, D), 1.0, 6.0, ((0, 32),)),
        "cotangent": normal_values(splits[1], (TOKENS, D), 1.0, 6.0, ((0, 32),)),
        "norm_gains": jnp.clip(1.0 + 0.1 * jax.random.normal(splits[2], (2, D), jnp.float32), 0.5, 1.5),
        "qkv_weight": normal_values(splits[3], (3, D, D), D ** -0.5, 0.125, ((1, 16), (2, 2))),
        "qkv_bias": normal_values(splits[4], (3, D), 0.5, 3.0),
        "out_weight": normal_values(splits[5], (D, D), (max(D // 256, 1)) ** -0.5, 2.0, ((0, 2), (1, 16))),
        "router_weight": normal_values(splits[6], (D, EXPERTS), (4 * D) ** -0.5, 0.0625),
        "shared_gate_vec": normal_values(splits[7], (D,), D ** -0.5, 0.125),
        "shared_gate_up": normal_values(splits[8], (2, D, SFF), D ** -0.5, 0.125, ((1, 16), (2, 2))),
        "shared_down": normal_values(splits[9], (SFF, D), (SFF // 2) ** -0.5, 0.109375, ((0, 2), (1, 16))),
        "expert_gate_up": normal_values(splits[10], (EXPERTS, 2, D, EFF), D ** -0.5, 0.125, ((0, 16), (3, 2))),
        "expert_down": normal_values(splits[11], (EXPERTS, EFF, D), 1.0, 6.0, ((0, 16), (1, 2))),
        "segments": draw_segments(jax.random.fold_in(splits[16], 71), 0),
        "valid_mask": place_ends((jax.random.randint(splits[13], (TOKENS,), 0, 8) < 7).astype(jnp.int32), jax.random.fold_in(splits[13], 1), 0, 1),
        "routes": draw_routes(jax.random.fold_in(splits[16], 71), 0),
        "slots": draw_slots(jax.random.fold_in(splits[16], 71), 0),
    }


HIGHEST = lax.Precision.HIGHEST
EPSILON = 1e-06
ROPE_BASE = 1000000.0
MASKED = -1e+30

@jax.custom_vjp
def low(v):
    return lax.optimization_barrier(v.astype(jnp.bfloat16)).astype(jnp.float32)

@jax.custom_vjp
def low_back(v):
    return v

def low_keep(v):
    return (low(v), None)

def low_pass(kept, grad):
    return (grad,)

def back_keep(v):
    return (v, None)

def back_low(kept, grad):
    return (low(grad),)
low.defvjp(low_keep, low_pass)
low_back.defvjp(back_keep, back_low)

def rope_tables(row_count, head_size):
    placing = jnp.arange(row_count, dtype=jnp.int32) % SEQ
    frequency = ROPE_BASE ** (-(jnp.arange(head_size // 2, dtype=jnp.float32) * 2.0 / head_size))
    angles = placing.astype(jnp.float32)[:, None] * frequency[None, :]
    return (jnp.cos(angles), jnp.sin(angles))

def rotate(vector, cos_table, sin_table):
    half_size = vector.shape[-1] // 2
    first_half = vector[..., :half_size]
    second_half = vector[..., half_size:]
    cosine = cos_table[:, None, :]
    sine_part = sin_table[:, None, :]
    return jnp.concatenate([first_half * cosine - second_half * sine_part, second_half * cosine + first_half * sine_part], axis=-1)

def rms_norm(rows_in, gain):
    return rows_in * lax.rsqrt(lax.optimization_barrier(jnp.mean(rows_in * rows_in, axis=-1, keepdims=True)) + EPSILON) * gain

def swish(gate_in):
    return gate_in * jax.nn.sigmoid(gate_in)

def softmax_rows(logits):
    highest = lax.optimization_barrier(jnp.max(logits, axis=-1, keepdims=True))
    powers = jnp.exp(logits - highest)
    return powers / lax.optimization_barrier(jnp.sum(powers, axis=-1, keepdims=True))

def attend(queries, key_rows, values, segments, valid_mask):
    blocks = min(512, SEQ)
    block_count = TOKENS // blocks
    padding = jnp.zeros((WINDOW, HEADS, HEAD), queries.dtype)
    keys_pad = jnp.concatenate([padding, key_rows], 0)
    values_pad = jnp.concatenate([padding, values], 0)
    segs_pad = jnp.concatenate([jnp.full((WINDOW,), -1, jnp.int32), segments.astype(jnp.int32)], 0)
    valid_pad = jnp.concatenate([jnp.zeros((WINDOW,), jnp.int32), valid_mask.astype(jnp.int32)], 0)
    score_scale = HEAD ** (-0.5)

    def one_block(block_index):
        first_row = (block_index * blocks).astype(jnp.int32)
        query_block = lax.dynamic_slice_in_dim(queries, first_row, blocks, 0)
        key_block = lax.dynamic_slice_in_dim(keys_pad, first_row, blocks + WINDOW, 0)
        value_block = lax.dynamic_slice_in_dim(values_pad, first_row, blocks + WINDOW, 0)
        query_segs = lax.dynamic_slice_in_dim(segments.astype(jnp.int32), first_row, blocks, 0)
        key_segs = lax.dynamic_slice_in_dim(segs_pad, first_row, blocks + WINDOW, 0)
        key_valid = lax.dynamic_slice_in_dim(valid_pad, first_row, blocks + WINDOW, 0)
        distance = jnp.arange(blocks, dtype=jnp.int32)[:, None] + WINDOW - jnp.arange(blocks + WINDOW, dtype=jnp.int32)[None, :]
        allowed = (distance >= 0) & (distance < WINDOW) & (query_segs[:, None] == key_segs[None, :]) & ((key_valid[None, :] == 1) | (distance == 0))
        scores = low_back(jnp.einsum('qhd,khd->hqk', query_block, key_block, precision=HIGHEST) * score_scale)
        scores = jnp.where(allowed[None], scores, MASKED)
        weights = softmax_rows(scores)
        return jnp.einsum('hqk,khd->qhd', low(weights), value_block, precision=HIGHEST)
    results = lax.map(jax.checkpoint(one_block), jnp.arange(block_count, dtype=jnp.int32))
    return results.reshape(TOKENS, HEADS, HEAD)

def experts(normed, routes, slots, gate_up, down):
    blocks = TOKENS // TOK_DP
    owner_block = jnp.arange(TOKENS, dtype=jnp.int32) // TOK_DP
    slot_index = (routes * (blocks * CAP) + owner_block[:, None] * CAP + slots).reshape(-1).astype(jnp.int32)
    copies = jnp.broadcast_to(normed[:, None, :], (TOKENS, TOP, D)).reshape(TOKENS * TOP, D)
    expert_rows = jnp.zeros((EXPERTS * blocks * CAP, D), normed.dtype).at[slot_index].set(copies)
    expert_rows = expert_rows.reshape(EXPERTS, blocks * CAP, D)
    gate_up_out = low_back(jnp.einsum('erd,ejdf->ejrf', expert_rows, gate_up, precision=HIGHEST))
    hidden = low(swish(gate_up_out[:, 0]) * gate_up_out[:, 1])
    hidden_parts = hidden.reshape(EXPERTS, blocks * CAP, N_MP, EFF // N_MP)
    down_parts = down.reshape(EXPERTS, N_MP, EFF // N_MP, D)
    returned = low(low_back(jnp.einsum('erpf,epfd->erpd', hidden_parts, down_parts, precision=HIGHEST)))
    returned = lax.optimization_barrier(jnp.sum(returned, axis=2)).reshape(EXPERTS * blocks * CAP, D)
    return returned[slot_index].reshape(TOKENS, TOP, D)

def forward(hidden_in, norm_gains, qkv_weight, qkv_bias, out_weight, router_weight, shared_gate_vec, shared_gate_up, shared_down, expert_gate_up, expert_down, segments, valid_mask, routes, slots):
    cos_table, sin_table = rope_tables(TOKENS, HEAD)
    normed_attn = low(rms_norm(hidden_in, norm_gains[0]))
    projected = low_back(jnp.einsum('td,jdc->jtc', normed_attn, qkv_weight, precision=HIGHEST) + qkv_bias[:, None, :])
    head_shape = (TOKENS, HEADS, HEAD)
    queries = low(rotate(projected[0].reshape(head_shape), cos_table, sin_table))
    key_rows = low(rotate(projected[1].reshape(head_shape), cos_table, sin_table))
    values = low(projected[2].reshape(head_shape))
    attended = low(low_back(attend(queries, key_rows, values, segments, valid_mask).reshape(TOKENS, D)))
    attn_out = low_back(jnp.dot(attended, out_weight, precision=HIGHEST))
    middle = hidden_in + attn_out
    normed_moe = low(rms_norm(middle, norm_gains[1]))
    router_probs = softmax_rows(jnp.dot(normed_moe, router_weight, precision=HIGHEST))
    one_hot = (routes[:, :, None] == jnp.arange(EXPERTS, dtype=jnp.int32)[None, None, :]).astype(router_probs.dtype)
    gate_probs = jnp.einsum('tke,te->tk', one_hot, router_probs, precision=HIGHEST)
    picked = experts(normed_moe, routes, slots, expert_gate_up, expert_down)
    shared_in = low_back(jnp.einsum('td,jdf->jtf', normed_moe, shared_gate_up, precision=HIGHEST))
    shared_hidden = low(swish(shared_in[0]) * shared_in[1])
    shared_out = low_back(jnp.dot(shared_hidden, shared_down, precision=HIGHEST))
    shared_gate = jax.nn.sigmoid(jnp.dot(normed_moe, shared_gate_vec, precision=HIGHEST))
    moe_out = low_back(jnp.einsum('tk,tkd->td', gate_probs, picked, precision=HIGHEST) + shared_gate[:, None] * shared_out)
    return (middle + moe_out, attn_out, moe_out)

def reference(hidden_in, cotangent, norm_gains, qkv_weight, qkv_bias, out_weight, router_weight, shared_gate_vec, shared_gate_up, shared_down, expert_gate_up, expert_down, segments, valid_mask, routes, slots):
    params = tuple((array.astype(jnp.float32) for array in (hidden_in, norm_gains, qkv_weight, qkv_bias, out_weight, router_weight, shared_gate_vec, shared_gate_up, shared_down, expert_gate_up, expert_down)))

    def forward_of(*inputs):
        return forward(*inputs, segments, valid_mask, routes, slots)
    (output, attn_out, moe_out), pullback = jax.vjp(forward_of, *params)
    gradients = pullback((cotangent.astype(jnp.float32), jnp.zeros_like(attn_out), jnp.zeros_like(moe_out)))
    weight = valid_mask.astype(jnp.float32)[:, None]
    valid_count = jnp.maximum(jnp.sum(weight), 1.0)

    def spread(rows_in):
        return jnp.sqrt(jnp.sum(weight * rows_in * rows_in) / (valid_count * D))
    return (output.astype(jnp.bfloat16), gradients[0], gradients[1], gradients[2], gradients[3], gradients[4], gradients[5], gradients[6], gradients[7], gradients[8], gradients[9], gradients[10], spread(params[0]), spread(attn_out), spread(moe_out))
```

```python
import functools

import jax
import jax.numpy as jnp
from jax import lax
from jax.experimental import pallas as pl
from jax.experimental.pallas import tpu as pltpu
from jax.sharding import Mesh
from jax.sharding import PartitionSpec as P

HEAD = 128
SEQ = 4096
WINDOW = 1024

EPSILON = 1e-06
ROPE_BASE = 1000000.0
MASKED = -1e30

LINE = 4
GROUP = ("z", "y", "c")
EVERY = ("g", "z", "y", "c", "x")
SWAP = [(0, 1), (1, 0)]
ORDERS = (("x", "y", "z"), ("y", "z", "x"), ("z", "x", "y"))
VMEM_LIMIT = 56 * 1024 * 1024

F32 = jnp.float32
BF16 = jnp.bfloat16


def swap(value, axis):
    return lax.ppermute(value, axis, SWAP)


def pair_gather(value, axis):
    index = lax.axis_index(axis)
    other = swap(value, axis)
    return jnp.where(index == 0, jnp.stack([value, other]), jnp.stack([other, value]))


def line_gather(value, axis):
    index = lax.axis_index(axis)
    up = [(k, k + 1) for k in range(LINE - 1)]
    down = [(k + 1, k) for k in range(LINE - 1)]
    below, above = [], []
    rising = falling = value
    for step in range(1, LINE):
        rising = lax.ppermute(rising, axis, up[step - 1 :])
        falling = lax.ppermute(falling, axis, down[: LINE - step])
        below.append(rising)
        above.append(falling)
    placed = []
    for slot in range(LINE):
        block = value
        for here in range(LINE):
            if here != slot:
                source = below[here - slot - 1] if slot < here else above[slot - here - 1]
                block = jnp.where(index == here, source, block)
        placed.append(block)
    return jnp.stack(placed)


def gather_axis(value, axis):
    return line_gather(value, axis) if axis == "z" else pair_gather(value, axis)


def take(value, index, dim):
    return lax.dynamic_index_in_dim(value, index, dim, keepdims=False)


def pair_scatter(value, axis, dim):
    index = lax.axis_index(axis)
    other = swap(take(value, 1 - index, dim), axis)
    return take(value, index, dim).astype(F32) + other.astype(F32)


def line_scatter(value, axis, dim):
    index = lax.axis_index(axis)
    up = [(k, k + 1) for k in range(LINE - 1)]
    down = [(k + 1, k) for k in range(LINE - 1)]
    rising = falling = None
    for step in range(1, LINE):
        going_up = take(value, jnp.minimum(index + LINE - step, LINE - 1), dim)
        going_down = take(value, jnp.maximum(index - (LINE - step), 0), dim)
        if step > 1:
            going_up = (going_up.astype(F32) + rising.astype(F32)).astype(value.dtype)
            going_down = (going_down.astype(F32) + falling.astype(F32)).astype(value.dtype)
        rising = lax.ppermute(going_up, axis, up[:step])
        falling = lax.ppermute(going_down, axis, down[LINE - 1 - step :])
    return take(value, index, dim).astype(F32) + rising.astype(F32) + falling.astype(F32)


def scatter_axis(value, axis, dim):
    return line_scatter(value, axis, dim) if axis == "z" else pair_scatter(value, axis, dim)


def cuts_of(rows):
    unit = rows // 8
    return (0, 2 * unit, 5 * unit, rows)


def gather_group(shard):
    rows, width = shard.shape
    cuts = cuts_of(rows)
    pieces = []
    for piece, order in enumerate(ORDERS):
        value = shard[cuts[piece] : cuts[piece + 1]]
        axes = []
        for axis in order + ("c",):
            value = gather_axis(value, axis)
            axes.insert(0, axis)
        turned = [axes.index(axis) for axis in ("z", "y", "c", "x")]
        value = value.transpose(*turned, 4, 5)
        pieces.append(value.reshape(8 * LINE, cuts[piece + 1] - cuts[piece], width))
    return jnp.concatenate(pieces, 1).reshape(8 * LINE * rows, width)


def scatter_group(partial_rows):
    total, width = partial_rows.shape
    rows = total // (8 * LINE)
    cuts = cuts_of(rows)
    whole = partial_rows.reshape(LINE, 2, 2, 2, rows, width)
    pieces = []
    for piece, order in enumerate(ORDERS):
        value = whole[:, :, :, :, cuts[piece] : cuts[piece + 1]]
        axes = ["z", "y", "c", "x"]
        for axis in ("c",) + order[::-1]:
            dim = axes.index(axis)
            value = scatter_axis(value, axis, dim)
            axes.pop(dim)
            if axes:
                value = value.astype(BF16)
        pieces.append(value)
    return jnp.concatenate(pieces, 0)


def gather_plane(shard):
    rows, width = shard.shape
    half = rows // 2
    pieces = []
    for piece, order in enumerate((("x", "y"), ("y", "x"))):
        value = shard[piece * half : (piece + 1) * half]
        for axis in order:
            value = pair_gather(value, axis)
        if piece == 0:
            value = pair_gather(value, "c").transpose(1, 0, 2, 3, 4)
        else:
            value = pair_gather(value, "c").transpose(2, 0, 1, 3, 4)
        pieces.append(value.reshape(8, half, width))
    return jnp.concatenate(pieces, 1).reshape(8 * rows, width)


def scatter_plane(partial_rows):
    total, width = partial_rows.shape
    rows = total // 8
    half = rows // 2
    whole = partial_rows.reshape(2, 2, 2, rows, width)
    pieces = []
    for piece, order in enumerate((("y", "x"), ("x", "y"))):
        value = whole[:, :, :, piece * half : (piece + 1) * half]
        axes = ["y", "c", "x"]
        for axis in ("c",) + order:
            dim = axes.index(axis)
            value = pair_scatter(value, axis, dim)
            axes.pop(dim)
            if axes:
                value = value.astype(BF16)
        pieces.append(value)
    return jnp.concatenate(pieces, 0)


def exchange(value, axes):
    return lax.all_to_all(value, axes, split_axis=0, concat_axis=0, tiled=True)


def turn(value, cosine, sine):
    return value * cosine + pltpu.roll(value, HEAD // 2, 1) * sine


def turn_back(value, cosine, sine):
    return value * cosine - pltpu.roll(value, HEAD // 2, 1) * sine


def project_kernel(heads, rows_ref, weight_ref, bias_ref, cos_ref, sin_ref, out_ref):
    projected = (
        jnp.dot(rows_ref[...], weight_ref[...], preferred_element_type=F32) + bias_ref[...]
    )
    for part in range(3 * heads):
        block = projected[:, part * HEAD : (part + 1) * HEAD]
        if part < 2 * heads:
            block = turn(block, cos_ref[...], sin_ref[...])
        out_ref[:, part * HEAD : (part + 1) * HEAD] = block.astype(BF16)


def project(rows, weight, bias, cosine, sine):
    count, model = rows.shape
    width = weight.shape[1]
    step = count // 4
    return pl.pallas_call(
        functools.partial(project_kernel, width // (3 * HEAD)),
        grid=(4,),
        in_specs=[
            pl.BlockSpec((step, model), lambda i: (i, 0)),
            pl.BlockSpec((model, width), lambda i: (0, 0)),
            pl.BlockSpec((1, width), lambda i: (0, 0)),
            pl.BlockSpec((step, HEAD), lambda i: (i, 0)),
            pl.BlockSpec((step, HEAD), lambda i: (i, 0)),
        ],
        out_specs=pl.BlockSpec((step, width), lambda i: (i, 0)),
        out_shape=jax.ShapeDtypeStruct((count, width), BF16),
        compiler_params=pltpu.CompilerParams(vmem_limit_bytes=VMEM_LIMIT),
        cost_estimate=pl.CostEstimate(
            flops=2 * count * model * width,
            bytes_accessed=2 * (count * model + model * width + count * width),
            transcendentals=0,
        ),
        name="project",
    )(rows, weight, bias, cosine, sine)


def block_probs(query, keys, seg_q, seg_k, valid_k, first, reach):
    rows, span = query.shape[0], keys.shape[0]
    scores = lax.dot_general(query, keys, (((1,), (1,)), ((), ())), preferred_element_type=F32)
    scores = scores * (HEAD ** (-0.5))
    distance = (
        reach
        + lax.broadcasted_iota(jnp.int32, (rows, span), 0)
        - lax.broadcasted_iota(jnp.int32, (rows, span), 1)
    )
    allowed = (
        (distance >= 0)
        & (distance < WINDOW)
        & (seg_q == seg_k)
        & ((valid_k == 1) | (distance == 0))
    )
    scores = jnp.where(allowed, scores, MASKED)
    powers = jnp.exp(scores - jnp.max(scores, axis=-1, keepdims=True))
    return powers / jnp.sum(powers, axis=-1, keepdims=True)


def attend_kernel(step, reach, q_ref, k_ref, v_ref, segq_ref, segk_ref, valid_ref, out_ref):
    first = pl.multiple_of(pl.program_id(1) * step, step)
    span = pl.ds(first, step + reach)
    probs = block_probs(
        q_ref[...], k_ref[span, :], segq_ref[...], segk_ref[:, span], valid_ref[:, span], first, reach
    )
    out_ref[...] = jnp.dot(
        probs.astype(BF16), v_ref[span, :], preferred_element_type=F32
    ).astype(BF16)


def attend(queries, keys, values, seg_q, seg_k, valid_k):
    count, width = queries.shape
    held = keys.shape[0]
    reach = held - count
    step = count // 4
    heads = width // HEAD
    flops = 4 * count * (step + reach) * width
    return pl.pallas_call(
        functools.partial(attend_kernel, step, reach),
        grid=(heads, 4),
        in_specs=[
            pl.BlockSpec((step, HEAD), lambda h, i: (i, h)),
            pl.BlockSpec((held, HEAD), lambda h, i: (0, h)),
            pl.BlockSpec((held, HEAD), lambda h, i: (0, h)),
            pl.BlockSpec((step, 1), lambda h, i: (i, 0)),
            pl.BlockSpec((1, held), lambda h, i: (0, 0)),
            pl.BlockSpec((1, held), lambda h, i: (0, 0)),
        ],
        out_specs=pl.BlockSpec((step, HEAD), lambda h, i: (i, h)),
        out_shape=jax.ShapeDtypeStruct((count, width), BF16),
        compiler_params=pltpu.CompilerParams(vmem_limit_bytes=VMEM_LIMIT),
        cost_estimate=pl.CostEstimate(
            flops=flops, bytes_accessed=8 * held * width, transcendentals=flops // (4 * HEAD)
        ),
        name="attend",
    )(queries, keys, values, seg_q, seg_k, valid_k)


def attend_back_kernel(
    step, reach, q_ref, k_ref, v_ref, g_ref, segq_ref, segk_ref, valid_ref, cos_ref, sin_ref,
    dq_ref, dk_ref, dv_ref,
):
    block = pl.program_id(1)
    first = pl.multiple_of(block * step, step)
    span = pl.ds(first, step + reach)

    @pl.when(block == 0)
    def _():
        dk_ref[...] = jnp.zeros_like(dk_ref)
        dv_ref[...] = jnp.zeros_like(dv_ref)

    query, keys, grad = q_ref[...], k_ref[span, :], g_ref[...]
    probs = block_probs(
        query, keys, segq_ref[...], segk_ref[:, span], valid_ref[:, span], first, reach
    )
    g_probs = lax.dot_general(
        grad, v_ref[span, :], (((1,), (1,)), ((), ())), preferred_element_type=F32
    )
    inner = jnp.sum(probs * g_probs, axis=-1, keepdims=True)
    g_scores = (probs * (g_probs - inner)).astype(BF16)
    scale = HEAD ** (-0.5)
    dq = jnp.dot(g_scores, keys, preferred_element_type=F32) * scale
    here = pl.ds(pl.multiple_of(first + reach, step), step)
    dq_ref[...] = turn_back(dq, cos_ref[here, :], sin_ref[here, :]).astype(BF16)
    dk_ref[span, :] += (
        lax.dot_general(g_scores, query, (((0,), (0,)), ((), ())), preferred_element_type=F32)
        * scale
    )
    dv_ref[span, :] += lax.dot_general(
        probs.astype(BF16), grad, (((0,), (0,)), ((), ())), preferred_element_type=F32
    )

    @pl.when(block == pl.num_programs(1) - 1)
    def _():
        dk_ref[...] = turn_back(dk_ref[...], cos_ref[...], sin_ref[...])


def attend_back(queries, keys, values, grad, seg_q, seg_k, valid_k, cosine, sine):
    count, width = queries.shape
    held = keys.shape[0]
    reach = held - count
    step = count // 4
    heads = width // HEAD
    flops = 10 * count * (step + reach) * width
    head_rows = pl.BlockSpec((step, HEAD), lambda h, i: (i, h))
    head_all = pl.BlockSpec((held, HEAD), lambda h, i: (0, h))
    return pl.pallas_call(
        functools.partial(attend_back_kernel, step, reach),
        grid=(heads, 4),
        in_specs=[
            head_rows,
            head_all,
            head_all,
            head_rows,
            pl.BlockSpec((step, 1), lambda h, i: (i, 0)),
            pl.BlockSpec((1, held), lambda h, i: (0, 0)),
            pl.BlockSpec((1, held), lambda h, i: (0, 0)),
            pl.BlockSpec((held, HEAD), lambda h, i: (0, 0)),
            pl.BlockSpec((held, HEAD), lambda h, i: (0, 0)),
        ],
        out_specs=[head_rows, head_all, head_all],
        out_shape=[
            jax.ShapeDtypeStruct((count, width), BF16),
            jax.ShapeDtypeStruct((held, width), F32),
            jax.ShapeDtypeStruct((held, width), F32),
        ],
        compiler_params=pltpu.CompilerParams(vmem_limit_bytes=VMEM_LIMIT),
        cost_estimate=pl.CostEstimate(
            flops=flops, bytes_accessed=24 * held * width, transcendentals=flops // (10 * HEAD)
        ),
        name="attend_back",
    )(queries, keys, values, grad, seg_q, seg_k, valid_k, cosine, sine)


def combine_kernel(hidden_ref, weight_ref, place_ref, rows_ref, out_ref):
    own = jnp.dot(hidden_ref[...], weight_ref[...], preferred_element_type=F32)
    routed = lax.dot_general(
        place_ref[0], rows_ref[0], (((0,), (0,)), ((), ())), preferred_element_type=F32
    )
    out_ref[...] = (own + routed).astype(BF16)


def combine(hidden, weight, place, rows):
    count, inner = hidden.shape
    model = weight.shape[1]
    blocks, slots, step = place.shape
    return pl.pallas_call(
        combine_kernel,
        grid=(blocks,),
        in_specs=[
            pl.BlockSpec((step, inner), lambda i: (i, 0)),
            pl.BlockSpec((inner, model), lambda i: (0, 0)),
            pl.BlockSpec((1, slots, step), lambda i: (i, 0, 0)),
            pl.BlockSpec((1, slots, model), lambda i: (i, 0, 0)),
        ],
        out_specs=pl.BlockSpec((step, model), lambda i: (i, 0)),
        out_shape=jax.ShapeDtypeStruct((count, model), BF16),
        compiler_params=pltpu.CompilerParams(vmem_limit_bytes=VMEM_LIMIT),
        cost_estimate=pl.CostEstimate(
            flops=2 * count * model * (inner + slots),
            bytes_accessed=2 * (count * model + count * inner + blocks * slots * model),
            transcendentals=0,
        ),
        name="combine",
    )(hidden, weight, place, rows)


def norm_scale(rows_in):
    return lax.rsqrt(jnp.mean(rows_in * rows_in, axis=-1, keepdims=True) + EPSILON)


def norm_back(rows_in, scaling, gain, grad):
    unit_rows = rows_in * scaling
    grad_unit = grad * gain
    return scaling * (
        grad_unit - unit_rows * jnp.mean(grad_unit * unit_rows, axis=-1, keepdims=True)
    )


def swish(gate_in):
    return gate_in * jax.nn.sigmoid(gate_in)


def swish_back(gate_in, up_in, grad):
    sigma = jax.nn.sigmoid(gate_in)
    grad_gate = grad * up_in * sigma * (1.0 + gate_in * (1.0 - sigma))
    return (grad_gate, grad * gate_in * sigma)


def rope_tables(first_row, row_count):
    placing = (first_row + jnp.arange(row_count, dtype=jnp.int32)) % SEQ
    frequency = ROPE_BASE ** (-(jnp.arange(HEAD // 2, dtype=F32) * 2.0 / HEAD))
    angles = placing.astype(F32)[:, None] * frequency[None, :]
    cosine, sine = jnp.cos(angles), jnp.sin(angles)
    return (
        jnp.concatenate([cosine, cosine], 1),
        jnp.concatenate([-sine, sine], 1),
    )


def per_device(
    hidden_in,
    cotangent,
    norm_gains,
    qkv_weight,
    qkv_bias,
    out_weight,
    router_weight,
    shared_gate_vec,
    shared_gate_up,
    shared_down,
    expert_gate_up,
    expert_down,
    segments,
    valid_mask,
    routes,
    slots,
):
    groups = lax.axis_size("g")
    blocks = segments.shape[0]
    rows_here, model = hidden_in.shape
    weight_rows, local_cols = qkv_weight.shape[1:]
    shared_cols = shared_gate_up.shape[2]
    experts = router_weight.shape[1]
    in_group = 4 * LINE
    cols = local_cols // 4
    hidden_own = shared_cols // in_group
    expert_cols = expert_down.shape[1]
    capacity = -(-(blocks * routes.shape[1] * 4 // (3 * experts)) // 16) * 16
    plane_rows = 4 * blocks
    group_rows = in_group * blocks
    z, y, c, x = (lax.axis_index(axis) for axis in ("z", "y", "c", "x"))
    g = lax.axis_index("g")
    expert = ((g * LINE + z) * 2 + y) * 2 + c

    numbers = jnp.concatenate([segments[None], valid_mask[None], routes.T, slots.T], 0)
    numbers = lax.all_gather(numbers, ("g",) + GROUP, axis=0)
    top = routes.shape[1]

    residual = hidden_in.astype(F32)
    gain_attn, gain_moe = norm_gains[0], norm_gains[1]
    scale_attn = norm_scale(residual)
    rows_attn = gather_plane((residual * scale_attn * gain_attn).astype(BF16))
    qkv_cut = (
        qkv_weight.reshape(3, weight_rows, 4, cols)
        .transpose(2, 1, 0, 3)
        .reshape(4, weight_rows, 3 * cols)
    )
    w_qkv = exchange(qkv_cut, ("y", "c")).reshape(4 * weight_rows, 3 * cols)
    w_qkv = lax.all_gather(w_qkv, ("g", "z"), axis=0, tiled=True)
    w_out = lax.all_gather(out_weight.T, ("x", "g") + GROUP, axis=0, tiled=True)
    w_out = w_out.reshape(2, model, local_cols)
    shared_cut = jnp.concatenate(
        [
            shared_gate_up[0].reshape(weight_rows, in_group, hidden_own),
            shared_gate_up[1].reshape(weight_rows, in_group, hidden_own),
            shared_down.T.reshape(weight_rows, in_group, hidden_own),
        ],
        2,
    ).transpose(1, 0, 2)
    w_shared = exchange(shared_cut, GROUP).reshape(in_group * weight_rows, 3 * hidden_own)
    w_shared = lax.all_gather(w_shared, "g", axis=0, tiled=True) if groups > 1 else w_shared

    here = x * local_cols + (y * 2 + c) * cols
    bias = lax.dynamic_slice_in_dim(qkv_bias, here, cols, 1).astype(F32).reshape(1, 3 * cols)
    cosine, sine = rope_tables((z + LINE - 1) * plane_rows, 2 * plane_rows)
    projected = project(rows_attn, w_qkv, bias, cosine[plane_rows:], sine[plane_rows:])
    queries = projected[:, :cols]
    ahead = [(k, k + 1) for k in range(LINE - 1)]
    key_value = projected[:, cols:]
    before = lax.ppermute(key_value, "z", ahead)
    key_value = jnp.concatenate([before, key_value], 0)
    keys, values = key_value[:, :cols], key_value[:, cols:]
    group_numbers = lax.dynamic_slice_in_dim(numbers, g * in_group, in_group, 0)
    padded = jnp.concatenate([jnp.full((4, 2, blocks), -1, jnp.int32), group_numbers[:, :2]], 0)
    near = lax.dynamic_slice_in_dim(padded, z * 4, 8, 0)
    seg_k = near[:, 0].reshape(1, 2 * plane_rows)
    valid_k = near[:, 1].reshape(1, 2 * plane_rows)
    seg_q = near[4:, 0].reshape(plane_rows, 1)
    attended = attend(queries, keys, values, seg_q, seg_k, valid_k)
    leaving = attended.reshape(2, 2, 2, rows_here, cols).transpose(2, 0, 1, 3, 4)
    arrived = exchange(leaving.reshape(8, rows_here, cols), ("x", "y", "c"))
    attn_flat = arrived.reshape(2, 4, rows_here, cols).transpose(0, 2, 1, 3)
    attn_flat = attn_flat.reshape(2, rows_here, local_cols)
    attn_rows = jnp.einsum("xtc,xdc->td", attn_flat, w_out, preferred_element_type=F32)
    middle = residual + attn_rows
    scale_moe = norm_scale(middle)
    own_moe = (middle * scale_moe * gain_moe).astype(BF16)

    rows_moe = gather_group(own_moe)
    rows_grad = gather_group(cotangent)
    if groups > 1:
        all_moe = lax.all_gather(rows_moe, "g", axis=0, tiled=True)
        all_grad = lax.all_gather(rows_grad, "g", axis=0, tiled=True)
    else:
        all_moe, all_grad = rows_moe, rows_grad
    block_count = numbers.shape[0]

    shared_gu = w_shared[:, : 2 * hidden_own]
    shared_dn = w_shared[:, 2 * hidden_own :]
    gate_vec = shared_gate_vec.astype(F32)
    small = jnp.concatenate([router_weight, shared_gate_vec[:, None]], 1)
    shared_in = jnp.dot(rows_moe, shared_gu, preferred_element_type=F32)
    shared_raw = jnp.dot(rows_grad, shared_dn, preferred_element_type=F32)
    logits_all = jnp.dot(all_moe, small, preferred_element_type=F32)
    router_all = jax.nn.softmax(logits_all[:, :experts], axis=-1)
    picks_here = jnp.arange(experts, dtype=jnp.int32)[None, :] == expert
    gate_all = jnp.sum(jnp.where(picks_here, router_all, 0.0), axis=-1)
    shared_gate = jax.nn.sigmoid(
        lax.dynamic_slice_in_dim(logits_all[:, experts], g * group_rows, group_rows, 0)
    )
    sh_gate, sh_up = shared_in[:, :hidden_own], shared_in[:, hidden_own:]
    shared_hidden = swish(sh_gate) * sh_up
    scaled_hidden = (shared_gate[:, None] * shared_hidden).astype(BF16)
    grad_hidden = shared_gate[:, None] * shared_raw
    signal_part = jnp.sum(shared_hidden * grad_hidden, axis=-1) * (1.0 - shared_gate)
    grad_shared_in = jnp.concatenate(swish_back(sh_gate, sh_up, grad_hidden), 1).astype(BF16)

    slot_here = jnp.max(jnp.where(numbers[:, 2 : 2 + top] == expert, numbers[:, 2 + top :], -1), 1)
    chosen = slot_here[:, None, :] == jnp.arange(capacity, dtype=jnp.int32)[None, :, None]
    place = chosen.astype(BF16)
    gate_blocks = gate_all.reshape(block_count, 1, blocks)
    gate_rows = jnp.sum(jnp.where(chosen, gate_blocks, 0.0), axis=-1).reshape(-1, 1)

    def to_rows(tokens):
        picked = jnp.einsum(
            "bst,btd->bsd",
            place,
            tokens.reshape(block_count, blocks, model),
            preferred_element_type=BF16,
        )
        return picked.reshape(block_count * capacity, model)

    expert_in = to_rows(all_moe)
    expert_grad = to_rows(all_grad)
    w_gate, w_up, w_down = expert_gate_up[0, 0], expert_gate_up[0, 1], expert_down[0]
    ex_gate = jnp.dot(expert_in, w_gate, preferred_element_type=F32)
    ex_up = jnp.dot(expert_in, w_up, preferred_element_type=F32)
    ex_raw = jnp.einsum("rd,fd->rf", expert_grad, w_down, preferred_element_type=F32)
    expert_hidden = swish(ex_gate) * ex_up
    scaled_expert = (gate_rows * expert_hidden).astype(BF16)
    gate_grad_rows = jnp.sum(expert_hidden * ex_raw, axis=-1)
    grad_ex_gate, grad_ex_up = swish_back(ex_gate, ex_up, gate_rows * ex_raw)
    grad_ex_gate, grad_ex_up = grad_ex_gate.astype(BF16), grad_ex_up.astype(BF16)
    grad_rows = jnp.einsum("rf,df->rd", grad_ex_gate, w_gate, preferred_element_type=F32)
    grad_rows = grad_rows + jnp.einsum("rf,df->rd", grad_ex_up, w_up, preferred_element_type=F32)
    grad_rows = grad_rows.astype(BF16).reshape(block_count, capacity, model)

    gate_grad = jnp.sum(
        jnp.where(chosen, gate_grad_rows.reshape(block_count, capacity, 1), 0.0), axis=1
    ).reshape(-1)
    signal_all = signal_part
    if groups > 1:
        signal_all = lax.dynamic_update_slice_in_dim(
            jnp.zeros((groups * group_rows,), F32), signal_part, g * group_rows, 0
        )
    signals = jnp.stack([gate_grad, signal_all]).reshape(2, -1, rows_here).transpose(1, 0, 2)
    signals = exchange(signals, EVERY).reshape(experts, 2, 2, rows_here)
    grad_router_probs = jnp.sum(signals[:, :, 0], axis=1).T
    gate_signal = jnp.sum(signals[:, :, 1], axis=(0, 1))

    def to_owners(hidden, weight, rows):
        if groups == 1:
            return scatter_group(combine(hidden, weight, place, rows))
        routed = jnp.einsum("bst,bsd->btd", place, rows, preferred_element_type=BF16)
        routed = lax.psum_scatter(
            routed.reshape(-1, model), "g", scatter_dimension=0, tiled=True
        )
        own = jnp.dot(hidden, weight, preferred_element_type=F32)
        return scatter_group((own + routed.astype(F32)).astype(BF16))

    grad_normed = to_owners(grad_shared_in, shared_gu.T, grad_rows)

    own_logits = jnp.dot(own_moe, router_weight, preferred_element_type=F32)
    router_probs = jax.nn.softmax(own_logits, axis=-1)
    grad_logits = router_probs * (
        grad_router_probs - jnp.sum(router_probs * grad_router_probs, axis=-1, keepdims=True)
    )
    grad_normed = (
        grad_normed
        + gate_signal[:, None] * gate_vec[None, :]
        + jnp.einsum("te,de->td", grad_logits, router_weight.astype(F32))
    )
    own_float = own_moe.astype(F32)
    grad_router = jnp.einsum("td,te->de", own_float, grad_logits)
    grad_gate_vec = jnp.sum(gate_signal[:, None] * own_float, axis=0)
    grad_gain_moe = jnp.sum(grad_normed * (middle * scale_moe), axis=0)
    grad_middle = cotangent.astype(F32) + norm_back(middle, scale_moe, gain_moe, grad_normed)
    grad_attn = grad_middle.astype(BF16)

    grad_attended = jnp.einsum("td,xdc->xtc", grad_attn, w_out, preferred_element_type=F32)
    grad_attended = grad_attended.astype(BF16).reshape(2, rows_here, 4, cols)
    grad_attended = grad_attended.transpose(0, 2, 1, 3).reshape(8, rows_here, cols)
    grad_attended = exchange(grad_attended, ("x", "y", "c")).reshape(2, 4, rows_here, cols)
    grad_attended = grad_attended.transpose(1, 0, 2, 3).reshape(plane_rows, cols)
    dq, dk, dv = attend_back(
        queries, keys, values, grad_attended, seg_q, seg_k, valid_k, cosine, sine
    )
    behind = [(k + 1, k) for k in range(LINE - 1)]
    sent = jnp.concatenate([dk[:plane_rows], dv[:plane_rows]], 1).astype(BF16)
    sent = lax.ppermute(sent, "z", behind).astype(F32)
    grad_projected = jnp.concatenate(
        [
            dq,
            (dk[plane_rows:] + sent[:, :cols]).astype(BF16),
            (dv[plane_rows:] + sent[:, cols:]).astype(BF16),
        ],
        1,
    )
    back_rows = jnp.einsum("tc,dc->td", grad_projected, w_qkv, preferred_element_type=F32)
    gain_sum = jnp.sum(back_rows * rows_attn.astype(F32), axis=0) / gain_attn
    back_own = scatter_plane(back_rows.astype(BF16))
    input_grad = grad_middle + norm_back(residual, scale_attn, gain_attn, back_own)
    bias_sum = jnp.sum(grad_projected.astype(F32), axis=0).reshape(3, cols)
    grad_bias = lax.dynamic_update_slice_in_dim(jnp.zeros((3, model), F32), bias_sum, here, 1)

    out_rows = jnp.dot(scaled_expert, w_down, preferred_element_type=F32)
    out_rows = out_rows.astype(BF16).reshape(block_count, capacity, model)
    moe_rows = to_owners(scaled_hidden, shared_dn.T, out_rows)
    output = (middle + moe_rows).astype(BF16)

    grad_egu = jnp.stack(
        [
            jnp.einsum("rd,rf->df", expert_in, grad, preferred_element_type=F32)
            for grad in (grad_ex_gate, grad_ex_up)
        ]
    )[None]
    grad_edown = jnp.einsum("rf,rd->fd", scaled_expert, expert_grad, preferred_element_type=F32)
    shared_grad = jnp.concatenate(
        [
            jnp.einsum("td,tf->df", rows_moe, grad_shared_in, preferred_element_type=F32),
            jnp.einsum("td,tf->df", rows_grad, scaled_hidden, preferred_element_type=F32),
        ],
        1,
    ).astype(BF16)
    if groups > 1:
        shared_grad = lax.psum_scatter(shared_grad, "g", scatter_dimension=0, tiled=True)
    shared_grad = exchange(shared_grad.reshape(in_group, weight_rows, 3 * hidden_own), GROUP)
    shared_grad = shared_grad.reshape(in_group, weight_rows, 3, hidden_own)
    shared_grad = shared_grad.transpose(2, 1, 0, 3).reshape(3, weight_rows, shared_cols)
    shared_grad = shared_grad.astype(F32)
    plane_grad = gather_plane(grad_attn)
    attn_grad = jnp.concatenate(
        [
            jnp.einsum("td,tc->dc", rows_attn, grad_projected, preferred_element_type=F32),
            jnp.einsum("td,tc->dc", plane_grad, attended, preferred_element_type=F32),
        ],
        1,
    ).astype(BF16)
    attn_grad = lax.psum_scatter(attn_grad, ("g", "z"), scatter_dimension=0, tiled=True)
    attn_grad = exchange(attn_grad.reshape(4, weight_rows, 4 * cols), ("y", "c"))
    attn_grad = attn_grad.reshape(4, weight_rows, 4, cols).astype(F32)
    attn_grad = attn_grad.transpose(2, 1, 0, 3).reshape(4, weight_rows, local_cols)

    valid_rows = lax.dynamic_slice_in_dim(valid_mask, x * rows_here, rows_here, 0).astype(F32)
    valid_rows = valid_rows[:, None]
    early = lax.psum(
        (
            grad_gain_moe,
            grad_router,
            grad_gate_vec,
            jnp.stack(
                [
                    jnp.sum(valid_rows * residual * residual),
                    jnp.sum(valid_rows * attn_rows * attn_rows),
                    jnp.sum(valid_rows),
                ]
            ),
        ),
        EVERY,
    )
    late = lax.psum((gain_sum, grad_bias, jnp.sum(valid_rows * moe_rows * moe_rows)), EVERY)
    valid_count = jnp.maximum(early[3][2], 1.0) * model
    return (
        output,
        input_grad,
        jnp.stack([late[0], early[0]]),
        attn_grad[:3],
        late[1],
        attn_grad[3].T,
        early[1],
        early[2],
        shared_grad[:2],
        shared_grad[2].T,
        grad_egu,
        grad_edown[None],
        jnp.sqrt(early[3][0] / valid_count),
        jnp.sqrt(early[3][1] / valid_count),
        jnp.sqrt(late[2] / valid_count),
    )


def solution(mesh):
    dp, mp = mesh.shape["dp"], mesh.shape["mp"]
    inner = Mesh(mesh.devices.reshape(dp // (4 * LINE), LINE, 2, 2, mp), EVERY)
    d = ("g",) + GROUP
    placed = (
        P(EVERY, None),
        P(EVERY, None),
        P(),
        P(None, d, "x"),
        P(),
        P("x", d),
        P(),
        P(),
        P(None, d, "x"),
        P("x", d),
        P(d, None, None, "x"),
        P(d, "x", None),
        P(d),
        P(d),
        P(d, None),
        P(d, None),
    )
    return jax.shard_map(
        per_device,
        mesh=inner,
        in_specs=placed,
        out_specs=(
            P(EVERY, None),
            P(EVERY, None),
            P(),
            P(None, d, "x"),
            P(),
            P("x", d),
            P(),
            P(),
            P(None, d, "x"),
            P("x", d),
            P(d, None, None, "x"),
            P(d, "x", None),
            P(),
            P(),
            P(),
        ),
        check_vma=False,
    )
```

```python
import functools

import jax
import jax.numpy as jnp
from jax import lax
from jax.experimental import pallas as pl
from jax.experimental.pallas import tpu as pltpu
from jax.sharding import Mesh
from jax.sharding import PartitionSpec as P

HEAD = 128
SEQ = 4096
WINDOW = 1024

EPSILON = 1e-06
ROPE_BASE = 1000000.0
MASKED = -1e30

LINE = 4
OFFSETS = (0, 2, 1, 3)
GROUP = ("z", "y", "c")
EVERY = ("g", "z", "y", "c", "x")
SWAP = [(0, 1), (1, 0)]
VMEM_LIMIT = 56 * 1024 * 1024

F32 = jnp.float32
BF16 = jnp.bfloat16


def swap(value, axis):
    return lax.ppermute(value, axis, SWAP)


def cross(value, offset):
    return lax.ppermute(value, "z", [(k, k ^ offset) for k in range(LINE)])


def take(value, index, dim):
    return lax.dynamic_index_in_dim(value, index, dim, keepdims=False)


def split(value, index, dim):
    return take(value, index, dim), take(value, 1 - index, dim)


def stage(kernel, after, inputs, outputs, name):
    count, _, width = inputs[0].shape
    part = width // 4

    def spec(rows):
        return pl.BlockSpec((1, rows, part), lambda i, j: (i, 0, j))

    return pl.pallas_call(
        kernel,
        grid=(count, 4),
        in_specs=[pl.BlockSpec(memory_space=pltpu.SMEM)] + [spec(v.shape[1]) for v in inputs],
        out_specs=[spec(rows) for rows, _ in outputs],
        out_shape=[jax.ShapeDtypeStruct((count, rows, width), kind) for rows, kind in outputs],
        compiler_params=pltpu.CompilerParams(vmem_limit_bytes=VMEM_LIMIT),
        name=name,
    )(after.reshape(1), *inputs)


def pair_kernel(after_ref, first, first_x, second, second_y, out_first, out_second):
    half = first.shape[1]
    out_first[0, :half] = first[0]
    out_first[0, half:] = first_x[0]
    out_second[0, :half] = second[0]
    out_second[0, half:] = second_y[0]


def plane_kernel(after_ref, first, first_y, second, second_x, out):
    rows = first.shape[1]
    half = rows // 2
    for y, source in enumerate((first, first_y)):
        out[0, 2 * y * rows : (2 * y + 1) * rows] = source[0]
    for x, source in enumerate((second, second_x)):
        for y in range(2):
            start = (2 * y + 1) * rows + x * half
            out[0, start : start + half] = source[0, y * half : (y + 1) * half]


def slot_gather(shards, after_pair, after_plane):
    rows = shards.shape[1]
    half = rows // 2
    first, second = shards[:, :half], shards[:, half:]
    first, second = stage(
        pair_kernel,
        after_pair,
        [first, swap(first, "x"), second, swap(second, "y")],
        [(rows, BF16)] * 2,
        "pair",
    )
    (own,) = stage(
        plane_kernel,
        after_plane,
        [first, swap(first, "y"), second, swap(second, "x")],
        [(4 * rows, BF16)],
        "plane",
    )
    return (own, swap(own, "c")), (first, own)


def core_sum_kernel(after_ref, keep, arrived, first, first_send, second, second_send):
    rows = first.shape[1]
    half = rows // 2

    def total(start, count):
        here = slice(start, start + count)
        return keep[0, here].astype(F32) + arrived[0, here].astype(F32)

    first[0] = total(0, rows)
    first_send[0] = total(2 * rows, rows).astype(BF16)
    for y in range(2):
        start = (2 * y + 1) * rows
        second[0, y * half : (y + 1) * half] = total(start, half)
        second_send[0, y * half : (y + 1) * half] = total(start + half, half).astype(BF16)


def pair_sum_kernel(after_ref, first, first_y, second, second_x, first_keep, first_send, second_keep, second_send):
    half = first_keep.shape[1]
    for value, arrived, keep, send in (
        (first, first_y, first_keep, first_send),
        (second, second_x, second_keep, second_send),
    ):
        keep[0] = value[0, :half] + arrived[0, :half].astype(F32)
        send[0] = (value[0, half:] + arrived[0, half:].astype(F32)).astype(BF16)


def last_sum_kernel(after_ref, first, first_x, second, second_y, out):
    half = first.shape[1]
    out[0, :half] = first[0] + first_x[0].astype(F32)
    out[0, half:] = second[0] + second_y[0].astype(F32)


def slot_scatter(keep, send, after_core, after_pair, after_last):
    rows = keep.shape[1] // 4
    first, first_send, second, second_send = stage(
        core_sum_kernel,
        after_core,
        [keep, swap(send, "c")],
        [(rows, F32), (rows, BF16)] * 2,
        "core_sum",
    )
    first_y, second_x = swap(first_send, "y"), swap(second_send, "x")
    first_keep, first_send, second_keep, second_send = stage(
        pair_sum_kernel,
        after_pair,
        [first, first_y, second, second_x],
        [(rows // 2, F32), (rows // 2, BF16)] * 2,
        "pair_sum",
    )
    first_x, second_y = swap(first_send, "x"), swap(second_send, "y")
    (whole,) = stage(
        last_sum_kernel,
        after_last,
        [first_keep, first_x, second_keep, second_y],
        [(rows, F32)],
        "last_sum",
    )
    return whole, (first, first_y, first_keep, first_x)


def tick_kernel(marker_ref, out_ref):
    corner = marker_ref[...].astype(F32)
    out_ref[0, 0] = jnp.where(jnp.max(corner) <= 3.4e38, 0, 1).astype(jnp.int32)


def tick(marker):
    lead = marker.ndim - 2
    block = (1,) * lead + (min(16, marker.shape[-2]), min(HEAD, marker.shape[-1]))
    flag = pl.pallas_call(
        tick_kernel,
        grid=(1,),
        in_specs=[pl.BlockSpec(block, lambda i: (0,) * marker.ndim)],
        out_specs=pl.BlockSpec(memory_space=pltpu.SMEM),
        out_shape=jax.ShapeDtypeStruct((1, 1), jnp.int32),
        name="tick",
    )(marker)
    return flag[0, 0]


def hold(value, flag):
    return jnp.where(flag == 0, value, jnp.zeros_like(value))


def all_sum(value):
    for axis in ("c", "x", "y"):
        value = value + swap(value, axis)
    for offset in (1, 2):
        value = value + cross(value, offset)
    return lax.psum(value, "g") if lax.axis_size("g") > 1 else value


def flip(value, index, dim):
    return jnp.where(index == 0, value, jnp.flip(value, dim))


def slot_shards(shard):
    return jnp.stack([shard] + [cross(shard, offset) for offset in OFFSETS[1:]])


def from_slots(near, far):
    arrived = cross(far.astype(BF16), 1)
    pair = near + arrived.astype(F32)
    return pair[0] + cross(pair[1].astype(BF16), 2).astype(F32), arrived


def gather_line(value, flag):
    z = lax.axis_index("z")
    across = cross(value, 2)
    others = cross(jnp.stack([value, across]), 1)
    held = [[value, others[0]], [across, others[1]]]
    placed = []
    for high in range(2):
        for low in range(2):
            rows = [jnp.where(z % 2 == low, held[k][0], held[k][1]) for k in range(2)]
            placed.append(jnp.where(z // 2 == high, rows[0], rows[1]))
    return hold(jnp.concatenate(placed, 0), flag)


def scatter_line(value):
    z = lax.axis_index("z")
    parts = value.reshape(2, 2, -1, value.shape[-1])
    keep, send = split(parts, z % 2, 1)
    arrived = cross(send, 1)
    keep = keep.astype(F32) + arrived.astype(F32)
    keep, send = split(keep, z // 2, 0)
    return keep + cross(send.astype(BF16), 2).astype(F32), arrived


def exchange(value, axes):
    return lax.all_to_all(value, axes, split_axis=0, concat_axis=0, tiled=True)


def turn(value, cosine, sine):
    return value * cosine + pltpu.roll(value, HEAD // 2, 1) * sine


def turn_back(value, cosine, sine):
    return value * cosine - pltpu.roll(value, HEAD // 2, 1) * sine


def own_order(target_ref, source_ref, x):
    part = source_ref.shape[0] // 4
    for half in range(2):
        for offset in range(2):
            side = x if offset == 0 else 1 - x
            place = pl.multiple_of((side * 2 + half) * part, part)
            start = (half * 2 + offset) * part
            target_ref[pl.ds(place, part), :] = source_ref[start : start + part, :]


def offset_order(target_ref, source_ref, x):
    part = source_ref.shape[0] // 4
    for half in range(2):
        for offset in range(2):
            side = x if offset == 0 else 1 - x
            place = pl.multiple_of((side * 2 + half) * part, part)
            start = (half * 2 + offset) * part
            target_ref[start : start + part, :] = source_ref[pl.ds(place, part), :]


def place_block(own_ref, halves, half_steps, x):
    for half, source in enumerate(halves):

        @pl.when(pl.program_id(0) // half_steps == half)
        def _():
            own_order(own_ref, source, x)


def project_kernel(heads, half_steps, order_ref, rows_ref, other_ref, weight_ref, bias_ref, cos_ref, sin_ref, own_ref, out_ref):
    place_block(own_ref, (rows_ref, other_ref), half_steps, order_ref[0])
    projected = (
        jnp.dot(own_ref[...], weight_ref[...], preferred_element_type=F32) + bias_ref[...]
    )
    for part in range(3 * heads):
        block = projected[:, part * HEAD : (part + 1) * HEAD]
        if part < 2 * heads:
            block = turn(block, cos_ref[...], sin_ref[...])
        out_ref[:, part * HEAD : (part + 1) * HEAD] = block.astype(BF16)


def plain_kernel(half_steps, order_ref, rows_ref, other_ref, weight_ref, own_ref, out_ref):
    place_block(own_ref, (rows_ref, other_ref), half_steps, order_ref[0])
    out_ref[...] = jnp.dot(
        own_ref[...], weight_ref[...], preferred_element_type=F32
    ).astype(BF16)


def project(order, halves, weight, bias=None, cosine=None, sine=None):
    slots, half_rows, model = halves[0].shape
    halves = [half.reshape(slots * half_rows, model) for half in halves]
    count = 2 * slots * half_rows
    width = weight.shape[1]
    step = half_rows // 2
    steps = 2 * slots
    arrived = [
        pl.BlockSpec((step, model), lambda i, order: (jnp.minimum(i, steps - 1), 0)),
        pl.BlockSpec((step, model), lambda i, order: (jnp.maximum(i - steps, 0), 0)),
    ]
    whole = pl.BlockSpec((model, width), lambda i, order: (0, 0))

    def placed(columns):
        return pl.BlockSpec((step, columns), lambda i, order: (order[i + 1], 0))

    if bias is None:
        kernel, specs, extra = functools.partial(plain_kernel, steps), arrived + [whole], ()
    else:
        kernel = functools.partial(project_kernel, width // (3 * HEAD), steps)
        row = pl.BlockSpec((1, width), lambda i, order: (0, 0))
        specs = arrived + [whole, row, placed(HEAD), placed(HEAD)]
        extra = (bias, cosine, sine)
    return pl.pallas_call(
        kernel,
        grid_spec=pltpu.PrefetchScalarGridSpec(
            num_scalar_prefetch=1,
            grid=(2 * steps,),
            in_specs=specs,
            out_specs=[placed(model), placed(width)],
        ),
        out_shape=[
            jax.ShapeDtypeStruct((count, model), BF16),
            jax.ShapeDtypeStruct((count, width), BF16),
        ],
        compiler_params=pltpu.CompilerParams(vmem_limit_bytes=VMEM_LIMIT),
        cost_estimate=pl.CostEstimate(
            flops=2 * count * model * width,
            bytes_accessed=2 * (2 * count * model + model * width + count * width),
            transcendentals=0,
        ),
        name="project",
    )(order, *halves, weight, *extra)


def spread_kernel(order_ref, act_ref, weight_ref, rows_ref, out_ref, sum_ref, held_ref):
    offset_order(held_ref, act_ref, order_ref[0])
    partial_rows = jnp.dot(held_ref[...], weight_ref[...], preferred_element_type=F32)
    out_ref[...] = partial_rows.astype(BF16)
    products = jnp.sum(partial_rows * rows_ref[...].astype(F32), axis=0, keepdims=True)

    @pl.when(pl.program_id(0) == 0)
    def _():
        sum_ref[...] = products

    @pl.when(pl.program_id(0) > 0)
    def _():
        sum_ref[...] += products


def spread_plain_kernel(order_ref, act_ref, weight_ref, out_ref, held_ref):
    offset_order(held_ref, act_ref, order_ref[0])
    out_ref[...] = jnp.dot(held_ref[...], weight_ref[...], preferred_element_type=F32).astype(BF16)


def spread(order, act, weight, core, rows=None):
    count, inner = act.shape
    model = weight.shape[1]
    slots = order.shape[0] // 4
    step = count // (4 * slots)

    first = core * 2 * slots + 1
    specs = [
        pl.BlockSpec((step, inner), lambda i, order: (order[first + i], 0)),
        pl.BlockSpec((inner, model), lambda i, order: (0, 0)),
    ]
    out_specs = [pl.BlockSpec((step, model), lambda i, order: (i, 0))]
    out_shape = [jax.ShapeDtypeStruct((count // 2, model), BF16)]
    operands = (order, act, weight)
    if rows is not None:
        specs.append(pl.BlockSpec((step, model), lambda i, order: (i, 0)))
        out_specs.append(pl.BlockSpec((1, model), lambda i, order: (0, 0)))
        out_shape.append(jax.ShapeDtypeStruct((1, model), F32))
        operands = operands + (rows.reshape(count // 2, model),)
    results = pl.pallas_call(
        spread_plain_kernel if rows is None else spread_kernel,
        grid_spec=pltpu.PrefetchScalarGridSpec(
            num_scalar_prefetch=1,
            grid=(2 * slots,),
            in_specs=specs,
            out_specs=out_specs,
            scratch_shapes=[pltpu.VMEM((step, inner), BF16)],
        ),
        out_shape=out_shape,
        compiler_params=pltpu.CompilerParams(vmem_limit_bytes=VMEM_LIMIT),
        cost_estimate=pl.CostEstimate(
            flops=count * model * inner,
            bytes_accessed=2 * (count * model + model * inner),
            transcendentals=0,
        ),
        name="spread",
    )(*operands)
    return (results[0].reshape(slots, -1, model),) + tuple(results[1:])


def block_probs(query, keys, seg_q, seg_k, valid_k, first, reach):
    rows, span = query.shape[0], keys.shape[0]
    scores = lax.dot_general(query, keys, (((1,), (1,)), ((), ())), preferred_element_type=F32)
    scores = scores * (HEAD ** (-0.5))
    distance = (
        reach
        + lax.broadcasted_iota(jnp.int32, (rows, span), 0)
        - lax.broadcasted_iota(jnp.int32, (rows, span), 1)
    )
    allowed = (
        (distance >= 0)
        & (distance < WINDOW)
        & (seg_q == seg_k)
        & ((valid_k == 1) | (distance == 0))
    )
    scores = jnp.where(allowed, scores, MASKED)
    powers = jnp.exp(scores - jnp.max(scores, axis=-1, keepdims=True))
    return powers / jnp.sum(powers, axis=-1, keepdims=True)


def attend_kernel(step, reach, q_ref, k_ref, v_ref, segq_ref, segk_ref, valid_ref, out_ref):
    first = pl.multiple_of(pl.program_id(1) * step, step)
    span = pl.ds(first, step + reach)
    probs = block_probs(
        q_ref[...], k_ref[span, :], segq_ref[...], segk_ref[:, span], valid_ref[:, span], first, reach
    )
    out_ref[...] = jnp.dot(
        probs.astype(BF16), v_ref[span, :], preferred_element_type=F32
    ).astype(BF16)


def head_specs(count, step, heads):
    ahead = count // (2 * step)
    return [
        pl.BlockSpec((step, HEAD), lambda h, i: (i + ahead, h)),
        pl.BlockSpec((count, HEAD), lambda h, i: (0, heads + h)),
        pl.BlockSpec((count, HEAD), lambda h, i: (0, 2 * heads + h)),
    ]


def attend(projected, seg_q, seg_k, valid_k):
    held, width = projected.shape
    count, width = held // 2, width // 3
    step = count // 4
    heads = width // HEAD
    flops = 4 * count * (step + count) * width
    return pl.pallas_call(
        functools.partial(attend_kernel, step, count),
        grid=(heads, 4),
        in_specs=head_specs(held, step, heads)
        + [
            pl.BlockSpec((step, 1), lambda h, i: (i, 0)),
            pl.BlockSpec((1, held), lambda h, i: (0, 0)),
            pl.BlockSpec((1, held), lambda h, i: (0, 0)),
        ],
        out_specs=pl.BlockSpec((step, HEAD), lambda h, i: (i, h)),
        out_shape=jax.ShapeDtypeStruct((count, width), BF16),
        compiler_params=pltpu.CompilerParams(vmem_limit_bytes=VMEM_LIMIT),
        cost_estimate=pl.CostEstimate(
            flops=flops, bytes_accessed=8 * held * width, transcendentals=flops // (4 * HEAD)
        ),
        name="attend",
    )(projected, projected, projected, seg_q, seg_k, valid_k)


def attend_back_kernel(
    step, reach, heads, q_ref, k_ref, v_ref, g_ref, segq_ref, segk_ref, valid_ref, cos_ref, sin_ref,
    out_ref, dk_ref, dv_ref,
):
    head, block = pl.program_id(0), pl.program_id(1)
    first = pl.multiple_of(block * step, step)
    span = pl.ds(first, step + reach)
    columns = [pl.ds(pl.multiple_of((part * heads + head) * HEAD, HEAD), HEAD) for part in range(3)]

    @pl.when(block == 0)
    def _():
        dk_ref[...] = jnp.zeros_like(dk_ref)
        dv_ref[...] = jnp.zeros_like(dv_ref)
        out_ref[0:reach, columns[0]] = jnp.zeros((reach, HEAD), BF16)

    query, keys, grad = q_ref[...], k_ref[span, :], g_ref[...]
    probs = block_probs(
        query, keys, segq_ref[...], segk_ref[:, span], valid_ref[:, span], first, reach
    )
    g_probs = lax.dot_general(
        grad, v_ref[span, :], (((1,), (1,)), ((), ())), preferred_element_type=F32
    )
    inner = jnp.sum(probs * g_probs, axis=-1, keepdims=True)
    g_scores = (probs * (g_probs - inner)).astype(BF16)
    scale = HEAD ** (-0.5)
    dq = jnp.dot(g_scores, keys, preferred_element_type=F32) * scale
    here = pl.ds(pl.multiple_of(first + reach, step), step)
    out_ref[here, columns[0]] = turn_back(dq, cos_ref[here, :], sin_ref[here, :]).astype(BF16)
    dk_ref[span, :] += (
        lax.dot_general(g_scores, query, (((0,), (0,)), ((), ())), preferred_element_type=F32)
        * scale
    )
    dv_ref[span, :] += lax.dot_general(
        probs.astype(BF16), grad, (((0,), (0,)), ((), ())), preferred_element_type=F32
    )

    @pl.when(block == pl.num_programs(1) - 1)
    def _():
        out_ref[:, columns[1]] = turn_back(dk_ref[...], cos_ref[...], sin_ref[...]).astype(BF16)
        out_ref[:, columns[2]] = dv_ref[...].astype(BF16)


def attend_back(projected, grad, seg_q, seg_k, valid_k, cosine, sine):
    held, width = projected.shape
    count, width = held // 2, width // 3
    step = count // 4
    heads = width // HEAD
    flops = 10 * count * (step + count) * width
    return pl.pallas_call(
        functools.partial(attend_back_kernel, step, count, heads),
        grid=(heads, 4),
        in_specs=head_specs(held, step, heads)
        + [
            pl.BlockSpec((step, HEAD), lambda h, i: (i, h)),
            pl.BlockSpec((step, 1), lambda h, i: (i, 0)),
            pl.BlockSpec((1, held), lambda h, i: (0, 0)),
            pl.BlockSpec((1, held), lambda h, i: (0, 0)),
            pl.BlockSpec((held, HEAD), lambda h, i: (0, 0)),
            pl.BlockSpec((held, HEAD), lambda h, i: (0, 0)),
        ],
        out_specs=pl.BlockSpec((held, 3 * width), lambda h, i: (0, 0)),
        out_shape=jax.ShapeDtypeStruct((held, 3 * width), BF16),
        scratch_shapes=[pltpu.VMEM((held, HEAD), F32)] * 2,
        compiler_params=pltpu.CompilerParams(vmem_limit_bytes=VMEM_LIMIT),
        cost_estimate=pl.CostEstimate(
            flops=flops, bytes_accessed=12 * held * width, transcendentals=flops // (10 * HEAD)
        ),
        name="attend_back",
    )(projected, projected, projected, grad, seg_q, seg_k, valid_k, cosine, sine)


def one_hot(slot_row, capacity):
    rows = lax.broadcasted_iota(jnp.int32, (capacity, slot_row.shape[1]), 0)
    return slot_row == rows


def moe_in_kernel(
    shape, expert_ref, rows_ref, other_rows_ref, grad_ref, other_grad_ref, win_ref, wdn_ref, slot_ref,
    act_ref, hid_ref, sig_ref, erow_ref, egrad_ref, egate_ref,
):
    experts, own, held, capacity = shape
    here = pl.program_id(0) < pl.num_programs(0) // 2
    rows = jnp.where(here, rows_ref[...], other_rows_ref[...])
    grad = jnp.where(here, grad_ref[...], other_grad_ref[...])
    inputs = dot_nt(rows, win_ref[...])
    gate_in, up_in = inputs[:, :held], inputs[:, held:]
    raw = dot_nt(grad, wdn_ref[...])
    column = lax.broadcasted_iota(jnp.int32, (1, held), 1)
    is_router = (column >= own) & (column < own + experts)
    logits = jnp.where(is_router, up_in, MASKED)
    powers = jnp.exp(logits - jnp.max(logits, axis=-1, keepdims=True))
    picked = jnp.where(column == own + expert_ref[0], powers, 0.0)
    gate = jnp.sum(picked, axis=-1, keepdims=True) / jnp.sum(powers, axis=-1, keepdims=True)
    shared_in = jnp.sum(jnp.where(column == own + experts, up_in, 0.0), axis=-1, keepdims=True)
    shared_gate = 1.0 / (1.0 + jnp.exp(-shared_in))
    sigma = 1.0 / (1.0 + jnp.exp(-gate_in))
    swished = gate_in * sigma
    hidden = swished * up_in
    grad_hidden = shared_gate * raw
    act_ref[:, :held] = (grad_hidden * up_in * sigma * (1.0 + gate_in * (1.0 - sigma))).astype(BF16)
    act_ref[:, held:] = (grad_hidden * swished).astype(BF16)
    hid_ref[...] = (shared_gate * hidden).astype(BF16)
    sig_ref[...] = jnp.sum(hidden * grad_hidden, axis=-1, keepdims=True) * (1.0 - shared_gate)
    place = jnp.where(one_hot(slot_ref[0], capacity), 1.0, 0.0)
    place_low = place.astype(BF16)
    erow_ref[...] = jnp.dot(place_low, rows, preferred_element_type=F32).astype(BF16)
    egrad_ref[...] = jnp.dot(place_low, grad, preferred_element_type=F32).astype(BF16)
    egate_ref[...] = jnp.dot(
        place,
        jnp.broadcast_to(gate, (gate.shape[0], HEAD)),
        precision=lax.Precision.HIGHEST,
        preferred_element_type=F32,
    )


def moe_in(expert, rows, grads, chunk, w_in, w_dn, slot_rows, experts, own, capacity):
    blocks, _, step = slot_rows.shape
    model = rows[0].shape[1]
    held = w_dn.shape[0]
    count = blocks * step
    half = blocks // 2

    def row_spec(core):
        def block(i):
            return jnp.maximum(i - half, 0) if core else jnp.minimum(i, half - 1)

        return pl.BlockSpec((step, model), lambda i: (block(i), 0))

    def grad_spec(core):
        def block(i):
            i = jnp.maximum(i - half, 0) if core else jnp.minimum(i, half - 1)
            return ((i // 4) * 2 + chunk) * 4 + i % 4

        return pl.BlockSpec((step, model), lambda i: (block(i), 0))

    return pl.pallas_call(
        functools.partial(moe_in_kernel, (experts, own, held, capacity)),
        grid=(blocks,),
        in_specs=[
            pl.BlockSpec(memory_space=pltpu.SMEM),
            row_spec(0),
            row_spec(1),
            grad_spec(0),
            grad_spec(1),
            pl.BlockSpec((2 * held, model), lambda i: (0, 0)),
            pl.BlockSpec((held, model), lambda i: (0, 0)),
            pl.BlockSpec((1, 1, step), lambda i: (i, 0, 0)),
        ],
        out_specs=[
            pl.BlockSpec((step, 2 * held), lambda i: (i, 0)),
            pl.BlockSpec((step, held), lambda i: (i, 0)),
            pl.BlockSpec((step, 1), lambda i: (i, 0)),
            pl.BlockSpec((capacity, model), lambda i: (i, 0)),
            pl.BlockSpec((capacity, model), lambda i: (i, 0)),
            pl.BlockSpec((capacity, HEAD), lambda i: (i, 0)),
        ],
        out_shape=[
            jax.ShapeDtypeStruct((count, 2 * held), BF16),
            jax.ShapeDtypeStruct((count, held), BF16),
            jax.ShapeDtypeStruct((count, 1), F32),
            jax.ShapeDtypeStruct((blocks * capacity, model), BF16),
            jax.ShapeDtypeStruct((blocks * capacity, model), BF16),
            jax.ShapeDtypeStruct((blocks * capacity, HEAD), F32),
        ],
        compiler_params=pltpu.CompilerParams(vmem_limit_bytes=VMEM_LIMIT),
        cost_estimate=pl.CostEstimate(
            flops=2 * count * model * (3 * held + 2 * capacity),
            bytes_accessed=6 * count * model,
            transcendentals=2 * count * held,
        ),
        name="moe_in",
    )(expert, *rows, *grads, w_in, w_dn, slot_rows)


def dot_nt(left, right):
    return lax.dot_general(left, right, (((1,), (1,)), ((), ())), preferred_element_type=F32)


def expert_kernel(
    steps, after_ref, rows_ref, grad_ref, gate_ref, wgu_ref, wd_ref,
    back_ref, out_ref, dgu_ref, hid_ref, ggate_ref, acc_g, acc_u, acc_r,
):
    step = pl.program_id(0)

    @pl.when(step == 0)
    def _():
        acc_g[...] = dot_nt(rows_ref[...], wgu_ref[0])
        acc_u[...] = dot_nt(rows_ref[...], wgu_ref[1])
        acc_r[...] = dot_nt(grad_ref[...], wd_ref[...])

    @pl.when((step > 0) & (step < steps))
    def _():
        acc_g[...] += dot_nt(rows_ref[...], wgu_ref[0])
        acc_u[...] += dot_nt(rows_ref[...], wgu_ref[1])
        acc_r[...] += dot_nt(grad_ref[...], wd_ref[...])

    @pl.when(step == steps)
    def _():
        gate_in, up_in, raw, gates = acc_g[...], acc_u[...], acc_r[...], gate_ref[:, :1]
        sigma = 1.0 / (1.0 + jnp.exp(-gate_in))
        swished = gate_in * sigma
        hidden = swished * up_in
        ggate_ref[...] = jnp.sum(hidden * raw, axis=-1, keepdims=True)
        hid_ref[...] = (gates * hidden).astype(BF16)
        scaled = gates * raw
        dgu_ref[0] = (scaled * up_in * sigma * (1.0 + gate_in * (1.0 - sigma))).astype(BF16)
        dgu_ref[1] = (scaled * swished).astype(BF16)

    @pl.when(step >= steps)
    def _():
        back = jnp.dot(dgu_ref[0], wgu_ref[0], preferred_element_type=F32)
        back = back + jnp.dot(dgu_ref[1], wgu_ref[1], preferred_element_type=F32)
        back_ref[...] = back.astype(BF16)
        out_ref[...] = jnp.dot(hid_ref[...], wd_ref[...], preferred_element_type=F32).astype(BF16)


def run_expert(after, rows, grad, gates, w_gu, w_down):
    count, model = rows.shape
    cols = w_down.shape[0]
    steps = 4
    chunk = model // steps
    return pl.pallas_call(
        functools.partial(expert_kernel, steps),
        grid=(2 * steps,),
        in_specs=[
            pl.BlockSpec(memory_space=pltpu.SMEM),
            pl.BlockSpec((count, chunk), lambda i: (0, jnp.minimum(i, steps - 1))),
            pl.BlockSpec((count, chunk), lambda i: (0, jnp.minimum(i, steps - 1))),
            pl.BlockSpec((count, HEAD), lambda i: (0, 0)),
            pl.BlockSpec((2, cols, chunk), lambda i: (0, 0, i % steps)),
            pl.BlockSpec((cols, chunk), lambda i: (0, i % steps)),
        ],
        out_specs=[
            pl.BlockSpec((count, chunk), lambda i: (0, jnp.maximum(i - steps, 0))),
            pl.BlockSpec((count, chunk), lambda i: (0, jnp.maximum(i - steps, 0))),
            pl.BlockSpec((2, count, cols), lambda i: (0, 0, 0)),
            pl.BlockSpec((count, cols), lambda i: (0, 0)),
            pl.BlockSpec((count, 1), lambda i: (0, 0)),
        ],
        out_shape=[
            jax.ShapeDtypeStruct((count, model), BF16),
            jax.ShapeDtypeStruct((count, model), BF16),
            jax.ShapeDtypeStruct((2, count, cols), BF16),
            jax.ShapeDtypeStruct((count, cols), BF16),
            jax.ShapeDtypeStruct((count, 1), F32),
        ],
        scratch_shapes=[pltpu.VMEM((count, cols), F32)] * 3,
        compiler_params=pltpu.CompilerParams(vmem_limit_bytes=VMEM_LIMIT),
        cost_estimate=pl.CostEstimate(
            flops=12 * count * model * cols,
            bytes_accessed=8 * count * model + 12 * model * cols,
            transcendentals=count * cols,
        ),
        name="run_expert",
    )(after.reshape(1), rows, grad, gates, w_gu, w_down)


def sum_kernel(after_ref, *refs):
    lefts, rights = refs[: len(refs) // 2 - 1], refs[len(refs) // 2 - 1 : -2]
    out_ref, acc_ref = refs[-2:]
    tile = pl.program_id(2)
    total = None
    for left, right in zip(lefts, rights):
        part = lax.dot_general(
            left[0], right[...], (((0,), (0,)), ((), ())), preferred_element_type=F32
        )
        total = part if total is None else total + part

    @pl.when(tile == 0)
    def _():
        acc_ref[...] = total

    @pl.when(tile > 0)
    def _():
        acc_ref[...] += total

    @pl.when(tile == pl.num_programs(2) - 1)
    def _():
        out_ref[0] = acc_ref[...].astype(out_ref.dtype)


def weight_sum(after, terms, tile, steps_of_tiles, dtype):
    parts, _, inner = terms[0][0].shape
    model = terms[0][2].shape[1]
    steps = 4
    width = model // steps

    def left_spec(first):
        return pl.BlockSpec((1, tile, inner), lambda j, d, t: (j, t + first, 0))

    def right_spec(stride, first):
        return pl.BlockSpec((tile, width), lambda j, d, t: (t * stride + first, d))

    return pl.pallas_call(
        sum_kernel,
        grid=(parts, steps, steps_of_tiles),
        in_specs=[pl.BlockSpec(memory_space=pltpu.SMEM)]
        + [left_spec(term[1]) for term in terms]
        + [right_spec(*term[3:]) for term in terms],
        out_specs=pl.BlockSpec((1, inner, width), lambda j, d, t: (j, 0, d)),
        out_shape=jax.ShapeDtypeStruct((parts, inner, model), dtype),
        scratch_shapes=[pltpu.VMEM((inner, width), F32)],
        compiler_params=pltpu.CompilerParams(vmem_limit_bytes=VMEM_LIMIT),
        cost_estimate=pl.CostEstimate(
            flops=2 * len(terms) * parts * steps_of_tiles * tile * inner * model,
            bytes_accessed=len(terms) * 2 * steps_of_tiles * tile * (parts * inner + model)
            + 4 * parts * inner * model,
            transcendentals=0,
        ),
        name="weight_sum",
    )(after.reshape(1), *[term[0] for term in terms], *[term[2] for term in terms])


def combine_kernel(capacity, after_ref, act_ref, weight_ref, slot_ref, rows_ref, out_ref):
    place = jnp.where(one_hot(slot_ref[0], capacity), 1.0, 0.0).astype(BF16)
    routed = lax.dot_general(
        place, rows_ref[...], (((0,), (0,)), ((), ())), preferred_element_type=F32
    )
    own = jnp.dot(act_ref[...], weight_ref[...], preferred_element_type=F32)
    out_ref[...] = (own + routed).astype(BF16)


def combine(after, act, weight, slot_rows, rows, core):
    inner, model = weight.shape
    blocks, _, step = slot_rows.shape
    capacity = rows.shape[0] // blocks
    taken = blocks // 2

    def block(i):
        return core * taken + i

    return pl.pallas_call(
        functools.partial(combine_kernel, capacity),
        grid=(taken,),
        in_specs=[
            pl.BlockSpec(memory_space=pltpu.SMEM),
            pl.BlockSpec((step, inner), lambda i: (block(i), 0)),
            pl.BlockSpec((inner, model), lambda i: (0, 0)),
            pl.BlockSpec((1, 1, step), lambda i: (block(i), 0, 0)),
            pl.BlockSpec((capacity, model), lambda i: (block(i), 0)),
        ],
        out_specs=pl.BlockSpec((step, model), lambda i: (i, 0)),
        out_shape=jax.ShapeDtypeStruct((taken * step, model), BF16),
        compiler_params=pltpu.CompilerParams(vmem_limit_bytes=VMEM_LIMIT),
        cost_estimate=pl.CostEstimate(
            flops=2 * taken * step * model * (inner + capacity),
            bytes_accessed=2 * taken * (step * (model + inner) + capacity * model),
            transcendentals=0,
        ),
        name="combine",
    )(after.reshape(1), act, weight, slot_rows, rows)


def norm_scale(rows_in):
    return lax.rsqrt(jnp.mean(rows_in * rows_in, axis=-1, keepdims=True) + EPSILON)


def norm_back(rows_in, scaling, gain, grad):
    unit_rows = rows_in * scaling
    grad_unit = grad * gain
    return scaling * (
        grad_unit - unit_rows * jnp.mean(grad_unit * unit_rows, axis=-1, keepdims=True)
    )


def swish(gate_in):
    return gate_in * jax.nn.sigmoid(gate_in)


def swish_back(gate_in, up_in, grad):
    sigma = jax.nn.sigmoid(gate_in)
    grad_gate = grad * up_in * sigma * (1.0 + gate_in * (1.0 - sigma))
    return (grad_gate, grad * gate_in * sigma)


def rope_tables(first_row, row_count):
    placing = (first_row + jnp.arange(row_count, dtype=jnp.int32)) % SEQ
    frequency = ROPE_BASE ** (-(jnp.arange(HEAD // 2, dtype=F32) * 2.0 / HEAD))
    angles = placing.astype(F32)[:, None] * frequency[None, :]
    cosine, sine = jnp.cos(angles), jnp.sin(angles)
    return (
        jnp.concatenate([cosine, cosine], 1),
        jnp.concatenate([-sine, sine], 1),
    )


def per_device(
    hidden_in,
    cotangent,
    norm_gains,
    qkv_weight,
    qkv_bias,
    out_weight,
    router_weight,
    shared_gate_vec,
    shared_gate_up,
    shared_down,
    expert_gate_up,
    expert_down,
    segments,
    valid_mask,
    routes,
    slots,
):
    groups = lax.axis_size("g")
    blocks = segments.shape[0]
    rows_here, model = hidden_in.shape
    weight_rows, local_cols = qkv_weight.shape[1:]
    shared_cols = shared_gate_up.shape[2]
    experts, top = router_weight.shape[1], routes.shape[1]
    shares = groups * 4 * LINE
    cols = local_cols // 4
    own = shared_cols // shares
    held = -(-(own + experts + 1) // 128) * 128
    capacity = -(-(blocks * top * 4 // (3 * experts)) // 16) * 16
    plane_rows = 4 * blocks
    everywhere = ("g",) + GROUP
    g, z, y, c, x = (lax.axis_index(axis) for axis in EVERY)
    expert = ((g * LINE + z) * 2 + y) * 2 + c

    ahead = [(k, k + 1) for k in range(LINE - 1)]
    behind = [(k + 1, k) for k in range(LINE - 1)]

    residual = hidden_in.astype(F32)
    gain_attn, gain_moe = norm_gains[0], norm_gains[1]
    scale_attn = norm_scale(residual)
    own_attn = (residual * scale_attn * gain_attn).astype(BF16)
    before = lax.ppermute(own_attn, "z", ahead)
    grad_shards = slot_shards(cotangent)
    now = jnp.zeros((), jnp.int32)
    rows_attn, attn_marks = slot_gather(jnp.stack([before, own_attn]), now, now)
    flag = tick(attn_marks[0])
    slot_grads, grad_marks = slot_gather(hold(grad_shards, flag), now, now)
    slot_grads = [half.reshape(-1, model) for half in slot_grads]

    def cut_heads(value):
        return value.reshape(weight_rows, -1, 4, cols).transpose(2, 0, 1, 3)

    qkv_cut = cut_heads(qkv_weight.transpose(1, 0, 2)).reshape(4, weight_rows, 3 * cols)
    out_cut = cut_heads(out_weight.T).reshape(4, weight_rows, cols)
    w_heads = exchange(jnp.concatenate([qkv_cut, out_cut], 2), ("y", "c"))
    w_heads = w_heads.reshape(4 * weight_rows, 4 * cols)
    w_qkv = gather_line(w_heads[:, : 3 * cols], tick(grad_marks[0]))
    if groups > 1:
        w_qkv = lax.all_gather(w_qkv, "g", axis=0, tiled=True)
    later = tick(w_heads)

    numbers = jnp.concatenate([segments[None], valid_mask[None], routes.T, slots.T], 0) + later
    numbers = jnp.stack([numbers, swap(numbers, "y")])
    numbers = jnp.stack([numbers, swap(numbers, "c")])
    plane_numbers = flip(flip(numbers[:, :, :2], c, 0), y, 1).transpose(1, 0, 2, 3)
    plane_numbers = plane_numbers.reshape(4, 2, blocks).transpose(1, 0, 2).reshape(2, plane_rows)
    numbers = slot_shards(numbers)
    numbers = numbers.reshape(LINE, 1, 4, 2 + 2 * top, blocks)
    if groups > 1:
        numbers = lax.all_gather(numbers, "g", axis=1, tiled=True)
    slot_here = jnp.max(
        jnp.where(numbers[:, :, :, 2 : 2 + top] == expert, numbers[:, :, :, 2 + top :], -1), 3
    )
    slot_here = slot_here.reshape(LINE, groups, 4, 2, 2, rows_here // 2)
    slot_here = flip(slot_here, x, 3).transpose(0, 1, 2, 4, 3, 5)
    slot_here = slot_here.reshape(2, 2, groups, 2, 2, blocks)

    late_gu, late_dn = hold(shared_gate_up, later), hold(shared_down, later)
    shared_cut = jnp.concatenate(
        [
            late_gu[0].T.reshape(shares, own, weight_rows),
            late_gu[1].T.reshape(shares, own, weight_rows),
            late_dn.reshape(shares, own, weight_rows),
        ],
        1,
    )

    here = x * local_cols + (y * 2 + c) * cols
    bias = lax.dynamic_slice_in_dim(qkv_bias, here, cols, 1).astype(F32).reshape(1, 3 * cols)
    cosine, sine = rope_tables((z + LINE - 1) * plane_rows + later, 2 * plane_rows)
    order = jnp.stack([(y ^ j) * 2 + (c ^ i) for i in range(2) for j in range(2)])
    order = order.astype(jnp.int32)
    order_one = jnp.concatenate([x[None], order])
    order_two = jnp.concatenate([x[None], order[:2], order[:2] + 4, order[2:], order[2:] + 4])
    own_rows, projected = project(order_two, rows_attn, w_qkv, bias, cosine, sine)
    w_out = gather_line(hold(w_heads[:, 3 * cols :], tick(w_qkv)), now)
    if groups > 1:
        w_out = lax.all_gather(w_out, "g", axis=0, tiled=True)
    numbers_before = jnp.where(z == 0, -1, lax.ppermute(plane_numbers, "z", ahead))
    near = jnp.concatenate([numbers_before, plane_numbers], 1)
    seg_k, valid_k = near[:1], near[1:]
    seg_q = plane_numbers[0].reshape(plane_rows, 1)
    attended = attend(projected, seg_q, seg_k, valid_k)
    w_out_t = w_out.T
    order_late = order_one + tick(grad_marks[1])
    (send,) = spread(order_late, attended, w_out_t, 1)
    (keep,) = spread(order_late, attended, w_out_t, 0)
    attn_rows = slot_scatter(keep, send, now, now, now)[0][0]
    middle = residual + attn_rows
    scale_moe = norm_scale(middle)
    own_moe = (middle * scale_moe * gain_moe).astype(BF16)

    w_shared = exchange(hold(shared_cut, tick(attended)), everywhere)
    w_shared = w_shared.transpose(1, 0, 2).reshape(3 * own, model)

    def padded(*values):
        value = jnp.concatenate(values, 0)
        return jnp.pad(value, ((0, held - value.shape[0]), (0, 0)))

    shared_in = jnp.concatenate(
        [
            padded(w_shared[:own]),
            padded(w_shared[own : 2 * own], router_weight.T, shared_gate_vec[None]),
        ],
        0,
    )
    shared_dn = padded(w_shared[2 * own :])

    near_shards = jnp.stack([own_moe, cross(own_moe, 2)])
    far_shards = cross(near_shards, 1)
    near_rows, near_marks = slot_gather(near_shards, now, now)
    far_rows, far_marks = slot_gather(hold(far_shards, tick(near_marks[1])), now, now)
    chunk_rows = [[half.reshape(-1, model) for half in rows] for rows in (near_rows, far_rows)]
    if groups > 1:
        chunk_rows = [
            [lax.all_gather(half, "g", axis=0, tiled=True) for half in rows] for rows in chunk_rows
        ]
        slot_grads = [lax.all_gather(half, "g", axis=0, tiled=True) for half in slot_grads]

    w_gu, w_down = expert_gate_up[0].transpose(0, 2, 1), expert_down[0]
    expert_id = expert.reshape(1).astype(jnp.int32)

    def slots_of(table):
        return table.transpose(3, 2, 0, 1, 4, 5).reshape(-1, 1, blocks)

    def to_owners(act, weight, table, rows, after):
        halves = []
        for core in range(2):
            half = combine(after[1 - core], act, weight, table, rows, core)
            if groups > 1:
                half = lax.psum_scatter(half, "g", scatter_dimension=0, tiled=True)
            halves.append(half.reshape(-1, plane_rows // 2, model))
        total, marks = slot_scatter(*halves, *after[2:])
        return total, (halves[0],) + marks

    acts, hiddens, signals, inputs, grads, results = [], [], [], [], [], []
    gate_grads, totals = [], []
    start, begin = tick(far_marks[0]), tick(far_marks[1])
    for chunk, rows in enumerate(chunk_rows):
        table = slots_of(slot_here[chunk : chunk + 1])
        act, hid, sig, erow, egrad, egate = moe_in(
            expert_id + start,
            rows, slot_grads, chunk, shared_in, shared_dn, table, experts, own, capacity,
        )
        back, out, dgu, ehid, ggate = run_expert(now, erow, egrad, egate, w_gu, w_down)
        chosen = table == jnp.arange(capacity, dtype=jnp.int32)[None, :, None]
        ggate = ggate.reshape(-1, capacity, 1)
        gate_grads.append(jnp.sum(jnp.where(chosen, ggate, 0.0), axis=1))
        signals.append(sig.reshape(-1, blocks))
        total, marks = to_owners(act, shared_in, table, back, (begin, now, now, now, now))
        start, begin = tick(marks[1]), tick(marks[3])
        totals.append(total)
        acts.append(act)
        hiddens.append(hid)
        inputs.append((dgu, erow))
        grads.append((ehid, egrad))
        results.append(out)
    grad_normed, last_mark = from_slots(totals[0], totals[1])

    signals = jnp.stack([jnp.stack(gate_grads), jnp.stack(signals)])
    signals = signals.reshape(2, 2, 2, groups, 2, 2, 2, 2, rows_here // 2)
    for dim, index in ((1, z % 2), (2, c), (4, z // 2), (5, y), (7, x)):
        signals = flip(signals, index, dim)
    signals = signals.transpose(3, 4, 1, 5, 2, 7, 0, 6, 8).reshape(2 * shares, 2, rows_here)
    signals = exchange(signals, EVERY).reshape(experts, 2, 2, rows_here)
    grad_router_probs = jnp.sum(signals[:, :, 0], axis=1).T
    gate_signal = jnp.sum(signals[:, :, 1], axis=(0, 1))

    def over_chunks(parts):
        width = parts[0].shape[-1]
        parts = [part.reshape(2, groups, -1, width) for part in parts]
        return jnp.concatenate(parts, 2).reshape(-1, width)

    if groups == 1:
        moe_parts, moe_marks = to_owners(
            over_chunks(hiddens),
            shared_dn,
            slots_of(slot_here),
            over_chunks(results),
            (tick(marks[0]), tick(marks[2]), now, now, now),
        )
        moe_parts = [moe_parts[:2], moe_parts[2:]]
    else:
        moe_parts = []
        for chunk in range(2):
            table = slots_of(slot_here[chunk : chunk + 1])
            after = tick(moe_parts[-1] if moe_parts else last_mark)
            part, moe_marks = to_owners(
                hiddens[chunk], shared_dn, table, results[chunk], (after, after, now, now, now)
            )
            moe_parts.append(part)
    moe_rows, _ = from_slots(*moe_parts)
    output = (middle + moe_rows).astype(BF16)
    tiles = range(2)
    grad_sgu = weight_sum(
        tick(marks[4]),
        [
            (acts[chunk][None], core * groups, chunk_rows[chunk][core], 1, 0)
            for chunk in tiles
            for core in tiles
        ],
        plane_rows,
        groups,
        BF16,
    )[0]
    grad_sdn = weight_sum(
        tick(last_mark),
        [
            (hiddens[chunk][None], core * groups, slot_grads[core], 2, chunk)
            for chunk in tiles
            for core in tiles
        ],
        plane_rows,
        groups,
        BF16,
    )[0]
    shared_grad = jnp.concatenate(
        [grad_sgu[:own], grad_sgu[held : held + own], grad_sdn[:own]], 0
    )
    shared_grad = shared_grad.reshape(3 * own, shares, weight_rows).transpose(1, 0, 2)
    shared_grad = exchange(shared_grad, everywhere)
    shared_mark = tick(shared_grad)
    shared_grad = shared_grad.reshape(shares, 3, own, weight_rows).transpose(1, 0, 2, 3)
    shared_grad = shared_grad.reshape(3, shared_cols, weight_rows).astype(F32)

    own_logits = jnp.dot(own_moe, router_weight, preferred_element_type=F32)
    router_probs = jax.nn.softmax(own_logits, axis=-1)
    grad_logits = router_probs * (
        grad_router_probs - jnp.sum(router_probs * grad_router_probs, axis=-1, keepdims=True)
    )
    grad_normed = (
        grad_normed
        + gate_signal[:, None] * shared_gate_vec.astype(F32)[None, :]
        + jnp.einsum("te,de->td", grad_logits, router_weight.astype(F32))
    )
    own_float = own_moe.astype(F32)
    grad_router = jnp.einsum("td,te->ed", own_float, grad_logits)
    grad_gate_vec = jnp.sum(gate_signal[:, None] * own_float, axis=0)
    grad_gain_moe = jnp.sum(grad_normed * (middle * scale_moe), axis=0)
    grad_middle = cotangent.astype(F32) + norm_back(middle, scale_moe, gain_moe, grad_normed)
    grad_attn = grad_middle.astype(BF16)

    plane_grad, _ = slot_gather(grad_attn[None], now, now)
    plane_grad, grad_attended = project(order_one + tick(moe_marks[1]), plane_grad, w_out)
    grad_projected = attend_back(
        projected, grad_attended, seg_q, seg_k, valid_k, cosine, sine
    )
    w_qkv_t = w_qkv.T
    order_late = order_two + shared_mark
    send, sum_send = spread(order_late, grad_projected, w_qkv_t, 1, rows_attn[1])
    keep, sum_keep = spread(order_late, grad_projected, w_qkv_t, 0, rows_attn[0])
    gain_sum = (sum_send + sum_keep)[0] / gain_attn
    back_both, back_marks = slot_scatter(keep, send, tick(moe_marks[3]), now, now)
    back_own = back_both[1] + lax.ppermute(back_both[0].astype(BF16), "z", behind).astype(F32)
    input_grad = grad_middle + norm_back(residual, scale_attn, gain_attn, back_own)
    bias_sum = jnp.sum(grad_projected.astype(F32), axis=0).reshape(3, cols)
    grad_bias = lax.dynamic_update_slice_in_dim(jnp.zeros((3, model), F32), bias_sum, here, 1)

    def weight_grad(left, right):
        return lax.dot_general(left, right, (((0,), (0,)), ((), ())), preferred_element_type=F32)

    def to_weight_owners(value):
        if groups > 1:
            value = lax.psum_scatter(value, "g", scatter_dimension=0, tiled=True)
        value, mark = scatter_line(value)
        value = exchange(value.astype(BF16).reshape(4, weight_rows, -1), ("y", "c"))
        return value.astype(F32), mark

    grad_out, _ = to_weight_owners(weight_grad(plane_grad, attended).astype(BF16))
    grad_out = grad_out.transpose(1, 0, 2).reshape(weight_rows, local_cols).T
    grad_qkv, qkv_mark = to_weight_owners(weight_grad(own_rows, grad_projected).astype(BF16))
    grad_qkv = grad_qkv.reshape(4, weight_rows, 3, cols).transpose(2, 1, 0, 3)
    grad_qkv = grad_qkv.reshape(3, weight_rows, local_cols)

    tile = inputs[0][1].shape[0]
    grad_egu = weight_sum(
        tick(back_marks[1]), [(left, 0, right, 1, 0) for left, right in inputs], tile, 1, F32
    )
    grad_egu = grad_egu.transpose(0, 2, 1)[None]
    grad_edown = weight_sum(
        tick(qkv_mark), [(left[None], 0, right, 1, 0) for left, right in grads], tile, 1, F32
    )

    valid_rows = lax.dynamic_slice_in_dim(valid_mask, x * rows_here, rows_here, 0).astype(F32)
    valid_rows = valid_rows[:, None]

    def in_lanes(values):
        flat = jnp.stack(values)
        return jnp.pad(flat, (0, model - len(values)))[None]

    sums_of_all = all_sum(
        jnp.concatenate(
            [
                grad_router,
                grad_gate_vec[None],
                grad_gain_moe[None],
                gain_sum[None],
                grad_bias,
                in_lanes(
                    [
                        jnp.sum(valid_rows * residual * residual),
                        jnp.sum(valid_rows * attn_rows * attn_rows),
                        jnp.sum(valid_rows * moe_rows * moe_rows),
                        jnp.sum(valid_rows),
                    ]
                ),
            ],
            0,
        )
    )
    others = sums_of_all[experts:]
    root_means = jnp.sqrt(others[6, :3] / (jnp.maximum(others[6, 3], 1.0) * model))
    return (
        output,
        input_grad,
        jnp.stack([others[2], others[1]]),
        grad_qkv,
        others[3:6],
        grad_out,
        sums_of_all[:experts].T,
        others[0],
        shared_grad[:2].transpose(0, 2, 1),
        shared_grad[2],
        grad_egu,
        grad_edown,
        root_means[0],
        root_means[1],
        root_means[2],
    )


def solution(mesh):
    dp, mp = mesh.shape["dp"], mesh.shape["mp"]
    inner = Mesh(mesh.devices.reshape(dp // (4 * LINE), LINE, 2, 2, mp), EVERY)
    d = ("g",) + GROUP
    placed = (
        P(EVERY, None),
        P(EVERY, None),
        P(),
        P(None, d, "x"),
        P(),
        P("x", d),
        P(),
        P(),
        P(None, d, "x"),
        P("x", d),
        P(d, None, None, "x"),
        P(d, "x", None),
        P(d),
        P(d),
        P(d, None),
        P(d, None),
    )
    return jax.shard_map(
        per_device,
        mesh=inner,
        in_specs=placed,
        out_specs=(
            P(EVERY, None),
            P(EVERY, None),
            P(),
            P(None, d, "x"),
            P(),
            P("x", d),
            P(),
            P(),
            P(None, d, "x"),
            P("x", d),
            P(d, None, None, "x"),
            P(d, "x", None),
            P(),
            P(),
            P(),
        ),
        check_vma=False,
    )
```

```python
import functools

import jax
import jax.numpy as jnp
from jax import lax
from jax.experimental import pallas as pl
from jax.experimental.pallas import tpu as pltpu
from jax.sharding import Mesh
from jax.sharding import PartitionSpec as P

HEAD = 128
SEQ = 4096
WINDOW = 1024

EPSILON = 1e-06
ROPE_BASE = 1000000.0
MASKED = -1e30

LINE = 4
GROUP = ("z", "y", "c")
EVERY = ("g", "z", "y", "c", "x")
SWAP = [(0, 1), (1, 0)]
VMEM_LIMIT = 56 * 1024 * 1024

F32 = jnp.float32
BF16 = jnp.bfloat16


def swap(value, axis):
    return lax.ppermute(value, axis, SWAP)


def cross(value, offset):
    return lax.ppermute(value, "z", [(k, k ^ offset) for k in range(LINE)])


def take(value, index, dim):
    return lax.dynamic_index_in_dim(value, index, dim, keepdims=False)


def split(value, index, dim):
    return take(value, index, dim), take(value, 1 - index, dim)


ANYWHERE = pl.BlockSpec(memory_space=pl.ANY)


def without(count, kernel, first=0):
    def run(*refs):
        kernel(*refs[:first], *refs[first + count :])

    return run


def stage(kernel, after, inputs, outputs, name):
    count, _, width = inputs[0].shape
    parts = max(1, 4 // count)

    def spec(rows):
        return pl.BlockSpec((1, rows, width // parts), lambda i, j: (i, 0, j))

    return pl.pallas_call(
        without(len(after), kernel),
        grid=(count, parts),
        in_specs=[ANYWHERE] * len(after) + [spec(v.shape[1]) for v in inputs],
        out_specs=[spec(rows) for rows, _ in outputs],
        out_shape=[jax.ShapeDtypeStruct((count, rows, width), kind) for rows, kind in outputs],
        compiler_params=pltpu.CompilerParams(vmem_limit_bytes=VMEM_LIMIT),
        cost_estimate=pl.CostEstimate(
            flops=0, bytes_accessed=8 * count * width * sum(rows for rows, _ in outputs), transcendentals=0
        ),
        name=name,
    )(*after, *inputs)


def pair_kernel(first, first_x, second, second_y, out_first, out_second):
    half = first.shape[1]
    out_first[0, :half] = first[0]
    out_first[0, half:] = first_x[0]
    out_second[0, :half] = second[0]
    out_second[0, half:] = second_y[0]


def plane_kernel(first, first_y, second, second_x, out):
    rows = first.shape[1]
    half = rows // 2
    for y, source in enumerate((first, first_y)):
        out[0, 2 * y * rows : (2 * y + 1) * rows] = source[0]
    for x, source in enumerate((second, second_x)):
        for y in range(2):
            start = (2 * y + 1) * rows + x * half
            out[0, start : start + half] = source[0, y * half : (y + 1) * half]


def slot_pair(shards, after):
    rows = shards.shape[1]
    half = rows // 2
    first, second = shards[:, :half], shards[:, half:]
    pairs = stage(
        pair_kernel,
        after,
        [first, swap(first, "x"), second, swap(second, "y")],
        [(rows, BF16)] * 2,
        "pair",
    )
    arrived = swap(pairs[0], "y"), swap(pairs[1], "x")

    def plane(after):
        (own,) = stage(
            plane_kernel,
            after,
            [pairs[0], arrived[0], pairs[1], arrived[1]],
            [(4 * rows, BF16)],
            "plane",
        )
        return own, swap(own, "c")

    return pairs, plane, arrived


def slot_gather(shards, after_pair, after_plane):
    pairs, plane, _ = slot_pair(shards, after_pair)
    halves = plane(after_plane)
    return halves, (pairs[0], halves[0])


def core_sum_kernel(keep, arrived, first, first_send, second, second_send):
    rows = first.shape[1]
    half = rows // 2

    def total(start, count):
        here = slice(start, start + count)
        return keep[0, here].astype(F32) + arrived[0, here].astype(F32)

    first[0] = total(0, rows)
    first_send[0] = total(2 * rows, rows).astype(BF16)
    for y in range(2):
        start = (2 * y + 1) * rows
        second[0, y * half : (y + 1) * half] = total(start, half)
        second_send[0, y * half : (y + 1) * half] = total(start + half, half).astype(BF16)


def pair_sum_kernel(first, first_y, second, second_x, first_keep, first_send, second_keep, second_send):
    half = first_keep.shape[1]
    for value, arrived, keep, send in (
        (first, first_y, first_keep, first_send),
        (second, second_x, second_keep, second_send),
    ):
        keep[0] = value[0, :half] + arrived[0, :half].astype(F32)
        send[0] = (value[0, half:] + arrived[0, half:].astype(F32)).astype(BF16)


def last_sum_kernel(first, first_x, second, second_y, out):
    half = first.shape[1]
    out[0, :half] = first[0] + first_x[0].astype(F32)
    out[0, half:] = second[0] + second_y[0].astype(F32)


def scatter_core(keep, send, after):
    rows = keep.shape[1] // 4
    first, first_send, second, second_send = stage(
        core_sum_kernel,
        after,
        [keep, swap(send, "c")],
        [(rows, F32), (rows, BF16)] * 2,
        "core_sum",
    )
    return first, swap(first_send, "y"), second, swap(second_send, "x")


def scatter_pair(steps, after):
    half = steps[0].shape[1] // 2
    first, first_send, second, second_send = stage(
        pair_sum_kernel,
        after,
        list(steps),
        [(half, F32), (half, BF16)] * 2,
        "pair_sum",
    )
    return first, swap(first_send, "x"), second, swap(second_send, "y")


def scatter_last(steps, after):
    (whole,) = stage(
        last_sum_kernel, after, list(steps), [(2 * steps[0].shape[1], F32)], "last_sum"
    )
    return whole


def slot_scatter(keep, send, after_core, after_pair, after_last):
    core = scatter_core(keep, send, after_core)
    pair = scatter_pair(core, after_pair)
    return scatter_last(pair, after_last), (core[0], core[1], pair[0], pair[1])


def tick_kernel(marker_ref, out_ref):
    corner = marker_ref[...].astype(F32)
    out_ref[0, 0] = jnp.where(jnp.max(corner) <= 3.4e38, 0, 1).astype(jnp.int32)


def tick(marker):
    lead = marker.ndim - 2
    block = (1,) * lead + (min(16, marker.shape[-2]), min(HEAD, marker.shape[-1]))
    flag = pl.pallas_call(
        tick_kernel,
        grid=(1,),
        in_specs=[pl.BlockSpec(block, lambda i: (0,) * marker.ndim)],
        out_specs=pl.BlockSpec(memory_space=pltpu.SMEM),
        out_shape=jax.ShapeDtypeStruct((1, 1), jnp.int32),
        name="tick",
    )(marker)
    return flag[0, 0]


def hold(value, flag):
    return jnp.where(flag == 0, value, jnp.zeros_like(value))


def all_sum(value):
    for axis in ("c", "x", "y"):
        value = value + swap(value, axis)
    for offset in (1, 2):
        value = value + cross(value, offset)
    return lax.psum(value, "g") if lax.axis_size("g") > 1 else value


def flip(value, index, dim):
    return jnp.where(index == 0, value, jnp.flip(value, dim))


def gather_line(value, across):
    z = lax.axis_index("z")
    others = cross(jnp.stack([value, across]), 1)
    held = [[value, others[0]], [across, others[1]]]
    placed = []
    for high in range(2):
        for low in range(2):
            rows = [jnp.where(z % 2 == low, held[k][0], held[k][1]) for k in range(2)]
            placed.append(jnp.where(z // 2 == high, rows[0], rows[1]))
    return jnp.concatenate(placed, 0), others


def scatter_line(value):
    z = lax.axis_index("z")
    parts = value.reshape(2, 2, -1, value.shape[-1])
    keep, send = split(parts, z % 2, 1)
    marks = [send, cross(send, 1)]
    keep = keep.astype(F32) + marks[1].astype(F32)
    keep, send = split(keep, z // 2, 0)
    marks.append(cross(send.astype(BF16), 2))
    return (keep + marks[2].astype(F32)).astype(BF16), marks


def exchange(value, axes):
    return lax.all_to_all(value, axes, split_axis=0, concat_axis=0, tiled=True)


def turn(value, cosine, sine):
    return value * cosine + pltpu.roll(value, HEAD // 2, 1) * sine


def turn_back(value, cosine, sine):
    return value * cosine - pltpu.roll(value, HEAD // 2, 1) * sine


def own_order(target_ref, source_ref, x):
    part = source_ref.shape[0] // 4
    for half in range(2):
        for offset in range(2):
            side = x if offset == 0 else 1 - x
            place = pl.multiple_of((side * 2 + half) * part, part)
            start = (half * 2 + offset) * part
            target_ref[pl.ds(place, part), :] = source_ref[start : start + part, :]


def offset_order(target_ref, source_ref, x):
    part = source_ref.shape[0] // 4
    for half in range(2):
        for offset in range(2):
            side = x if offset == 0 else 1 - x
            place = pl.multiple_of((side * 2 + half) * part, part)
            start = (half * 2 + offset) * part
            target_ref[start : start + part, :] = source_ref[pl.ds(place, part), :]


def place_block(own_ref, halves, half_steps, x):
    for half, source in enumerate(halves):

        @pl.when(pl.program_id(0) // half_steps == half)
        def _():
            own_order(own_ref, source, x)


def project_kernel(heads, half_steps, order_ref, rows_ref, other_ref, weight_ref, bias_ref, cos_ref, sin_ref, own_ref, out_ref):
    place_block(own_ref, (rows_ref, other_ref), half_steps, order_ref[0])
    projected = (
        jnp.dot(own_ref[...], weight_ref[...], preferred_element_type=F32) + bias_ref[...]
    )
    for part in range(3 * heads):
        block = projected[:, part * HEAD : (part + 1) * HEAD]
        if part < 2 * heads:
            block = turn(block, cos_ref[...], sin_ref[...])
        out_ref[:, part * HEAD : (part + 1) * HEAD] = block.astype(BF16)


def plain_kernel(half_steps, order_ref, rows_ref, other_ref, weight_ref, own_ref, out_ref):
    place_block(own_ref, (rows_ref, other_ref), half_steps, order_ref[0])
    out_ref[...] = jnp.dot(
        own_ref[...], weight_ref[...], preferred_element_type=F32
    ).astype(BF16)


def project(after, order, halves, weight, bias=None, cosine=None, sine=None):
    slots, half_rows, model = halves[0].shape
    halves = [half.reshape(slots * half_rows, model) for half in halves]
    count = 2 * slots * half_rows
    width = weight.shape[1]
    step = half_rows // 2
    steps = 2 * slots
    arrived = [
        pl.BlockSpec((step, model), lambda i, order: (jnp.minimum(i, steps - 1), 0)),
        pl.BlockSpec((step, model), lambda i, order: (jnp.maximum(i - steps, 0), 0)),
    ]
    whole = pl.BlockSpec((model, width), lambda i, order: (0, 0))

    def placed(columns):
        return pl.BlockSpec((step, columns), lambda i, order: (order[i + 1], 0))

    if bias is None:
        kernel, specs, extra = functools.partial(plain_kernel, steps), arrived + [whole], ()
    else:
        kernel = functools.partial(project_kernel, width // (3 * HEAD), steps)
        row = pl.BlockSpec((1, width), lambda i, order: (0, 0))
        specs = arrived + [whole, row, placed(HEAD), placed(HEAD)]
        extra = (bias, cosine, sine)
    return pl.pallas_call(
        without(len(after), kernel, 1),
        grid_spec=pltpu.PrefetchScalarGridSpec(
            num_scalar_prefetch=1,
            grid=(2 * steps,),
            in_specs=[ANYWHERE] * len(after) + specs,
            out_specs=[placed(model), placed(width)],
        ),
        out_shape=[
            jax.ShapeDtypeStruct((count, model), BF16),
            jax.ShapeDtypeStruct((count, width), BF16),
        ],
        compiler_params=pltpu.CompilerParams(vmem_limit_bytes=VMEM_LIMIT),
        cost_estimate=pl.CostEstimate(
            flops=3 * (2 * count * model * width),
            bytes_accessed=2 * (2 * count * model + model * width + count * width),
            transcendentals=0,
        ),
        name="project",
    )(order, *after, *halves, weight, *extra)


def spread_kernel(order_ref, act_ref, weight_ref, rows_ref, out_ref, sum_ref, held_ref):
    offset_order(held_ref, act_ref, order_ref[0])
    partial_rows = jnp.dot(held_ref[...], weight_ref[...], preferred_element_type=F32)
    out_ref[...] = partial_rows.astype(BF16)
    products = jnp.sum(partial_rows * rows_ref[...].astype(F32), axis=0, keepdims=True)

    @pl.when(pl.program_id(0) == 0)
    def _():
        sum_ref[...] = products

    @pl.when(pl.program_id(0) > 0)
    def _():
        sum_ref[...] += products


def spread_plain_kernel(order_ref, act_ref, weight_ref, out_ref, held_ref):
    offset_order(held_ref, act_ref, order_ref[0])
    out_ref[...] = jnp.dot(held_ref[...], weight_ref[...], preferred_element_type=F32).astype(BF16)


def spread(after, order, act, weight, core, rows=None):
    count, inner = act.shape
    model = weight.shape[1]
    slots = order.shape[0] // 4
    step = count // (4 * slots)

    first = core * 2 * slots + 1
    specs = [
        pl.BlockSpec((step, inner), lambda i, order: (order[first + i], 0)),
        pl.BlockSpec((inner, model), lambda i, order: (0, 0)),
    ]
    out_specs = [pl.BlockSpec((step, model), lambda i, order: (i, 0))]
    out_shape = [jax.ShapeDtypeStruct((count // 2, model), BF16)]
    operands = (order, *after, act, weight)
    if rows is not None:
        specs.append(pl.BlockSpec((step, model), lambda i, order: (i, 0)))
        out_specs.append(pl.BlockSpec((1, model), lambda i, order: (0, 0)))
        out_shape.append(jax.ShapeDtypeStruct((1, model), F32))
        operands = operands + (rows.reshape(count // 2, model),)
    results = pl.pallas_call(
        without(len(after), spread_plain_kernel if rows is None else spread_kernel, 1),
        grid_spec=pltpu.PrefetchScalarGridSpec(
            num_scalar_prefetch=1,
            grid=(2 * slots,),
            in_specs=[ANYWHERE] * len(after) + specs,
            out_specs=out_specs,
            scratch_shapes=[pltpu.VMEM((step, inner), BF16)],
        ),
        out_shape=out_shape,
        compiler_params=pltpu.CompilerParams(vmem_limit_bytes=VMEM_LIMIT),
        cost_estimate=pl.CostEstimate(
            flops=3 * (count * model * inner),
            bytes_accessed=2 * (count * model + model * inner),
            transcendentals=0,
        ),
        name="spread",
    )(*operands)
    return (results[0].reshape(slots, -1, model),) + tuple(results[1:])


def block_probs(query, keys, seg_q, seg_k, valid_k, first, reach):
    rows, span = query.shape[0], keys.shape[0]
    scores = lax.dot_general(query, keys, (((1,), (1,)), ((), ())), preferred_element_type=F32)
    scores = scores * (HEAD ** (-0.5))
    distance = (
        reach
        + lax.broadcasted_iota(jnp.int32, (rows, span), 0)
        - lax.broadcasted_iota(jnp.int32, (rows, span), 1)
    )
    allowed = (
        (distance >= 0)
        & (distance < WINDOW)
        & (seg_q == seg_k)
        & ((valid_k == 1) | (distance == 0))
    )
    scores = jnp.where(allowed, scores, MASKED)
    powers = jnp.exp(scores - jnp.max(scores, axis=-1, keepdims=True))
    return powers / jnp.sum(powers, axis=-1, keepdims=True)


def attend_kernel(step, reach, q_ref, k_ref, v_ref, segq_ref, segk_ref, valid_ref, out_ref):
    first = pl.multiple_of(pl.program_id(1) * step, step)
    span = pl.ds(first, step + reach)
    probs = block_probs(
        q_ref[...], k_ref[span, :], segq_ref[...], segk_ref[:, span], valid_ref[:, span], first, reach
    )
    out_ref[...] = jnp.dot(
        probs.astype(BF16), v_ref[span, :], preferred_element_type=F32
    ).astype(BF16)


def head_specs(count, step, heads):
    ahead = count // (2 * step)
    return [
        pl.BlockSpec((step, HEAD), lambda h, i: (i + ahead, h)),
        pl.BlockSpec((count, HEAD), lambda h, i: (0, heads + h)),
        pl.BlockSpec((count, HEAD), lambda h, i: (0, 2 * heads + h)),
    ]


def attend(after, projected, seg_q, seg_k, valid_k):
    held, width = projected.shape
    count, width = held // 2, width // 3
    step = count // 4
    heads = width // HEAD
    flops = 4 * count * (step + count) * width
    return pl.pallas_call(
        without(len(after), functools.partial(attend_kernel, step, count)),
        grid=(heads, 4),
        in_specs=[ANYWHERE] * len(after)
        + head_specs(held, step, heads)
        + [
            pl.BlockSpec((step, 1), lambda h, i: (i, 0)),
            pl.BlockSpec((1, held), lambda h, i: (0, 0)),
            pl.BlockSpec((1, held), lambda h, i: (0, 0)),
        ],
        out_specs=pl.BlockSpec((step, HEAD), lambda h, i: (i, h)),
        out_shape=jax.ShapeDtypeStruct((count, width), BF16),
        compiler_params=pltpu.CompilerParams(vmem_limit_bytes=VMEM_LIMIT),
        cost_estimate=pl.CostEstimate(
            flops=9 * (flops), bytes_accessed=8 * held * width, transcendentals=flops // (4 * HEAD)
        ),
        name="attend",
    )(*after, projected, projected, projected, seg_q, seg_k, valid_k)


def attend_back_kernel(
    step, reach, heads, q_ref, k_ref, v_ref, g_ref, segq_ref, segk_ref, valid_ref, cos_ref, sin_ref,
    out_ref, dk_ref, dv_ref,
):
    head, block = pl.program_id(0), pl.program_id(1)
    first = pl.multiple_of(block * step, step)
    span = pl.ds(first, step + reach)
    columns = [pl.ds(pl.multiple_of((part * heads + head) * HEAD, HEAD), HEAD) for part in range(3)]

    @pl.when(block == 0)
    def _():
        dk_ref[...] = jnp.zeros_like(dk_ref)
        dv_ref[...] = jnp.zeros_like(dv_ref)
        out_ref[0:reach, columns[0]] = jnp.zeros((reach, HEAD), BF16)

    query, keys, grad = q_ref[...], k_ref[span, :], g_ref[...]
    probs = block_probs(
        query, keys, segq_ref[...], segk_ref[:, span], valid_ref[:, span], first, reach
    )
    g_probs = lax.dot_general(
        grad, v_ref[span, :], (((1,), (1,)), ((), ())), preferred_element_type=F32
    )
    inner = jnp.sum(probs * g_probs, axis=-1, keepdims=True)
    g_scores = (probs * (g_probs - inner)).astype(BF16)
    scale = HEAD ** (-0.5)
    dq = jnp.dot(g_scores, keys, preferred_element_type=F32) * scale
    here = pl.ds(pl.multiple_of(first + reach, step), step)
    out_ref[here, columns[0]] = turn_back(dq, cos_ref[here, :], sin_ref[here, :]).astype(BF16)
    dk_ref[span, :] += (
        lax.dot_general(g_scores, query, (((0,), (0,)), ((), ())), preferred_element_type=F32)
        * scale
    )
    dv_ref[span, :] += lax.dot_general(
        probs.astype(BF16), grad, (((0,), (0,)), ((), ())), preferred_element_type=F32
    )

    @pl.when(block == pl.num_programs(1) - 1)
    def _():
        out_ref[:, columns[1]] = turn_back(dk_ref[...], cos_ref[...], sin_ref[...]).astype(BF16)
        out_ref[:, columns[2]] = dv_ref[...].astype(BF16)


def attend_back(after, projected, grad, seg_q, seg_k, valid_k, cosine, sine):
    held, width = projected.shape
    count, width = held // 2, width // 3
    step = count // 4
    heads = width // HEAD
    flops = 10 * count * (step + count) * width
    return pl.pallas_call(
        without(len(after), functools.partial(attend_back_kernel, step, count, heads)),
        grid=(heads, 4),
        in_specs=[ANYWHERE] * len(after)
        + head_specs(held, step, heads)
        + [
            pl.BlockSpec((step, HEAD), lambda h, i: (i, h)),
            pl.BlockSpec((step, 1), lambda h, i: (i, 0)),
            pl.BlockSpec((1, held), lambda h, i: (0, 0)),
            pl.BlockSpec((1, held), lambda h, i: (0, 0)),
            pl.BlockSpec((held, HEAD), lambda h, i: (0, 0)),
            pl.BlockSpec((held, HEAD), lambda h, i: (0, 0)),
        ],
        out_specs=pl.BlockSpec((held, 3 * width), lambda h, i: (0, 0)),
        out_shape=jax.ShapeDtypeStruct((held, 3 * width), BF16),
        scratch_shapes=[pltpu.VMEM((held, HEAD), F32)] * 2,
        compiler_params=pltpu.CompilerParams(vmem_limit_bytes=VMEM_LIMIT),
        cost_estimate=pl.CostEstimate(
            flops=6 * (flops), bytes_accessed=12 * held * width, transcendentals=flops // (10 * HEAD)
        ),
        name="attend_back",
    )(*after, projected, projected, projected, grad, seg_q, seg_k, valid_k, cosine, sine)


def one_hot(slot_row, capacity):
    rows = lax.broadcasted_iota(jnp.int32, (capacity, slot_row.shape[1]), 0)
    return slot_row == rows


def moe_in_kernel(
    shape, expert_ref, rows_ref, other_rows_ref, grad_ref, other_grad_ref, win_ref, wdn_ref, slot_ref,
    act_ref, hid_ref, sig_ref, erow_ref, egrad_ref, egate_ref,
):
    experts, own, held, capacity = shape
    here = pl.program_id(0) < pl.num_programs(0) // 2
    rows = jnp.where(here, rows_ref[...], other_rows_ref[...])
    grad = jnp.where(here, grad_ref[...], other_grad_ref[...])
    inputs = dot_nt(rows, win_ref[...])
    gate_in, up_in = inputs[:, :held], inputs[:, held:]
    raw = dot_nt(grad, wdn_ref[...])
    column = lax.broadcasted_iota(jnp.int32, (1, held), 1)
    is_router = (column >= own) & (column < own + experts)
    logits = jnp.where(is_router, up_in, MASKED)
    powers = jnp.exp(logits - jnp.max(logits, axis=-1, keepdims=True))
    picked = jnp.where(column == own + expert_ref[0], powers, 0.0)
    gate = jnp.sum(picked, axis=-1, keepdims=True) / jnp.sum(powers, axis=-1, keepdims=True)
    shared_in = jnp.sum(jnp.where(column == own + experts, up_in, 0.0), axis=-1, keepdims=True)
    shared_gate = 1.0 / (1.0 + jnp.exp(-shared_in))
    sigma = 1.0 / (1.0 + jnp.exp(-gate_in))
    swished = gate_in * sigma
    hidden = swished * up_in
    grad_hidden = shared_gate * raw
    act_ref[:, :held] = (grad_hidden * up_in * sigma * (1.0 + gate_in * (1.0 - sigma))).astype(BF16)
    act_ref[:, held:] = (grad_hidden * swished).astype(BF16)
    hid_ref[...] = (shared_gate * hidden).astype(BF16)
    sig_ref[...] = jnp.sum(hidden * grad_hidden, axis=-1, keepdims=True) * (1.0 - shared_gate)
    place = jnp.where(one_hot(slot_ref[0], capacity), 1.0, 0.0)
    place_low = place.astype(BF16)
    erow_ref[...] = jnp.dot(place_low, rows, preferred_element_type=F32).astype(BF16)
    egrad_ref[...] = jnp.dot(place_low, grad, preferred_element_type=F32).astype(BF16)
    egate_ref[...] = jnp.dot(
        place,
        jnp.broadcast_to(gate, (gate.shape[0], HEAD)),
        precision=lax.Precision.HIGHEST,
        preferred_element_type=F32,
    )


def moe_in(after, expert, rows, grads, chunk, w_in, w_dn, slot_rows, experts, own, capacity):
    blocks, _, step = slot_rows.shape
    model = rows[0].shape[1]
    held = w_dn.shape[0]
    count = blocks * step
    half = blocks // 2

    def row_spec(core):
        def block(i):
            return jnp.maximum(i - half, 0) if core else jnp.minimum(i, half - 1)

        return pl.BlockSpec((step, model), lambda i: (block(i), 0))

    def grad_spec(core):
        def block(i):
            i = jnp.maximum(i - half, 0) if core else jnp.minimum(i, half - 1)
            return ((i // 4) * 2 + chunk) * 4 + i % 4

        return pl.BlockSpec((step, model), lambda i: (block(i), 0))

    return pl.pallas_call(
        without(len(after), functools.partial(moe_in_kernel, (experts, own, held, capacity))),
        grid=(blocks,),
        in_specs=[ANYWHERE] * len(after)
        + [
            pl.BlockSpec(memory_space=pltpu.SMEM),
            row_spec(0),
            row_spec(1),
            grad_spec(0),
            grad_spec(1),
            pl.BlockSpec((2 * held, model), lambda i: (0, 0)),
            pl.BlockSpec((held, model), lambda i: (0, 0)),
            pl.BlockSpec((1, 1, step), lambda i: (i, 0, 0)),
        ],
        out_specs=[
            pl.BlockSpec((step, 2 * held), lambda i: (i, 0)),
            pl.BlockSpec((step, held), lambda i: (i, 0)),
            pl.BlockSpec((step, 1), lambda i: (i, 0)),
            pl.BlockSpec((capacity, model), lambda i: (i, 0)),
            pl.BlockSpec((capacity, model), lambda i: (i, 0)),
            pl.BlockSpec((capacity, HEAD), lambda i: (i, 0)),
        ],
        out_shape=[
            jax.ShapeDtypeStruct((count, 2 * held), BF16),
            jax.ShapeDtypeStruct((count, held), BF16),
            jax.ShapeDtypeStruct((count, 1), F32),
            jax.ShapeDtypeStruct((blocks * capacity, model), BF16),
            jax.ShapeDtypeStruct((blocks * capacity, model), BF16),
            jax.ShapeDtypeStruct((blocks * capacity, HEAD), F32),
        ],
        compiler_params=pltpu.CompilerParams(vmem_limit_bytes=VMEM_LIMIT),
        cost_estimate=pl.CostEstimate(
            flops=2 * (2 * count * model * (3 * held + 2 * capacity)),
            bytes_accessed=6 * count * model,
            transcendentals=2 * count * held,
        ),
        name="moe_in",
    )(*after, expert, *rows, *grads, w_in, w_dn, slot_rows)


def dot_nt(left, right):
    return lax.dot_general(left, right, (((1,), (1,)), ((), ())), preferred_element_type=F32)


def expert_kernel(
    steps, rows_ref, grad_ref, gate_ref, wgu_ref, wd_ref,
    back_ref, out_ref, dgu_ref, hid_ref, ggate_ref, acc_g, acc_u, acc_r,
):
    step = pl.program_id(0)

    @pl.when(step == 0)
    def _():
        acc_g[...] = dot_nt(rows_ref[...], wgu_ref[0])
        acc_u[...] = dot_nt(rows_ref[...], wgu_ref[1])
        acc_r[...] = dot_nt(grad_ref[...], wd_ref[...])

    @pl.when((step > 0) & (step < steps))
    def _():
        acc_g[...] += dot_nt(rows_ref[...], wgu_ref[0])
        acc_u[...] += dot_nt(rows_ref[...], wgu_ref[1])
        acc_r[...] += dot_nt(grad_ref[...], wd_ref[...])

    @pl.when(step == steps)
    def _():
        gate_in, up_in, raw, gates = acc_g[...], acc_u[...], acc_r[...], gate_ref[:, :1]
        sigma = 1.0 / (1.0 + jnp.exp(-gate_in))
        swished = gate_in * sigma
        hidden = swished * up_in
        ggate_ref[...] = jnp.sum(hidden * raw, axis=-1, keepdims=True)
        hid_ref[...] = (gates * hidden).astype(BF16)
        scaled = gates * raw
        dgu_ref[0] = (scaled * up_in * sigma * (1.0 + gate_in * (1.0 - sigma))).astype(BF16)
        dgu_ref[1] = (scaled * swished).astype(BF16)

    @pl.when(step >= steps)
    def _():
        back = jnp.dot(dgu_ref[0], wgu_ref[0], preferred_element_type=F32)
        back = back + jnp.dot(dgu_ref[1], wgu_ref[1], preferred_element_type=F32)
        back_ref[...] = back.astype(BF16)
        out_ref[...] = jnp.dot(hid_ref[...], wd_ref[...], preferred_element_type=F32).astype(BF16)


def run_expert(after, rows, grad, gates, w_gu, w_down):
    count, model = rows.shape
    cols = w_down.shape[0]
    steps = 4
    chunk = model // steps
    return pl.pallas_call(
        without(len(after), functools.partial(expert_kernel, steps)),
        grid=(2 * steps,),
        in_specs=[ANYWHERE] * len(after)
        + [
            pl.BlockSpec((count, chunk), lambda i: (0, jnp.minimum(i, steps - 1))),
            pl.BlockSpec((count, chunk), lambda i: (0, jnp.minimum(i, steps - 1))),
            pl.BlockSpec((count, HEAD), lambda i: (0, 0)),
            pl.BlockSpec((2, cols, chunk), lambda i: (0, 0, i % steps)),
            pl.BlockSpec((cols, chunk), lambda i: (0, i % steps)),
        ],
        out_specs=[
            pl.BlockSpec((count, chunk), lambda i: (0, jnp.maximum(i - steps, 0))),
            pl.BlockSpec((count, chunk), lambda i: (0, jnp.maximum(i - steps, 0))),
            pl.BlockSpec((2, count, cols), lambda i: (0, 0, 0)),
            pl.BlockSpec((count, cols), lambda i: (0, 0)),
            pl.BlockSpec((count, 1), lambda i: (0, 0)),
        ],
        out_shape=[
            jax.ShapeDtypeStruct((count, model), BF16),
            jax.ShapeDtypeStruct((count, model), BF16),
            jax.ShapeDtypeStruct((2, count, cols), BF16),
            jax.ShapeDtypeStruct((count, cols), BF16),
            jax.ShapeDtypeStruct((count, 1), F32),
        ],
        scratch_shapes=[pltpu.VMEM((count, cols), F32)] * 3,
        compiler_params=pltpu.CompilerParams(vmem_limit_bytes=VMEM_LIMIT),
        cost_estimate=pl.CostEstimate(
            flops=2 * (12 * count * model * cols),
            bytes_accessed=8 * count * model + 12 * model * cols,
            transcendentals=count * cols,
        ),
        name="run_expert",
    )(*after, rows, grad, gates, w_gu, w_down)


def sum_kernel(*refs):
    lefts, rights = refs[: len(refs) // 2 - 1], refs[len(refs) // 2 - 1 : -2]
    out_ref, acc_ref = refs[-2:]
    tile = pl.program_id(2)
    total = None
    for left, right in zip(lefts, rights):
        part = lax.dot_general(
            left[0], right[...], (((0,), (0,)), ((), ())), preferred_element_type=F32
        )
        total = part if total is None else total + part

    @pl.when(tile == 0)
    def _():
        acc_ref[...] = total

    @pl.when(tile > 0)
    def _():
        acc_ref[...] += total

    @pl.when(tile == pl.num_programs(2) - 1)
    def _():
        out_ref[0] = acc_ref[...].astype(out_ref.dtype)


def weight_sum(after, terms, tile, steps_of_tiles, dtype):
    parts, _, inner = terms[0][0].shape
    model = terms[0][2].shape[1]
    steps = 4
    width = model // steps

    def left_spec(first):
        return pl.BlockSpec((1, tile, inner), lambda j, d, t: (j, t + first, 0))

    def right_spec(stride, first):
        return pl.BlockSpec((tile, width), lambda j, d, t: (t * stride + first, d))

    return pl.pallas_call(
        without(len(after), sum_kernel),
        grid=(parts, steps, steps_of_tiles),
        in_specs=[ANYWHERE] * len(after)
        + [left_spec(term[1]) for term in terms]
        + [right_spec(*term[3:]) for term in terms],
        out_specs=pl.BlockSpec((1, inner, width), lambda j, d, t: (j, 0, d)),
        out_shape=jax.ShapeDtypeStruct((parts, inner, model), dtype),
        scratch_shapes=[pltpu.VMEM((inner, width), F32)],
        compiler_params=pltpu.CompilerParams(vmem_limit_bytes=VMEM_LIMIT),
        cost_estimate=pl.CostEstimate(
            flops=2 * (2 * len(terms) * parts * steps_of_tiles * tile * inner * model),
            bytes_accessed=len(terms) * 2 * steps_of_tiles * tile * (parts * inner + model)
            + 4 * parts * inner * model,
            transcendentals=0,
        ),
        name="weight_sum",
    )(*after, *[term[0] for term in terms], *[term[2] for term in terms])


def combine_kernel(capacity, taken, *refs):
    out_ref = refs[-1]

    def write(act_ref, weight_ref, slot_ref, rows_ref):
        place = jnp.where(one_hot(slot_ref[0], capacity), 1.0, 0.0).astype(BF16)
        routed = lax.dot_general(
            place, rows_ref[...], (((0,), (0,)), ((), ())), preferred_element_type=F32
        )
        own = jnp.dot(act_ref[...], weight_ref[...], preferred_element_type=F32)
        out_ref[...] = (own + routed).astype(BF16)

    for term in range(len(refs) // 4):
        pl.when(pl.program_id(0) // taken == term)(
            functools.partial(write, *refs[4 * term : 4 * term + 4])
        )


def combine(after, terms, core):
    blocks, _, step = terms[0][2].shape
    model = terms[0][1].shape[1]
    capacity = terms[0][3].shape[0] // blocks
    taken = blocks // 2
    specs, operands, flops = [], [], 0
    for term, (act, weight, slot_rows, rows) in enumerate(terms):
        inner = weight.shape[0]

        def block(i, term=term):
            return core * taken + jnp.clip(i - term * taken, 0, taken - 1)

        specs += [
            pl.BlockSpec((step, inner), lambda i, block=block: (block(i), 0)),
            pl.BlockSpec((inner, model), lambda i: (0, 0)),
            pl.BlockSpec((1, 1, step), lambda i, block=block: (block(i), 0, 0)),
            pl.BlockSpec((capacity, model), lambda i, block=block: (block(i), 0)),
        ]
        operands += [act, weight, slot_rows, rows]
        flops += 2 * taken * step * model * (inner + capacity)
    count = len(terms) * taken * step
    return pl.pallas_call(
        without(len(after), functools.partial(combine_kernel, capacity, taken)),
        grid=(len(terms) * taken,),
        in_specs=[ANYWHERE] * len(after) + specs,
        out_specs=pl.BlockSpec((step, model), lambda i: (i, 0)),
        out_shape=jax.ShapeDtypeStruct((count, model), BF16),
        compiler_params=pltpu.CompilerParams(vmem_limit_bytes=VMEM_LIMIT),
        cost_estimate=pl.CostEstimate(
            flops=3 * (flops),
            bytes_accessed=2 * count * model * (step + capacity) // step,
            transcendentals=0,
        ),
        name="combine",
    )(*after, *operands)


def finish_kernel(hidden_ref, attn_ref, valid_ref, first, second, third, fourth, out_ref, sum_ref):
    residual, attn, valid = hidden_ref[...].astype(F32), attn_ref[...], valid_ref[...]
    moe = first[...] + second[...].astype(F32) + third[...].astype(F32) + fourth[...].astype(F32)
    out_ref[...] = (residual + attn + moe).astype(BF16)
    for place, value in enumerate((residual, attn, moe)):
        sum_ref[0, place] = jnp.sum(valid * value * value)
    sum_ref[0, 3] = jnp.sum(valid)


def finish(after, hidden_in, attn_rows, valid_rows, moe_parts):
    return pl.pallas_call(
        without(len(after), finish_kernel),
        in_specs=[ANYWHERE] * len(after) + [pl.BlockSpec(memory_space=pltpu.VMEM)] * 7,
        out_specs=[pl.BlockSpec(memory_space=pltpu.VMEM), pl.BlockSpec(memory_space=pltpu.SMEM)],
        out_shape=[
            jax.ShapeDtypeStruct(hidden_in.shape, BF16),
            jax.ShapeDtypeStruct((1, 4), F32),
        ],
        compiler_params=pltpu.CompilerParams(vmem_limit_bytes=VMEM_LIMIT),
        name="finish",
    )(*after, hidden_in, attn_rows, valid_rows, *moe_parts)


def norm_scale(rows_in):
    return lax.rsqrt(jnp.mean(rows_in * rows_in, axis=-1, keepdims=True) + EPSILON)


def norm_back(rows_in, scaling, gain, grad):
    unit_rows = rows_in * scaling
    grad_unit = grad * gain
    return scaling * (
        grad_unit - unit_rows * jnp.mean(grad_unit * unit_rows, axis=-1, keepdims=True)
    )


def swish(gate_in):
    return gate_in * jax.nn.sigmoid(gate_in)


def swish_back(gate_in, up_in, grad):
    sigma = jax.nn.sigmoid(gate_in)
    grad_gate = grad * up_in * sigma * (1.0 + gate_in * (1.0 - sigma))
    return (grad_gate, grad * gate_in * sigma)


def rope_tables(first_row, row_count):
    placing = (first_row + jnp.arange(row_count, dtype=jnp.int32)) % SEQ
    frequency = ROPE_BASE ** (-(jnp.arange(HEAD // 2, dtype=F32) * 2.0 / HEAD))
    angles = placing.astype(F32)[:, None] * frequency[None, :]
    cosine, sine = jnp.cos(angles), jnp.sin(angles)
    return (
        jnp.concatenate([cosine, cosine], 1),
        jnp.concatenate([-sine, sine], 1),
    )


def per_device(
    hidden_in,
    cotangent,
    norm_gains,
    qkv_weight,
    qkv_bias,
    out_weight,
    router_weight,
    shared_gate_vec,
    shared_gate_up,
    shared_down,
    expert_gate_up,
    expert_down,
    segments,
    valid_mask,
    routes,
    slots,
):
    groups = lax.axis_size("g")
    blocks = segments.shape[0]
    rows_here, model = hidden_in.shape
    weight_rows, local_cols = qkv_weight.shape[1:]
    shared_cols = shared_gate_up.shape[2]
    experts, top = router_weight.shape[1], routes.shape[1]
    shares = groups * 4 * LINE
    cols = local_cols // 4
    own = shared_cols // shares
    held = -(-(own + experts + 1) // 128) * 128
    capacity = -(-(blocks * top * 4 // (3 * experts)) // 16) * 16
    plane_rows = 4 * blocks
    everywhere = ("g",) + GROUP
    g, z, y, c, x = (lax.axis_index(axis) for axis in EVERY)
    expert = ((g * LINE + z) * 2 + y) * 2 + c

    ahead = [(k, k + 1) for k in range(LINE - 1)]
    behind = [(k + 1, k) for k in range(LINE - 1)]

    residual = hidden_in.astype(F32)
    gain_attn, gain_moe = norm_gains[0], norm_gains[1]
    scale_attn = norm_scale(residual)
    own_attn = (residual * scale_attn * gain_attn).astype(BF16)
    numbers = jnp.concatenate([segments[None], valid_mask[None], routes.T, slots.T], 0)
    numbers = jnp.stack([numbers, swap(numbers, "y")])
    numbers = jnp.stack([numbers, swap(numbers, "c")])
    numbers_here = flip(flip(numbers[:, :, :2], c, 0), y, 1).transpose(2, 1, 0, 3)
    numbers_here = numbers_here.reshape(2, plane_rows)
    numbers_before = jnp.where(z == 0, -1, lax.ppermute(numbers_here, "z", ahead))

    before = lax.ppermute(own_attn, "z", ahead)
    crossed = [cross(cotangent, offset) for offset in range(1, LINE)]

    def cut_heads(value):
        return value.reshape(weight_rows, -1, 4, cols).transpose(2, 0, 1, 3)

    qkv_cut = cut_heads(qkv_weight.transpose(1, 0, 2)).reshape(4, weight_rows, 3 * cols)
    out_cut = cut_heads(out_weight.T).reshape(4, weight_rows, cols)
    w_heads = exchange(jnp.concatenate([qkv_cut, out_cut], 2), ("y", "c"))
    w_heads = w_heads.reshape(4 * weight_rows, 4 * cols)
    qkv_rows = w_heads[:, : 3 * cols]
    qkv_across = cross(qkv_rows, 2)
    later = tick(w_heads)
    attn_pairs, attn_plane, _ = slot_pair(jnp.stack([before, own_attn]), (w_heads, numbers_before))
    rows_attn = attn_plane(tuple(crossed) + (qkv_across,))
    grad_pairs, grad_plane, grad_arrived = slot_pair(
        hold(jnp.stack([cotangent] + crossed), tick(attn_pairs[0])), ()
    )
    w_qkv, qkv_others = gather_line(qkv_rows, qkv_across)
    if groups > 1:
        w_qkv = lax.all_gather(w_qkv, "g", axis=0, tiled=True)

    late_gu, late_dn = hold(shared_gate_up, later), hold(shared_down, later)
    shared_cut = jnp.concatenate(
        [
            late_gu[0].T.reshape(shares, own, weight_rows),
            late_gu[1].T.reshape(shares, own, weight_rows),
            late_dn.reshape(shares, own, weight_rows),
        ],
        1,
    )

    here = x * local_cols + (y * 2 + c) * cols
    bias = lax.dynamic_slice_in_dim(qkv_bias, here, cols, 1).astype(F32).reshape(1, 3 * cols)
    cosine, sine = rope_tables((z + LINE - 1) * plane_rows + later, 2 * plane_rows)
    order = jnp.stack([(y ^ j) * 2 + (c ^ i) for i in range(2) for j in range(2)])
    order = order.astype(jnp.int32)
    order_one = jnp.concatenate([x[None], order])
    order_two = jnp.concatenate([x[None], order[:2], order[:2] + 4, order[2:], order[2:] + 4])
    own_rows, projected = project((), order_two, rows_attn, w_qkv, bias, cosine, sine)
    w_out_rows = hold(w_heads[:, 3 * cols :], tick(qkv_others))
    w_out, _ = gather_line(w_out_rows, hold(cross(w_out_rows, 2), tick(projected)))
    if groups > 1:
        w_out = lax.all_gather(w_out, "g", axis=0, tiled=True)
    numbers = hold(numbers, tick(projected))
    numbers = jnp.stack([numbers] + [cross(numbers, offset) for offset in range(1, LINE)])
    numbers = numbers.reshape(LINE, 1, 4, 2 + 2 * top, blocks)
    if groups > 1:
        numbers = lax.all_gather(numbers, "g", axis=1, tiled=True)
    slot_here = jnp.max(
        jnp.where(numbers[:, :, :, 2 : 2 + top] == expert, numbers[:, :, :, 2 + top :], -1), 3
    )
    slot_here = slot_here.reshape(LINE * groups * 4, 2, 2, rows_here // 2)
    slot_here = flip(slot_here, x, 1).transpose(0, 2, 1, 3).reshape(2, 2, groups, 2, 2, blocks)
    near = jnp.concatenate([numbers_before, numbers_here], 1)
    seg_k, valid_k = near[:1], near[1:]
    seg_q = numbers_here[0].reshape(plane_rows, 1)
    attended = attend(grad_arrived, projected, seg_q, seg_k, valid_k)
    w_out_t = w_out.T
    (send,) = spread((), order_one, attended, w_out_t, 1)
    (keep,) = spread((send,), order_one, attended, w_out_t, 0)
    attn_rows = slot_scatter(keep, send, (slot_here.reshape(-1, blocks),), (), ())[0][0]
    middle = residual + attn_rows
    scale_moe = norm_scale(middle)
    own_moe = (middle * scale_moe * gain_moe).astype(BF16)
    all_grads = [half.reshape(-1, model) for half in grad_plane((own_moe,))]
    crossed = [cross(own_moe, offset) for offset in range(1, LINE)]
    near_pairs, near_plane, _ = slot_pair(jnp.stack([own_moe, crossed[0]]), tuple(crossed[1:]))
    w_shared = exchange(hold(shared_cut, tick(near_pairs[0])), everywhere)
    near_rows = near_plane(())
    far_pairs, far_plane, _ = slot_pair(hold(jnp.stack(crossed[1:]), tick(near_rows[0])), ())
    def whole_slots(halves):
        halves = [half.reshape(-1, model) for half in halves]
        if groups > 1:
            halves = [lax.all_gather(half, "g", axis=0, tiled=True) for half in halves]
        return halves

    all_grads = whole_slots(all_grads)
    chunk_rows = [whole_slots(near_rows)]

    w_shared = w_shared.transpose(1, 0, 2).reshape(3 * own, model)

    def padded(*values):
        value = jnp.concatenate(values, 0)
        return jnp.pad(value, ((0, held - value.shape[0]), (0, 0)))

    shared_in = jnp.concatenate(
        [
            padded(w_shared[:own]),
            padded(w_shared[own : 2 * own], router_weight.T, shared_gate_vec[None]),
        ],
        0,
    )
    shared_dn = padded(w_shared[2 * own :])

    w_gu, w_down = expert_gate_up[0].transpose(0, 2, 1), expert_down[0]
    expert_id = expert.reshape(1).astype(jnp.int32)

    def slots_of(table):
        return table.transpose(3, 2, 0, 1, 4, 5).reshape(-1, 1, blocks)

    def core_part(after, terms, core):
        if groups == 1:
            part = combine(after, terms, core)
        else:
            parts = [combine(after, [term], core) for term in terms]
            parts = [lax.psum_scatter(v, "g", scatter_dimension=0, tiled=True) for v in parts]
            part = jnp.concatenate(parts, 0)
        return part.reshape(-1, plane_rows // 2, model)

    tables = [slots_of(slot_here[chunk : chunk + 1]) for chunk in range(2)]
    acts, hiddens, signals, inputs, grads, results = [], [], [], [], [], []
    gate_grads, backs = [], []

    def enter_chunk(chunk, after):
        act, hid, sig, erow, egrad, egate = moe_in(
            after, expert_id,
            chunk_rows[chunk], all_grads, chunk, shared_in, shared_dn, tables[chunk],
            experts, own, capacity,
        )
        signals.append(sig.reshape(-1, blocks))
        acts.append(act)
        hiddens.append(hid)
        return erow, egrad, egate

    def run_chunk(chunk, after, erow, egrad, egate):
        back, out, dgu, ehid, ggate = run_expert(after, erow, egrad, egate, w_gu, w_down)
        chosen = tables[chunk] == jnp.arange(capacity, dtype=jnp.int32)[None, :, None]
        ggate = ggate.reshape(-1, capacity, 1)
        gate_grads.append(jnp.sum(jnp.where(chosen, ggate, 0.0), axis=1))
        inputs.append((dgu, erow))
        grads.append((ehid, egrad))
        results.append(out)
        backs.append(back)

    def grad_term(chunk):
        return [(acts[chunk], shared_in, tables[chunk], backs[chunk])]

    def moe_term(chunk):
        return [(hiddens[chunk], shared_dn, tables[chunk], results[chunk])]

    entered = enter_chunk(0, (far_pairs[0],))
    far_rows = far_plane((acts[0],))
    chunk_rows.append(whole_slots(far_rows))
    run_chunk(0, (), *entered)
    send = core_part((far_rows[0],), grad_term(0), 1)
    keep = core_part((send,), grad_term(0), 0)
    near_steps = scatter_core(keep, send, ())
    run_chunk(1, (), *enter_chunk(1, (near_steps[0],)))
    near_steps = scatter_pair(near_steps, ())
    send = core_part((near_steps[0],), grad_term(1), 1)
    keep = core_part((send,), grad_term(1), 0)
    near_total = scatter_last(near_steps, ())
    near_cross = cross(near_total[1].astype(BF16), 1)

    far_steps = scatter_core(keep, send, (near_total,))
    moe_terms = moe_term(0) + moe_term(1)
    moe_send = core_part((far_steps[0],), moe_terms, 1)
    moe_keep = core_part((moe_send,), moe_terms, 0)
    signals = jnp.stack([jnp.stack(gate_grads), jnp.stack(signals)])
    signals = signals.reshape(2, 2, 2, groups, 2, 2, 2, 2, rows_here // 2)
    for dim, index in ((1, z // 2), (2, c), (4, z % 2), (5, y), (7, x)):
        signals = flip(signals, index, dim)
    signals = signals.transpose(3, 1, 4, 5, 2, 7, 0, 6, 8).reshape(2 * shares, 2, rows_here)
    far_steps = scatter_pair(far_steps, (moe_keep,))
    moe_steps = scatter_core(moe_keep, moe_send, (far_steps[0],))
    far_total = scatter_last(far_steps, (moe_steps[0],))
    far_cross = [cross(far_total[k].astype(BF16), 2 + k) for k in range(2)]
    moe_steps = scatter_pair(moe_steps, (far_total,))

    tiles = range(2)
    shared_time = (far_total,)
    grad_sgu = weight_sum(
        shared_time,
        [
            (acts[chunk][None], core * groups, chunk_rows[chunk][core], 1, 0)
            for chunk in tiles
            for core in tiles
        ],
        plane_rows,
        groups,
        BF16,
    )[0]
    grad_sdn = weight_sum(
        shared_time,
        [
            (hiddens[chunk][None], core * groups, all_grads[core], 2, chunk)
            for chunk in tiles
            for core in tiles
        ],
        plane_rows,
        groups,
        BF16,
    )[0]
    grad_normed = near_total[0] + near_cross.astype(F32)
    grad_normed = grad_normed + far_cross[0].astype(F32) + far_cross[1].astype(F32)
    grad_normed = hold(grad_normed, tick(grad_sgu) + tick(grad_sdn) + tick(moe_steps[0]))
    shared_grad = jnp.concatenate(
        [grad_sgu[:own], grad_sgu[held : held + own], grad_sdn[:own]], 0
    )
    shared_grad = shared_grad.reshape(3 * own, shares, weight_rows).transpose(1, 0, 2)
    shared_grad = exchange(shared_grad, everywhere)
    shared_grad_sent = shared_grad
    shared_grad = shared_grad.reshape(shares, 3, own, weight_rows).transpose(1, 0, 2, 3)
    shared_grad = shared_grad.reshape(3, shared_cols, weight_rows).astype(F32)
    grad_sgu = shared_grad[:2].transpose(0, 2, 1)

    signals = exchange(hold(signals, tick(far_total)), EVERY)
    signals = signals.reshape(experts, 2, 2, rows_here)
    grad_router_probs = jnp.sum(signals[:, :, 0], axis=1).T
    gate_signal = jnp.sum(signals[:, :, 1], axis=(0, 1))

    own_logits = jnp.dot(own_moe, router_weight, preferred_element_type=F32)
    router_probs = jax.nn.softmax(own_logits, axis=-1)
    grad_logits = router_probs * (
        grad_router_probs - jnp.sum(router_probs * grad_router_probs, axis=-1, keepdims=True)
    )
    grad_normed = (
        grad_normed
        + gate_signal[:, None] * shared_gate_vec.astype(F32)[None, :]
        + jnp.einsum("te,de->td", grad_logits, router_weight.astype(F32))
    )
    own_float = own_moe.astype(F32)
    grad_router = jnp.einsum("td,te->ed", own_float, grad_logits)
    grad_gate_vec = jnp.sum(gate_signal[:, None] * own_float, axis=0)
    grad_gain_moe = jnp.sum(grad_normed * (middle * scale_moe), axis=0)
    grad_middle = cotangent.astype(F32) + norm_back(middle, scale_moe, gain_moe, grad_normed)
    grad_attn = grad_middle.astype(BF16)

    _, plane, _ = slot_pair(grad_attn[None], (moe_steps[1], moe_steps[3]))
    moe_parts = scatter_last(moe_steps, (grad_attn,))
    moe_cross = [cross(moe_parts[k].astype(BF16), k) for k in range(1, LINE)]
    plane_grad, grad_attended = project((), order_one, plane((moe_parts,)), w_out)

    def weight_grad(left, right):
        return lax.dot_general(left, right, (((0,), (0,)), ((), ())), preferred_element_type=F32)

    def to_weight_owners(value):
        if groups > 1:
            value = lax.psum_scatter(value, "g", scatter_dimension=0, tiled=True)
        value, mark = scatter_line(value)
        return exchange(value.reshape(4, weight_rows, -1), ("y", "c")).astype(F32), mark

    grad_out = weight_grad(plane_grad, attended).astype(BF16)
    grad_projected = attend_back(
        (grad_out, shared_grad_sent, moe_cross[0]),
        projected, grad_attended, seg_q, seg_k, valid_k, cosine, sine,
    )
    grad_qkv = weight_grad(own_rows, grad_projected).astype(BF16)
    grad_out, out_marks = to_weight_owners(grad_out)
    grad_out = grad_out.transpose(1, 0, 2).reshape(weight_rows, local_cols).T
    tile = inputs[0][1].shape[0]
    grad_egu = weight_sum(
        (grad_projected,), [(left, 0, right, 1, 0) for left, right in inputs], tile, 1, F32
    )
    grad_qkv, qkv_marks = to_weight_owners(grad_qkv)
    grad_edown = weight_sum(
        (grad_egu,), [(left[None], 0, right, 1, 0) for left, right in grads], tile, 1, F32
    )
    grad_qkv = grad_qkv.reshape(4, weight_rows, 3, cols).transpose(2, 1, 0, 3)
    grad_qkv = grad_qkv.reshape(3, weight_rows, local_cols)
    w_qkv_t = w_qkv.T
    send, sum_send = spread(
        (qkv_marks[0], out_marks[1], moe_cross[1]),
        order_two, grad_projected, w_qkv_t, 1, rows_attn[1],
    )
    keep, sum_keep = spread((send, moe_cross[2], grad_egu), order_two, grad_projected, w_qkv_t, 0, rows_attn[0])
    gain_sum = (sum_send + sum_keep)[0] / gain_attn
    bias_sum = jnp.sum(grad_projected.astype(F32), axis=0).reshape(3, cols)
    grad_bias = lax.dynamic_update_slice_in_dim(jnp.zeros((3, model), F32), bias_sum, here, 1)

    valid_rows = lax.dynamic_slice_in_dim(valid_mask, x * rows_here, rows_here, 0).astype(F32)
    output, squares = finish(
        (grad_projected,), hidden_in, attn_rows, valid_rows[:, None], [moe_parts[0]] + moe_cross
    )

    sums_of_all = all_sum(
        jnp.concatenate(
            [
                grad_router,
                grad_gate_vec[None],
                grad_gain_moe[None],
                hold(gain_sum[None], tick(grad_edown) + tick(grad_sgu)),
                grad_bias,
                jnp.pad(squares, ((0, 0), (0, model - 4))),
            ],
            0,
        )
    )
    back_both, _ = slot_scatter(
        keep, send, (qkv_marks[1], out_marks[2]), (qkv_marks[2], grad_edown), ()
    )
    back_own = back_both[1] + lax.ppermute(back_both[0].astype(BF16), "z", behind).astype(F32)
    input_grad = grad_middle + norm_back(residual, scale_attn, gain_attn, back_own)
    others = sums_of_all[experts:]
    root_means = jnp.sqrt(others[6, :3] / (jnp.maximum(others[6, 3], 1.0) * model))
    return (
        output,
        input_grad,
        jnp.stack([others[2], others[1]]),
        grad_qkv,
        others[3:6],
        grad_out,
        sums_of_all[:experts].T,
        others[0],
        grad_sgu,
        shared_grad[2],
        grad_egu.transpose(0, 2, 1)[None],
        grad_edown,
        root_means[0],
        root_means[1],
        root_means[2],
    )


def solution(mesh):
    dp, mp = mesh.shape["dp"], mesh.shape["mp"]
    inner = Mesh(mesh.devices.reshape(dp // (4 * LINE), LINE, 2, 2, mp), EVERY)
    d = ("g",) + GROUP
    placed = (
        P(EVERY, None),
        P(EVERY, None),
        P(),
        P(None, d, "x"),
        P(),
        P("x", d),
        P(),
        P(),
        P(None, d, "x"),
        P("x", d),
        P(d, None, None, "x"),
        P(d, "x", None),
        P(d),
        P(d),
        P(d, None),
        P(d, None),
    )
    return jax.shard_map(
        per_device,
        mesh=inner,
        in_specs=placed,
        out_specs=(
            P(EVERY, None),
            P(EVERY, None),
            P(),
            P(None, d, "x"),
            P(),
            P("x", d),
            P(),
            P(),
            P(None, d, "x"),
            P("x", d),
            P(d, None, None, "x"),
            P(d, "x", None),
            P(),
            P(),
            P(),
        ),
        check_vma=False,
    )
```

```python
import functools

import jax
import jax.numpy as jnp
from jax import lax
from jax.experimental import pallas as pl
from jax.experimental.pallas import tpu as pltpu
from jax.sharding import Mesh
from jax.sharding import PartitionSpec as P

HEAD = 128
SEQ = 4096
WINDOW = 1024

EPSILON = 1e-06
ROPE_BASE = 1000000.0
MASKED = -1e30

LINE = 4
GROUP = ("z", "y", "c")
EVERY = ("g", "z", "y", "c", "x")
SWAP = [(0, 1), (1, 0)]
VMEM_LIMIT = 56 * 1024 * 1024

F32 = jnp.float32
BF16 = jnp.bfloat16


def swap(value, axis):
    return lax.ppermute(value, axis, SWAP)


def cross(value, offset):
    return lax.ppermute(value, "z", [(k, k ^ offset) for k in range(LINE)])


def take(value, index, dim):
    return lax.dynamic_index_in_dim(value, index, dim, keepdims=False)


def split(value, index, dim):
    return take(value, index, dim), take(value, 1 - index, dim)


ANYWHERE = pl.BlockSpec(memory_space=pl.ANY)


def without(count, kernel, first=0):
    def run(*refs):
        kernel(*refs[:first], *refs[first + count :])

    return run


def stage(kernel, after, inputs, outputs, name):
    count, _, width = inputs[0].shape
    parts = max(1, 4 // count)

    def spec(rows):
        return pl.BlockSpec((1, rows, width // parts), lambda i, j: (i, 0, j))

    return pl.pallas_call(
        without(len(after), kernel),
        grid=(count, parts),
        in_specs=[ANYWHERE] * len(after) + [spec(v.shape[1]) for v in inputs],
        out_specs=[spec(rows) for rows, _ in outputs],
        out_shape=[jax.ShapeDtypeStruct((count, rows, width), kind) for rows, kind in outputs],
        compiler_params=pltpu.CompilerParams(vmem_limit_bytes=VMEM_LIMIT),
        cost_estimate=pl.CostEstimate(
            flops=0, bytes_accessed=8 * count * width * sum(rows for rows, _ in outputs), transcendentals=0
        ),
        name=name,
    )(*after, *inputs)


def pair_kernel(first, first_x, second, second_y, out_first, out_second):
    half = first.shape[1]
    out_first[0, :half] = first[0]
    out_first[0, half:] = first_x[0]
    out_second[0, :half] = second[0]
    out_second[0, half:] = second_y[0]


def plane_kernel(first, first_y, second, second_x, out):
    rows = first.shape[1]
    half = rows // 2
    for y, source in enumerate((first, first_y)):
        out[0, 2 * y * rows : (2 * y + 1) * rows] = source[0]
    for x, source in enumerate((second, second_x)):
        for y in range(2):
            start = (2 * y + 1) * rows + x * half
            out[0, start : start + half] = source[0, y * half : (y + 1) * half]


def slot_pair(shards, after):
    rows = shards.shape[1]
    half = rows // 2
    first, second = shards[:, :half], shards[:, half:]
    pairs = stage(
        pair_kernel,
        after,
        [first, swap(first, "x"), second, swap(second, "y")],
        [(rows, BF16)] * 2,
        "pair",
    )
    arrived = swap(pairs[0], "y"), swap(pairs[1], "x")

    def plane(after):
        (own,) = stage(
            plane_kernel,
            after,
            [pairs[0], arrived[0], pairs[1], arrived[1]],
            [(4 * rows, BF16)],
            "plane",
        )
        return own, swap(own, "c")

    return pairs, plane, arrived


def slot_gather(shards, after_pair, after_plane):
    pairs, plane, _ = slot_pair(shards, after_pair)
    halves = plane(after_plane)
    return halves, (pairs[0], halves[0])


def core_sum_kernel(keep, arrived, first, first_send, second, second_send):
    rows = first.shape[1]
    half = rows // 2

    def total(start, count):
        here = slice(start, start + count)
        return keep[0, here].astype(F32) + arrived[0, here].astype(F32)

    first[0] = total(0, rows)
    first_send[0] = total(2 * rows, rows).astype(BF16)
    for y in range(2):
        start = (2 * y + 1) * rows
        second[0, y * half : (y + 1) * half] = total(start, half)
        second_send[0, y * half : (y + 1) * half] = total(start + half, half).astype(BF16)


def pair_sum_kernel(first, first_y, second, second_x, first_keep, first_send, second_keep, second_send):
    half = first_keep.shape[1]
    for value, arrived, keep, send in (
        (first, first_y, first_keep, first_send),
        (second, second_x, second_keep, second_send),
    ):
        keep[0] = value[0, :half] + arrived[0, :half].astype(F32)
        send[0] = (value[0, half:] + arrived[0, half:].astype(F32)).astype(BF16)


def last_sum_kernel(first, first_x, second, second_y, out):
    half = first.shape[1]
    out[0, :half] = first[0] + first_x[0].astype(F32)
    out[0, half:] = second[0] + second_y[0].astype(F32)


def scatter_core(keep, send, after):
    rows = keep.shape[1] // 4
    first, first_send, second, second_send = stage(
        core_sum_kernel,
        after,
        [keep, swap(send, "c")],
        [(rows, F32), (rows, BF16)] * 2,
        "core_sum",
    )
    return first, swap(first_send, "y"), second, swap(second_send, "x")


def scatter_pair(steps, after):
    half = steps[0].shape[1] // 2
    first, first_send, second, second_send = stage(
        pair_sum_kernel,
        after,
        list(steps),
        [(half, F32), (half, BF16)] * 2,
        "pair_sum",
    )
    return first, swap(first_send, "x"), second, swap(second_send, "y")


def scatter_last(steps, after):
    (whole,) = stage(
        last_sum_kernel, after, list(steps), [(2 * steps[0].shape[1], F32)], "last_sum"
    )
    return whole


def slot_scatter(keep, send, after_core, after_pair, after_last):
    core = scatter_core(keep, send, after_core)
    pair = scatter_pair(core, after_pair)
    return scatter_last(pair, after_last), (core[0], core[1], pair[0], pair[1])


def tick_kernel(marker_ref, out_ref):
    corner = marker_ref[...].astype(F32)
    out_ref[0, 0] = jnp.where(jnp.max(corner) <= 3.4e38, 0, 1).astype(jnp.int32)


def tick(marker):
    lead = marker.ndim - 2
    block = (1,) * lead + (min(16, marker.shape[-2]), min(HEAD, marker.shape[-1]))
    flag = pl.pallas_call(
        tick_kernel,
        grid=(1,),
        in_specs=[pl.BlockSpec(block, lambda i: (0,) * marker.ndim)],
        out_specs=pl.BlockSpec(memory_space=pltpu.SMEM),
        out_shape=jax.ShapeDtypeStruct((1, 1), jnp.int32),
        name="tick",
    )(marker)
    return flag[0, 0]


def hold(value, flag):
    return jnp.where(flag == 0, value, jnp.zeros_like(value))


def all_sum(value):
    for axis in ("c", "x", "y"):
        value = value + swap(value, axis)
    for offset in (1, 2):
        value = value + cross(value, offset)
    return lax.psum(value, "g") if lax.axis_size("g") > 1 else value


def flip(value, index, dim):
    return jnp.where(index == 0, value, jnp.flip(value, dim))


def gather_line(value, across):
    z = lax.axis_index("z")
    others = cross(jnp.stack([value, across]), 1)
    held = [[value, others[0]], [across, others[1]]]
    placed = []
    for high in range(2):
        for low in range(2):
            rows = [jnp.where(z % 2 == low, held[k][0], held[k][1]) for k in range(2)]
            placed.append(jnp.where(z // 2 == high, rows[0], rows[1]))
    return jnp.concatenate(placed, 0), others


def scatter_line(value):
    z = lax.axis_index("z")
    parts = value.reshape(2, 2, -1, value.shape[-1])
    keep, send = split(parts, z % 2, 1)
    marks = [send, cross(send, 1)]
    keep = keep.astype(F32) + marks[1].astype(F32)
    keep, send = split(keep, z // 2, 0)
    send = send.astype(BF16)
    marks += [cross(send, 2), send]
    return (keep + marks[2].astype(F32)).astype(BF16), marks


def exchange(value, axes):
    return lax.all_to_all(value, axes, split_axis=0, concat_axis=0, tiled=True)


def turn(value, cosine, sine):
    return value * cosine + pltpu.roll(value, HEAD // 2, 1) * sine


def turn_back(value, cosine, sine):
    return value * cosine - pltpu.roll(value, HEAD // 2, 1) * sine


def own_order(target_ref, source_ref, x):
    part = source_ref.shape[0] // 4
    for half in range(2):
        for offset in range(2):
            side = x if offset == 0 else 1 - x
            place = pl.multiple_of((side * 2 + half) * part, part)
            start = (half * 2 + offset) * part
            target_ref[pl.ds(place, part), :] = source_ref[start : start + part, :]


def offset_order(target_ref, source_ref, x):
    part = source_ref.shape[0] // 4
    for half in range(2):
        for offset in range(2):
            side = x if offset == 0 else 1 - x
            place = pl.multiple_of((side * 2 + half) * part, part)
            start = (half * 2 + offset) * part
            target_ref[start : start + part, :] = source_ref[pl.ds(place, part), :]


def place_block(own_ref, halves, half_steps, x):
    for half, source in enumerate(halves):

        @pl.when(pl.program_id(0) // half_steps == half)
        def _():
            own_order(own_ref, source, x)


def project_kernel(heads, half_steps, order_ref, rows_ref, other_ref, weight_ref, bias_ref, cos_ref, sin_ref, own_ref, out_ref):
    place_block(own_ref, (rows_ref, other_ref), half_steps, order_ref[0])
    projected = (
        jnp.dot(own_ref[...], weight_ref[...], preferred_element_type=F32) + bias_ref[...]
    )
    for part in range(3 * heads):
        block = projected[:, part * HEAD : (part + 1) * HEAD]
        if part < 2 * heads:
            block = turn(block, cos_ref[...], sin_ref[...])
        out_ref[:, part * HEAD : (part + 1) * HEAD] = block.astype(BF16)


def plain_kernel(half_steps, order_ref, rows_ref, other_ref, weight_ref, own_ref, out_ref):
    place_block(own_ref, (rows_ref, other_ref), half_steps, order_ref[0])
    out_ref[...] = jnp.dot(
        own_ref[...], weight_ref[...], preferred_element_type=F32
    ).astype(BF16)


def project(after, order, halves, weight, bias=None, cosine=None, sine=None):
    slots, half_rows, model = halves[0].shape
    halves = [half.reshape(slots * half_rows, model) for half in halves]
    count = 2 * slots * half_rows
    width = weight.shape[1]
    step = half_rows // 2
    steps = 2 * slots
    arrived = [
        pl.BlockSpec((step, model), lambda i, order: (jnp.minimum(i, steps - 1), 0)),
        pl.BlockSpec((step, model), lambda i, order: (jnp.maximum(i - steps, 0), 0)),
    ]
    whole = pl.BlockSpec((model, width), lambda i, order: (0, 0))

    def placed(columns):
        return pl.BlockSpec((step, columns), lambda i, order: (order[i + 1], 0))

    if bias is None:
        kernel, specs, extra = functools.partial(plain_kernel, steps), arrived + [whole], ()
    else:
        kernel = functools.partial(project_kernel, width // (3 * HEAD), steps)
        row = pl.BlockSpec((1, width), lambda i, order: (0, 0))
        specs = arrived + [whole, row, placed(HEAD), placed(HEAD)]
        extra = (bias, cosine, sine)
    return pl.pallas_call(
        without(len(after), kernel, 1),
        grid_spec=pltpu.PrefetchScalarGridSpec(
            num_scalar_prefetch=1,
            grid=(2 * steps,),
            in_specs=[ANYWHERE] * len(after) + specs,
            out_specs=[placed(model), placed(width)],
        ),
        out_shape=[
            jax.ShapeDtypeStruct((count, model), BF16),
            jax.ShapeDtypeStruct((count, width), BF16),
        ],
        compiler_params=pltpu.CompilerParams(vmem_limit_bytes=VMEM_LIMIT),
        cost_estimate=pl.CostEstimate(
            flops=3 * (2 * count * model * width),
            bytes_accessed=2 * (2 * count * model + model * width + count * width),
            transcendentals=0,
        ),
        name="project",
    )(order, *after, *halves, weight, *extra)


def spread_kernel(order_ref, act_ref, weight_ref, rows_ref, out_ref, sum_ref, held_ref):
    offset_order(held_ref, act_ref, order_ref[0])
    partial_rows = jnp.dot(held_ref[...], weight_ref[...], preferred_element_type=F32)
    out_ref[...] = partial_rows.astype(BF16)
    products = jnp.sum(partial_rows * rows_ref[...].astype(F32), axis=0, keepdims=True)

    @pl.when(pl.program_id(0) == 0)
    def _():
        sum_ref[...] = products

    @pl.when(pl.program_id(0) > 0)
    def _():
        sum_ref[...] += products


def spread_plain_kernel(order_ref, act_ref, weight_ref, out_ref, held_ref):
    offset_order(held_ref, act_ref, order_ref[0])
    out_ref[...] = jnp.dot(held_ref[...], weight_ref[...], preferred_element_type=F32).astype(BF16)


def spread(after, order, act, weight, core, rows=None):
    count, inner = act.shape
    model = weight.shape[1]
    slots = order.shape[0] // 4
    step = count // (4 * slots)

    first = core * 2 * slots + 1
    specs = [
        pl.BlockSpec((step, inner), lambda i, order: (order[first + i], 0)),
        pl.BlockSpec((inner, model), lambda i, order: (0, 0)),
    ]
    out_specs = [pl.BlockSpec((step, model), lambda i, order: (i, 0))]
    out_shape = [jax.ShapeDtypeStruct((count // 2, model), BF16)]
    operands = (order, *after, act, weight)
    if rows is not None:
        specs.append(pl.BlockSpec((step, model), lambda i, order: (i, 0)))
        out_specs.append(pl.BlockSpec((1, model), lambda i, order: (0, 0)))
        out_shape.append(jax.ShapeDtypeStruct((1, model), F32))
        operands = operands + (rows.reshape(count // 2, model),)
    results = pl.pallas_call(
        without(len(after), spread_plain_kernel if rows is None else spread_kernel, 1),
        grid_spec=pltpu.PrefetchScalarGridSpec(
            num_scalar_prefetch=1,
            grid=(2 * slots,),
            in_specs=[ANYWHERE] * len(after) + specs,
            out_specs=out_specs,
            scratch_shapes=[pltpu.VMEM((step, inner), BF16)],
        ),
        out_shape=out_shape,
        compiler_params=pltpu.CompilerParams(vmem_limit_bytes=VMEM_LIMIT),
        cost_estimate=pl.CostEstimate(
            flops=3 * (count * model * inner),
            bytes_accessed=2 * (count * model + model * inner),
            transcendentals=0,
        ),
        name="spread",
    )(*operands)
    return (results[0].reshape(slots, -1, model),) + tuple(results[1:])


def block_probs(query, keys, seg_q, seg_k, valid_k, first, reach):
    rows, span = query.shape[0], keys.shape[0]
    scores = lax.dot_general(query, keys, (((1,), (1,)), ((), ())), preferred_element_type=F32)
    scores = scores * (HEAD ** (-0.5))
    distance = (
        reach
        + lax.broadcasted_iota(jnp.int32, (rows, span), 0)
        - lax.broadcasted_iota(jnp.int32, (rows, span), 1)
    )
    allowed = (
        (distance >= 0)
        & (distance < WINDOW)
        & (seg_q == seg_k)
        & ((valid_k == 1) | (distance == 0))
    )
    scores = jnp.where(allowed, scores, MASKED)
    powers = jnp.exp(scores - jnp.max(scores, axis=-1, keepdims=True))
    return powers / jnp.sum(powers, axis=-1, keepdims=True)


def attend_kernel(step, reach, q_ref, k_ref, v_ref, segq_ref, segk_ref, valid_ref, out_ref):
    first = pl.multiple_of(pl.program_id(1) * step, step)
    span = pl.ds(first, step + reach)
    probs = block_probs(
        q_ref[...], k_ref[span, :], segq_ref[...], segk_ref[:, span], valid_ref[:, span], first, reach
    )
    out_ref[...] = jnp.dot(
        probs.astype(BF16), v_ref[span, :], preferred_element_type=F32
    ).astype(BF16)


def head_specs(count, step, heads):
    ahead = count // (2 * step)
    return [
        pl.BlockSpec((step, HEAD), lambda h, i: (i + ahead, h)),
        pl.BlockSpec((count, HEAD), lambda h, i: (0, heads + h)),
        pl.BlockSpec((count, HEAD), lambda h, i: (0, 2 * heads + h)),
    ]


def attend(after, projected, seg_q, seg_k, valid_k):
    held, width = projected.shape
    count, width = held // 2, width // 3
    step = count // 4
    heads = width // HEAD
    flops = 4 * count * (step + count) * width
    return pl.pallas_call(
        without(len(after), functools.partial(attend_kernel, step, count)),
        grid=(heads, 4),
        in_specs=[ANYWHERE] * len(after)
        + head_specs(held, step, heads)
        + [
            pl.BlockSpec((step, 1), lambda h, i: (i, 0)),
            pl.BlockSpec((1, held), lambda h, i: (0, 0)),
            pl.BlockSpec((1, held), lambda h, i: (0, 0)),
        ],
        out_specs=pl.BlockSpec((step, HEAD), lambda h, i: (i, h)),
        out_shape=jax.ShapeDtypeStruct((count, width), BF16),
        compiler_params=pltpu.CompilerParams(vmem_limit_bytes=VMEM_LIMIT),
        cost_estimate=pl.CostEstimate(
            flops=9 * (flops), bytes_accessed=8 * held * width, transcendentals=flops // (4 * HEAD)
        ),
        name="attend",
    )(*after, projected, projected, projected, seg_q, seg_k, valid_k)


def attend_back_kernel(
    step, reach, heads, q_ref, k_ref, v_ref, g_ref, segq_ref, segk_ref, valid_ref, cos_ref, sin_ref,
    out_ref, dk_ref, dv_ref,
):
    head, block = pl.program_id(0), pl.program_id(1)
    first = pl.multiple_of(block * step, step)
    span = pl.ds(first, step + reach)
    columns = [pl.ds(pl.multiple_of((part * heads + head) * HEAD, HEAD), HEAD) for part in range(3)]

    @pl.when(block == 0)
    def _():
        dk_ref[...] = jnp.zeros_like(dk_ref)
        dv_ref[...] = jnp.zeros_like(dv_ref)
        out_ref[0:reach, columns[0]] = jnp.zeros((reach, HEAD), BF16)

    query, keys, grad = q_ref[...], k_ref[span, :], g_ref[...]
    probs = block_probs(
        query, keys, segq_ref[...], segk_ref[:, span], valid_ref[:, span], first, reach
    )
    g_probs = lax.dot_general(
        grad, v_ref[span, :], (((1,), (1,)), ((), ())), preferred_element_type=F32
    )
    inner = jnp.sum(probs * g_probs, axis=-1, keepdims=True)
    g_scores = (probs * (g_probs - inner)).astype(BF16)
    scale = HEAD ** (-0.5)
    dq = jnp.dot(g_scores, keys, preferred_element_type=F32) * scale
    here = pl.ds(pl.multiple_of(first + reach, step), step)
    out_ref[here, columns[0]] = turn_back(dq, cos_ref[here, :], sin_ref[here, :]).astype(BF16)
    dk_ref[span, :] += (
        lax.dot_general(g_scores, query, (((0,), (0,)), ((), ())), preferred_element_type=F32)
        * scale
    )
    dv_ref[span, :] += lax.dot_general(
        probs.astype(BF16), grad, (((0,), (0,)), ((), ())), preferred_element_type=F32
    )

    @pl.when(block == pl.num_programs(1) - 1)
    def _():
        out_ref[:, columns[1]] = turn_back(dk_ref[...], cos_ref[...], sin_ref[...]).astype(BF16)
        out_ref[:, columns[2]] = dv_ref[...].astype(BF16)


def attend_back(after, projected, grad, seg_q, seg_k, valid_k, cosine, sine):
    held, width = projected.shape
    count, width = held // 2, width // 3
    step = count // 4
    heads = width // HEAD
    flops = 10 * count * (step + count) * width
    return pl.pallas_call(
        without(len(after), functools.partial(attend_back_kernel, step, count, heads)),
        grid=(heads, 4),
        in_specs=[ANYWHERE] * len(after)
        + head_specs(held, step, heads)
        + [
            pl.BlockSpec((step, HEAD), lambda h, i: (i, h)),
            pl.BlockSpec((step, 1), lambda h, i: (i, 0)),
            pl.BlockSpec((1, held), lambda h, i: (0, 0)),
            pl.BlockSpec((1, held), lambda h, i: (0, 0)),
            pl.BlockSpec((held, HEAD), lambda h, i: (0, 0)),
            pl.BlockSpec((held, HEAD), lambda h, i: (0, 0)),
        ],
        out_specs=pl.BlockSpec((held, 3 * width), lambda h, i: (0, 0)),
        out_shape=jax.ShapeDtypeStruct((held, 3 * width), BF16),
        scratch_shapes=[pltpu.VMEM((held, HEAD), F32)] * 2,
        compiler_params=pltpu.CompilerParams(vmem_limit_bytes=VMEM_LIMIT),
        cost_estimate=pl.CostEstimate(
            flops=6 * (flops), bytes_accessed=12 * held * width, transcendentals=flops // (10 * HEAD)
        ),
        name="attend_back",
    )(*after, projected, projected, projected, grad, seg_q, seg_k, valid_k, cosine, sine)


def one_hot(slot_row, capacity):
    rows = lax.broadcasted_iota(jnp.int32, (capacity, slot_row.shape[1]), 0)
    return slot_row == rows


def moe_in_kernel(
    shape, expert_ref, rows_ref, other_rows_ref, grad_ref, other_grad_ref, win_ref, wdn_ref, slot_ref,
    act_ref, hid_ref, sig_ref, erow_ref, egrad_ref, egate_ref,
):
    experts, own, held, capacity = shape
    here = pl.program_id(0) < pl.num_programs(0) // 2
    rows = jnp.where(here, rows_ref[...], other_rows_ref[...])
    grad = jnp.where(here, grad_ref[...], other_grad_ref[...])
    inputs = dot_nt(rows, win_ref[...])
    gate_in, up_in = inputs[:, :held], inputs[:, held:]
    raw = dot_nt(grad, wdn_ref[...])
    column = lax.broadcasted_iota(jnp.int32, (1, held), 1)
    is_router = (column >= own) & (column < own + experts)
    logits = jnp.where(is_router, up_in, MASKED)
    powers = jnp.exp(logits - jnp.max(logits, axis=-1, keepdims=True))
    picked = jnp.where(column == own + expert_ref[0], powers, 0.0)
    gate = jnp.sum(picked, axis=-1, keepdims=True) / jnp.sum(powers, axis=-1, keepdims=True)
    shared_in = jnp.sum(jnp.where(column == own + experts, up_in, 0.0), axis=-1, keepdims=True)
    shared_gate = 1.0 / (1.0 + jnp.exp(-shared_in))
    sigma = 1.0 / (1.0 + jnp.exp(-gate_in))
    swished = gate_in * sigma
    hidden = swished * up_in
    grad_hidden = shared_gate * raw
    act_ref[:, :held] = (grad_hidden * up_in * sigma * (1.0 + gate_in * (1.0 - sigma))).astype(BF16)
    act_ref[:, held:] = (grad_hidden * swished).astype(BF16)
    hid_ref[...] = (shared_gate * hidden).astype(BF16)
    sig_ref[...] = jnp.sum(hidden * grad_hidden, axis=-1, keepdims=True) * (1.0 - shared_gate)
    place = jnp.where(one_hot(slot_ref[0], capacity), 1.0, 0.0)
    place_low = place.astype(BF16)
    erow_ref[...] = jnp.dot(place_low, rows, preferred_element_type=F32).astype(BF16)
    egrad_ref[...] = jnp.dot(place_low, grad, preferred_element_type=F32).astype(BF16)
    egate_ref[...] = jnp.dot(
        place,
        jnp.broadcast_to(gate, (gate.shape[0], HEAD)),
        precision=lax.Precision.HIGHEST,
        preferred_element_type=F32,
    )


def moe_in(after, expert, rows, grads, w_in, w_dn, slot_rows, experts, own, capacity):
    blocks, _, step = slot_rows.shape
    model = rows[0].shape[1]
    held = w_dn.shape[0]
    count = blocks * step
    half = blocks // 2

    def row_spec(core):
        def block(i):
            return jnp.maximum(i - half, 0) if core else jnp.minimum(i, half - 1)

        return pl.BlockSpec((step, model), lambda i: (block(i), 0))

    return pl.pallas_call(
        without(len(after), functools.partial(moe_in_kernel, (experts, own, held, capacity))),
        grid=(blocks,),
        in_specs=[ANYWHERE] * len(after)
        + [
            pl.BlockSpec(memory_space=pltpu.SMEM),
            row_spec(0),
            row_spec(1),
            row_spec(0),
            row_spec(1),
            pl.BlockSpec((2 * held, model), lambda i: (0, 0)),
            pl.BlockSpec((held, model), lambda i: (0, 0)),
            pl.BlockSpec((1, 1, step), lambda i: (i, 0, 0)),
        ],
        out_specs=[
            pl.BlockSpec((step, 2 * held), lambda i: (i, 0)),
            pl.BlockSpec((step, held), lambda i: (i, 0)),
            pl.BlockSpec((step, 1), lambda i: (i, 0)),
            pl.BlockSpec((capacity, model), lambda i: (i, 0)),
            pl.BlockSpec((capacity, model), lambda i: (i, 0)),
            pl.BlockSpec((capacity, HEAD), lambda i: (i, 0)),
        ],
        out_shape=[
            jax.ShapeDtypeStruct((count, 2 * held), BF16),
            jax.ShapeDtypeStruct((count, held), BF16),
            jax.ShapeDtypeStruct((count, 1), F32),
            jax.ShapeDtypeStruct((blocks * capacity, model), BF16),
            jax.ShapeDtypeStruct((blocks * capacity, model), BF16),
            jax.ShapeDtypeStruct((blocks * capacity, HEAD), F32),
        ],
        compiler_params=pltpu.CompilerParams(vmem_limit_bytes=VMEM_LIMIT),
        cost_estimate=pl.CostEstimate(
            flops=2 * (2 * count * model * (3 * held + 2 * capacity)),
            bytes_accessed=6 * count * model,
            transcendentals=2 * count * held,
        ),
        name="moe_in",
    )(*after, expert, *rows, *grads, w_in, w_dn, slot_rows)


def dot_nt(left, right):
    return lax.dot_general(left, right, (((1,), (1,)), ((), ())), preferred_element_type=F32)


def expert_kernel(
    steps, rows_ref, grad_ref, gate_ref, wgu_ref, wd_ref,
    back_ref, out_ref, dgu_ref, hid_ref, ggate_ref, acc_g, acc_u, acc_r,
):
    step = pl.program_id(0)

    @pl.when(step == 0)
    def _():
        acc_g[...] = dot_nt(rows_ref[...], wgu_ref[0])
        acc_u[...] = dot_nt(rows_ref[...], wgu_ref[1])
        acc_r[...] = dot_nt(grad_ref[...], wd_ref[...])

    @pl.when((step > 0) & (step < steps))
    def _():
        acc_g[...] += dot_nt(rows_ref[...], wgu_ref[0])
        acc_u[...] += dot_nt(rows_ref[...], wgu_ref[1])
        acc_r[...] += dot_nt(grad_ref[...], wd_ref[...])

    @pl.when(step == steps)
    def _():
        gate_in, up_in, raw, gates = acc_g[...], acc_u[...], acc_r[...], gate_ref[:, :1]
        sigma = 1.0 / (1.0 + jnp.exp(-gate_in))
        swished = gate_in * sigma
        hidden = swished * up_in
        ggate_ref[...] = jnp.sum(hidden * raw, axis=-1, keepdims=True)
        hid_ref[...] = (gates * hidden).astype(BF16)
        scaled = gates * raw
        dgu_ref[0] = (scaled * up_in * sigma * (1.0 + gate_in * (1.0 - sigma))).astype(BF16)
        dgu_ref[1] = (scaled * swished).astype(BF16)

    @pl.when(step >= steps)
    def _():
        back = jnp.dot(dgu_ref[0], wgu_ref[0], preferred_element_type=F32)
        back = back + jnp.dot(dgu_ref[1], wgu_ref[1], preferred_element_type=F32)
        back_ref[...] = back.astype(BF16)
        out_ref[...] = jnp.dot(hid_ref[...], wd_ref[...], preferred_element_type=F32).astype(BF16)


def run_expert(after, rows, grad, gates, w_gu, w_down):
    count, model = rows.shape
    cols = w_down.shape[0]
    steps = 4
    chunk = model // steps
    return pl.pallas_call(
        without(len(after), functools.partial(expert_kernel, steps)),
        grid=(2 * steps,),
        in_specs=[ANYWHERE] * len(after)
        + [
            pl.BlockSpec((count, chunk), lambda i: (0, jnp.minimum(i, steps - 1))),
            pl.BlockSpec((count, chunk), lambda i: (0, jnp.minimum(i, steps - 1))),
            pl.BlockSpec((count, HEAD), lambda i: (0, 0)),
            pl.BlockSpec((2, cols, chunk), lambda i: (0, 0, i % steps)),
            pl.BlockSpec((cols, chunk), lambda i: (0, i % steps)),
        ],
        out_specs=[
            pl.BlockSpec((count, chunk), lambda i: (0, jnp.maximum(i - steps, 0))),
            pl.BlockSpec((count, chunk), lambda i: (0, jnp.maximum(i - steps, 0))),
            pl.BlockSpec((2, count, cols), lambda i: (0, 0, 0)),
            pl.BlockSpec((count, cols), lambda i: (0, 0)),
            pl.BlockSpec((count, 1), lambda i: (0, 0)),
        ],
        out_shape=[
            jax.ShapeDtypeStruct((count, model), BF16),
            jax.ShapeDtypeStruct((count, model), BF16),
            jax.ShapeDtypeStruct((2, count, cols), BF16),
            jax.ShapeDtypeStruct((count, cols), BF16),
            jax.ShapeDtypeStruct((count, 1), F32),
        ],
        scratch_shapes=[pltpu.VMEM((count, cols), F32)] * 3,
        compiler_params=pltpu.CompilerParams(vmem_limit_bytes=VMEM_LIMIT),
        cost_estimate=pl.CostEstimate(
            flops=2 * (12 * count * model * cols),
            bytes_accessed=8 * count * model + 12 * model * cols,
            transcendentals=count * cols,
        ),
        name="run_expert",
    )(*after, rows, grad, gates, w_gu, w_down)


def sum_kernel(*refs):
    lefts, rights = refs[: len(refs) // 2 - 1], refs[len(refs) // 2 - 1 : -2]
    out_ref, acc_ref = refs[-2:]
    tile = pl.program_id(2)
    total = None
    for left, right in zip(lefts, rights):
        part = lax.dot_general(
            left[0], right[...], (((0,), (0,)), ((), ())), preferred_element_type=F32
        )
        total = part if total is None else total + part

    @pl.when(tile == 0)
    def _():
        acc_ref[...] = total

    @pl.when(tile > 0)
    def _():
        acc_ref[...] += total

    @pl.when(tile == pl.num_programs(2) - 1)
    def _():
        out_ref[0] = acc_ref[...].astype(out_ref.dtype)


def weight_sum(after, terms, tile, steps_of_tiles, dtype):
    parts, _, inner = terms[0][0].shape
    model = terms[0][2].shape[1]
    steps = 4
    width = model // steps

    def left_spec(first):
        return pl.BlockSpec((1, tile, inner), lambda j, d, t: (j, t + first, 0))

    def right_spec(stride, first):
        return pl.BlockSpec((tile, width), lambda j, d, t: (t * stride + first, d))

    return pl.pallas_call(
        without(len(after), sum_kernel),
        grid=(parts, steps, steps_of_tiles),
        in_specs=[ANYWHERE] * len(after)
        + [left_spec(term[1]) for term in terms]
        + [right_spec(*term[3:]) for term in terms],
        out_specs=pl.BlockSpec((1, inner, width), lambda j, d, t: (j, 0, d)),
        out_shape=jax.ShapeDtypeStruct((parts, inner, model), dtype),
        scratch_shapes=[pltpu.VMEM((inner, width), F32)],
        compiler_params=pltpu.CompilerParams(vmem_limit_bytes=VMEM_LIMIT),
        cost_estimate=pl.CostEstimate(
            flops=2 * (2 * len(terms) * parts * steps_of_tiles * tile * inner * model),
            bytes_accessed=len(terms) * 2 * steps_of_tiles * tile * (parts * inner + model)
            + 4 * parts * inner * model,
            transcendentals=0,
        ),
        name="weight_sum",
    )(*after, *[term[0] for term in terms], *[term[2] for term in terms])


def combine_kernel(capacity, taken, *refs):
    out_ref = refs[-1]

    def write(act_ref, weight_ref, slot_ref, rows_ref):
        place = jnp.where(one_hot(slot_ref[0], capacity), 1.0, 0.0).astype(BF16)
        routed = lax.dot_general(
            place, rows_ref[...], (((0,), (0,)), ((), ())), preferred_element_type=F32
        )
        own = jnp.dot(act_ref[...], weight_ref[...], preferred_element_type=F32)
        out_ref[...] = (own + routed).astype(BF16)

    for term in range(len(refs) // 4):
        pl.when(pl.program_id(0) // taken == term)(
            functools.partial(write, *refs[4 * term : 4 * term + 4])
        )


def combine(after, terms, core):
    blocks, _, step = terms[0][2].shape
    model = terms[0][1].shape[1]
    capacity = terms[0][3].shape[0] // blocks
    taken = blocks // 2
    specs, operands, flops = [], [], 0
    for term, (act, weight, slot_rows, rows) in enumerate(terms):
        inner = weight.shape[0]

        def block(i, term=term):
            return core * taken + jnp.clip(i - term * taken, 0, taken - 1)

        specs += [
            pl.BlockSpec((step, inner), lambda i, block=block: (block(i), 0)),
            pl.BlockSpec((inner, model), lambda i: (0, 0)),
            pl.BlockSpec((1, 1, step), lambda i, block=block: (block(i), 0, 0)),
            pl.BlockSpec((capacity, model), lambda i, block=block: (block(i), 0)),
        ]
        operands += [act, weight, slot_rows, rows]
        flops += 2 * taken * step * model * (inner + capacity)
    count = len(terms) * taken * step
    return pl.pallas_call(
        without(len(after), functools.partial(combine_kernel, capacity, taken)),
        grid=(len(terms) * taken,),
        in_specs=[ANYWHERE] * len(after) + specs,
        out_specs=pl.BlockSpec((step, model), lambda i: (i, 0)),
        out_shape=jax.ShapeDtypeStruct((count, model), BF16),
        compiler_params=pltpu.CompilerParams(vmem_limit_bytes=VMEM_LIMIT),
        cost_estimate=pl.CostEstimate(
            flops=3 * (flops),
            bytes_accessed=2 * count * model * (step + capacity) // step,
            transcendentals=0,
        ),
        name="combine",
    )(*after, *operands)


def finish_kernel(hidden_ref, attn_ref, valid_ref, first, second, third, fourth, out_ref, sum_ref):
    residual, attn, valid = hidden_ref[...].astype(F32), attn_ref[...], valid_ref[...]
    moe = first[...] + second[...].astype(F32) + third[...].astype(F32) + fourth[...].astype(F32)
    out_ref[...] = (residual + attn + moe).astype(BF16)
    for place, value in enumerate((residual, attn, moe)):
        sum_ref[0, place] = jnp.sum(valid * value * value)
    sum_ref[0, 3] = jnp.sum(valid)


def finish(after, hidden_in, attn_rows, valid_rows, moe_parts):
    return pl.pallas_call(
        without(len(after), finish_kernel),
        in_specs=[ANYWHERE] * len(after) + [pl.BlockSpec(memory_space=pltpu.VMEM)] * 7,
        out_specs=[pl.BlockSpec(memory_space=pltpu.VMEM), pl.BlockSpec(memory_space=pltpu.SMEM)],
        out_shape=[
            jax.ShapeDtypeStruct(hidden_in.shape, BF16),
            jax.ShapeDtypeStruct((1, 4), F32),
        ],
        compiler_params=pltpu.CompilerParams(vmem_limit_bytes=VMEM_LIMIT),
        name="finish",
    )(*after, hidden_in, attn_rows, valid_rows, *moe_parts)


def norm_scale(rows_in):
    return lax.rsqrt(jnp.mean(rows_in * rows_in, axis=-1, keepdims=True) + EPSILON)


def norm_back(rows_in, scaling, gain, grad):
    unit_rows = rows_in * scaling
    grad_unit = grad * gain
    return scaling * (
        grad_unit - unit_rows * jnp.mean(grad_unit * unit_rows, axis=-1, keepdims=True)
    )


def swish(gate_in):
    return gate_in * jax.nn.sigmoid(gate_in)


def swish_back(gate_in, up_in, grad):
    sigma = jax.nn.sigmoid(gate_in)
    grad_gate = grad * up_in * sigma * (1.0 + gate_in * (1.0 - sigma))
    return (grad_gate, grad * gate_in * sigma)


def rope_tables(first_row, row_count):
    placing = (first_row + jnp.arange(row_count, dtype=jnp.int32)) % SEQ
    frequency = ROPE_BASE ** (-(jnp.arange(HEAD // 2, dtype=F32) * 2.0 / HEAD))
    angles = placing.astype(F32)[:, None] * frequency[None, :]
    cosine, sine = jnp.cos(angles), jnp.sin(angles)
    return (
        jnp.concatenate([cosine, cosine], 1),
        jnp.concatenate([-sine, sine], 1),
    )


def per_device(
    hidden_in,
    cotangent,
    norm_gains,
    qkv_weight,
    qkv_bias,
    out_weight,
    router_weight,
    shared_gate_vec,
    shared_gate_up,
    shared_down,
    expert_gate_up,
    expert_down,
    segments,
    valid_mask,
    routes,
    slots,
):
    groups = lax.axis_size("g")
    blocks = segments.shape[0]
    rows_here, model = hidden_in.shape
    weight_rows, local_cols = qkv_weight.shape[1:]
    shared_cols = shared_gate_up.shape[2]
    experts, top = router_weight.shape[1], routes.shape[1]
    shares = groups * 4 * LINE
    cols = local_cols // 4
    own = shared_cols // shares
    held = -(-(own + experts + 1) // 128) * 128
    capacity = -(-(blocks * top * 4 // (3 * experts)) // 16) * 16
    plane_rows = 4 * blocks
    everywhere = ("g",) + GROUP
    g, z, y, c, x = (lax.axis_index(axis) for axis in EVERY)
    expert = ((g * LINE + z) * 2 + y) * 2 + c

    ahead = [(k, k + 1) for k in range(LINE - 1)]
    behind = [(k + 1, k) for k in range(LINE - 1)]

    residual = hidden_in.astype(F32)
    gain_attn, gain_moe = norm_gains[0], norm_gains[1]
    scale_attn = norm_scale(residual)
    own_attn = (residual * scale_attn * gain_attn).astype(BF16)
    numbers = jnp.concatenate([segments[None], valid_mask[None], routes.T, slots.T], 0)
    numbers = jnp.stack([numbers, swap(numbers, "y")])
    numbers = jnp.stack([numbers, swap(numbers, "c")])
    numbers_here = flip(flip(numbers[:, :, :2], c, 0), y, 1).transpose(2, 1, 0, 3)
    numbers_here = numbers_here.reshape(2, plane_rows)
    numbers_before = jnp.where(z == 0, -1, lax.ppermute(numbers_here, "z", ahead))

    before = lax.ppermute(own_attn, "z", ahead)
    def cut_heads(value):
        return value.reshape(weight_rows, -1, 4, cols).transpose(2, 0, 1, 3)

    qkv_cut = cut_heads(qkv_weight.transpose(1, 0, 2)).reshape(4, weight_rows, 3 * cols)
    out_cut = cut_heads(out_weight.T).reshape(4, weight_rows, cols)
    w_heads = exchange(jnp.concatenate([qkv_cut, out_cut], 2), ("y", "c"))
    w_heads = w_heads.reshape(4 * weight_rows, 4 * cols)
    qkv_rows = w_heads[:, : 3 * cols]
    qkv_across = cross(qkv_rows, 2)
    later = tick(w_heads)
    attn_pairs, attn_plane, _ = slot_pair(jnp.stack([before, own_attn]), (w_heads, numbers_before))
    rows_attn = attn_plane((qkv_across,))
    grad_late = hold(cotangent, tick(rows_attn[0]))
    grad_crossed = [cross(grad_late, offset) for offset in range(1, LINE)]
    w_qkv, qkv_others = gather_line(qkv_rows, qkv_across)
    if groups > 1:
        w_qkv = lax.all_gather(w_qkv, "g", axis=0, tiled=True)

    late_gu, late_dn = hold(shared_gate_up, later), hold(shared_down, later)
    shared_cut = jnp.concatenate(
        [
            late_gu[0].T.reshape(shares, own, weight_rows),
            late_gu[1].T.reshape(shares, own, weight_rows),
            late_dn.reshape(shares, own, weight_rows),
        ],
        1,
    )

    here = x * local_cols + (y * 2 + c) * cols
    bias = lax.dynamic_slice_in_dim(qkv_bias, here, cols, 1).astype(F32).reshape(1, 3 * cols)
    cosine, sine = rope_tables((z + LINE - 1) * plane_rows + later, 2 * plane_rows)
    order = jnp.stack([(y ^ j) * 2 + (c ^ i) for i in range(2) for j in range(2)])
    order = order.astype(jnp.int32)
    order_one = jnp.concatenate([x[None], order])
    order_two = jnp.concatenate([x[None], order[:2], order[:2] + 4, order[2:], order[2:] + 4])
    own_rows, projected = project((), order_two, rows_attn, w_qkv, bias, cosine, sine)
    w_out_rows = hold(w_heads[:, 3 * cols :], tick(qkv_others))
    w_out, _ = gather_line(w_out_rows, hold(cross(w_out_rows, 2), tick(projected)))
    if groups > 1:
        w_out = lax.all_gather(w_out, "g", axis=0, tiled=True)
    numbers = hold(numbers, tick(projected))
    numbers = jnp.stack([numbers] + [cross(numbers, offset) for offset in range(1, LINE)])
    numbers = numbers.reshape(LINE, 1, 4, 2 + 2 * top, blocks)
    if groups > 1:
        numbers = lax.all_gather(numbers, "g", axis=1, tiled=True)
    slot_here = jnp.max(
        jnp.where(numbers[:, :, :, 2 : 2 + top] == expert, numbers[:, :, :, 2 + top :], -1), 3
    )
    slot_here = slot_here.reshape(LINE * groups * 4, 2, 2, rows_here // 2)
    slot_here = flip(slot_here, x, 1).transpose(0, 2, 1, 3).reshape(2, 2, groups, 2, 2, blocks)
    near = jnp.concatenate([numbers_before, numbers_here], 1)
    seg_k, valid_k = near[:1], near[1:]
    seg_q = numbers_here[0].reshape(plane_rows, 1)
    attended = attend((grad_crossed[1],), projected, seg_q, seg_k, valid_k)
    w_out_t = w_out.T
    (send,) = spread((grad_crossed[0],), order_one, attended, w_out_t, 1)
    (keep,) = spread((send,), order_one, attended, w_out_t, 0)
    attn_rows = slot_scatter(
        keep, send, (slot_here.reshape(-1, blocks),), (), (grad_crossed[2],)
    )[0][0]
    middle = residual + attn_rows
    scale_moe = norm_scale(middle)
    own_moe = (middle * scale_moe * gain_moe).astype(BF16)
    grad_pairs, grad_plane, grad_arrived = slot_pair(
        hold(jnp.stack([cotangent, grad_crossed[0]]), tick(own_moe)), ()
    )
    crossed = [cross(own_moe, offset) for offset in range(1, LINE)]
    near_pairs, near_plane, _ = slot_pair(
        jnp.stack([own_moe, crossed[0]]), tuple(crossed[1:]) + grad_arrived
    )
    w_shared = exchange(hold(shared_cut, tick(near_pairs[0])), everywhere)
    near_rows = near_plane(())
    near_grads = grad_plane((near_pairs[0],))
    far_pairs, far_plane, _ = slot_pair(hold(jnp.stack(crossed[1:]), tick(near_rows[0])), ())
    def whole_slots(halves):
        halves = [half.reshape(-1, model) for half in halves]
        if groups > 1:
            halves = [lax.all_gather(half, "g", axis=0, tiled=True) for half in halves]
        return halves

    chunk_rows, chunk_grads = [whole_slots(near_rows)], [whole_slots(near_grads)]

    w_shared = w_shared.transpose(1, 0, 2).reshape(3 * own, model)

    def padded(*values):
        value = jnp.concatenate(values, 0)
        return jnp.pad(value, ((0, held - value.shape[0]), (0, 0)))

    shared_in = jnp.concatenate(
        [
            padded(w_shared[:own]),
            padded(w_shared[own : 2 * own], router_weight.T, shared_gate_vec[None]),
        ],
        0,
    )
    shared_dn = padded(w_shared[2 * own :])

    w_gu, w_down = expert_gate_up[0].transpose(0, 2, 1), expert_down[0]
    expert_id = expert.reshape(1).astype(jnp.int32)

    def slots_of(table):
        return table.transpose(3, 2, 0, 1, 4, 5).reshape(-1, 1, blocks)

    def core_part(after, terms, core):
        if groups == 1:
            part = combine(after, terms, core)
        else:
            parts = [combine(after, [term], core) for term in terms]
            parts = [lax.psum_scatter(v, "g", scatter_dimension=0, tiled=True) for v in parts]
            part = jnp.concatenate(parts, 0)
        return part.reshape(-1, plane_rows // 2, model)

    tables = [slots_of(slot_here[chunk : chunk + 1]) for chunk in range(2)]
    acts, hiddens, signals, inputs, grads, results = [], [], [], [], [], []
    gate_grads, backs = [], []

    def enter_chunk(chunk, after):
        act, hid, sig, erow, egrad, egate = moe_in(
            after, expert_id,
            chunk_rows[chunk], chunk_grads[chunk], shared_in, shared_dn, tables[chunk],
            experts, own, capacity,
        )
        signals.append(sig.reshape(-1, blocks))
        acts.append(act)
        hiddens.append(hid)
        return erow, egrad, egate

    def run_chunk(chunk, after, erow, egrad, egate):
        back, out, dgu, ehid, ggate = run_expert(after, erow, egrad, egate, w_gu, w_down)
        chosen = tables[chunk] == jnp.arange(capacity, dtype=jnp.int32)[None, :, None]
        ggate = ggate.reshape(-1, capacity, 1)
        gate_grads.append(jnp.sum(jnp.where(chosen, ggate, 0.0), axis=1))
        inputs.append((dgu, erow))
        grads.append((ehid, egrad))
        results.append(out)
        backs.append(back)

    def grad_term(chunk):
        return [(acts[chunk], shared_in, tables[chunk], backs[chunk])]

    def moe_term(chunk):
        return [(hiddens[chunk], shared_dn, tables[chunk], results[chunk])]

    grad_pairs, grad_plane, _ = slot_pair(
        hold(jnp.stack(grad_crossed[1:]), tick(near_rows[0])), (far_pairs[0],)
    )
    entered = enter_chunk(0, (far_pairs[0], grad_pairs[0]))
    far_rows = far_plane((acts[0],))
    chunk_rows.append(whole_slots(far_rows))
    run_chunk(0, (), *entered)
    far_grads = grad_plane((backs[0],))
    chunk_grads.append(whole_slots(far_grads))
    send = core_part((far_rows[0],), grad_term(0), 1)
    keep = core_part((send, far_grads[0]), grad_term(0), 0)
    near_steps = scatter_core(keep, send, ())
    run_chunk(1, (), *enter_chunk(1, (near_steps[0],)))
    near_steps = scatter_pair(near_steps, ())
    send = core_part((near_steps[0],), grad_term(1), 1)
    keep = core_part((send,), grad_term(1), 0)
    near_total = scatter_last(near_steps, ())
    near_cross = cross(near_total[1].astype(BF16), 1)

    far_steps = scatter_core(keep, send, (near_total,))
    moe_terms = moe_term(0) + moe_term(1)
    moe_send = core_part((far_steps[0],), moe_terms, 1)
    moe_keep = core_part((moe_send,), moe_terms, 0)
    signals = jnp.stack([jnp.stack(gate_grads), jnp.stack(signals)])
    signals = signals.reshape(2, 2, 2, groups, 2, 2, 2, 2, rows_here // 2)
    for dim, index in ((1, z // 2), (2, c), (4, z % 2), (5, y), (7, x)):
        signals = flip(signals, index, dim)
    signals = signals.transpose(3, 1, 4, 5, 2, 7, 0, 6, 8).reshape(2 * shares, 2, rows_here)
    far_steps = scatter_pair(far_steps, (moe_keep,))
    moe_steps = scatter_core(moe_keep, moe_send, (far_steps[0],))
    far_total = scatter_last(far_steps, (moe_steps[0],))
    far_cross = [cross(far_total[k].astype(BF16), 2 + k) for k in range(2)]
    moe_steps = scatter_pair(moe_steps, (far_total,))

    tiles = range(2)
    shared_time = (far_total,)
    grad_sgu = weight_sum(
        shared_time,
        [
            (acts[chunk][None], core * groups, chunk_rows[chunk][core], 1, 0)
            for chunk in tiles
            for core in tiles
        ],
        plane_rows,
        groups,
        BF16,
    )[0]
    grad_sdn = weight_sum(
        shared_time,
        [
            (hiddens[chunk][None], core * groups, chunk_grads[chunk][core], 1, 0)
            for chunk in tiles
            for core in tiles
        ],
        plane_rows,
        groups,
        BF16,
    )[0]
    grad_normed = near_total[0] + near_cross.astype(F32)
    grad_normed = grad_normed + far_cross[0].astype(F32) + far_cross[1].astype(F32)
    grad_normed = hold(grad_normed, tick(grad_sgu) + tick(grad_sdn) + tick(moe_steps[0]))
    shared_grad = jnp.concatenate(
        [grad_sgu[:own], grad_sgu[held : held + own], grad_sdn[:own]], 0
    )
    shared_grad = shared_grad.reshape(3 * own, shares, weight_rows).transpose(1, 0, 2)
    shared_grad = exchange(shared_grad, everywhere)
    shared_grad_sent = shared_grad
    shared_grad = shared_grad.reshape(shares, 3, own, weight_rows).transpose(1, 0, 2, 3)
    shared_grad = shared_grad.reshape(3, shared_cols, weight_rows).astype(F32)
    grad_sgu = shared_grad[:2].transpose(0, 2, 1)

    signals = exchange(hold(signals, tick(far_total)), EVERY)
    signals = signals.reshape(experts, 2, 2, rows_here)
    grad_router_probs = jnp.sum(signals[:, :, 0], axis=1).T
    gate_signal = jnp.sum(signals[:, :, 1], axis=(0, 1))

    own_logits = jnp.dot(own_moe, router_weight, preferred_element_type=F32)
    router_probs = jax.nn.softmax(own_logits, axis=-1)
    grad_logits = router_probs * (
        grad_router_probs - jnp.sum(router_probs * grad_router_probs, axis=-1, keepdims=True)
    )
    grad_normed = (
        grad_normed
        + gate_signal[:, None] * shared_gate_vec.astype(F32)[None, :]
        + jnp.einsum("te,de->td", grad_logits, router_weight.astype(F32))
    )
    own_float = own_moe.astype(F32)
    grad_router = jnp.einsum("td,te->ed", own_float, grad_logits)
    grad_gate_vec = jnp.sum(gate_signal[:, None] * own_float, axis=0)
    grad_gain_moe = jnp.sum(grad_normed * (middle * scale_moe), axis=0)
    grad_middle = cotangent.astype(F32) + norm_back(middle, scale_moe, gain_moe, grad_normed)
    grad_attn = grad_middle.astype(BF16)

    _, plane, _ = slot_pair(grad_attn[None], (moe_steps[1], moe_steps[3]))
    moe_parts = scatter_last(moe_steps, (grad_attn,))
    moe_cross = [cross(moe_parts[k].astype(BF16), k) for k in range(1, LINE)]
    plane_grad, grad_attended = project((), order_one, plane((moe_parts,)), w_out)

    def weight_grad(left, right):
        return lax.dot_general(left, right, (((0,), (0,)), ((), ())), preferred_element_type=F32)

    def to_weight_owners(value):
        if groups > 1:
            value = lax.psum_scatter(value, "g", scatter_dimension=0, tiled=True)
        value, mark = scatter_line(value)
        return exchange(value.reshape(4, weight_rows, -1), ("y", "c")).astype(F32), mark

    grad_out = weight_grad(plane_grad, attended).astype(BF16)
    grad_projected = attend_back(
        (grad_out, shared_grad_sent, moe_cross[0]),
        projected, grad_attended, seg_q, seg_k, valid_k, cosine, sine,
    )
    grad_qkv = weight_grad(own_rows, grad_projected).astype(BF16)
    grad_out, out_marks = to_weight_owners(grad_out)
    grad_out = grad_out.transpose(1, 0, 2).reshape(weight_rows, local_cols).T
    tile = inputs[0][1].shape[0]
    grad_egu = weight_sum(
        (grad_projected,), [(left, 0, right, 1, 0) for left, right in inputs], tile, 1, F32
    )
    grad_qkv, qkv_marks = to_weight_owners(grad_qkv)
    grad_edown = weight_sum(
        (grad_egu,), [(left[None], 0, right, 1, 0) for left, right in grads], tile, 1, F32
    )
    grad_qkv = grad_qkv.reshape(4, weight_rows, 3, cols).transpose(2, 1, 0, 3)
    grad_qkv = grad_qkv.reshape(3, weight_rows, local_cols)
    w_qkv_t = w_qkv.T
    send, sum_send = spread(
        (qkv_marks[0], out_marks[1], moe_cross[1]),
        order_two, grad_projected, w_qkv_t, 1, rows_attn[1],
    )
    keep, sum_keep = spread((send, moe_cross[2], grad_egu, qkv_marks[3]), order_two, grad_projected, w_qkv_t, 0, rows_attn[0])
    gain_sum = (sum_send + sum_keep)[0] / gain_attn
    bias_sum = jnp.sum(grad_projected.astype(F32), axis=0).reshape(3, cols)
    grad_bias = lax.dynamic_update_slice_in_dim(jnp.zeros((3, model), F32), bias_sum, here, 1)

    valid_rows = lax.dynamic_slice_in_dim(valid_mask, x * rows_here, rows_here, 0).astype(F32)
    output, squares = finish(
        (grad_projected,), hidden_in, attn_rows, valid_rows[:, None], [moe_parts[0]] + moe_cross
    )

    sums_of_all = all_sum(
        jnp.concatenate(
            [
                grad_router,
                grad_gate_vec[None],
                grad_gain_moe[None],
                hold(gain_sum[None], tick(grad_edown) + tick(grad_sgu)),
                grad_bias,
                jnp.pad(squares, ((0, 0), (0, model - 4))),
            ],
            0,
        )
    )
    back_both, _ = slot_scatter(
        keep, send, (), (qkv_marks[2], out_marks[2], grad_edown), ()
    )
    back_own = back_both[1] + lax.ppermute(back_both[0].astype(BF16), "z", behind).astype(F32)
    input_grad = grad_middle + norm_back(residual, scale_attn, gain_attn, back_own)
    others = sums_of_all[experts:]
    root_means = jnp.sqrt(others[6, :3] / (jnp.maximum(others[6, 3], 1.0) * model))
    return (
        output,
        input_grad,
        jnp.stack([others[2], others[1]]),
        grad_qkv,
        others[3:6],
        grad_out,
        sums_of_all[:experts].T,
        others[0],
        grad_sgu,
        shared_grad[2],
        grad_egu.transpose(0, 2, 1)[None],
        grad_edown,
        root_means[0],
        root_means[1],
        root_means[2],
    )


def solution(mesh):
    dp, mp = mesh.shape["dp"], mesh.shape["mp"]
    inner = Mesh(mesh.devices.reshape(dp // (4 * LINE), LINE, 2, 2, mp), EVERY)
    d = ("g",) + GROUP
    placed = (
        P(EVERY, None),
        P(EVERY, None),
        P(),
        P(None, d, "x"),
        P(),
        P("x", d),
        P(),
        P(),
        P(None, d, "x"),
        P("x", d),
        P(d, None, None, "x"),
        P(d, "x", None),
        P(d),
        P(d),
        P(d, None),
        P(d, None),
    )
    return jax.shard_map(
        per_device,
        mesh=inner,
        in_specs=placed,
        out_specs=(
            P(EVERY, None),
            P(EVERY, None),
            P(),
            P(None, d, "x"),
            P(),
            P("x", d),
            P(),
            P(),
            P(None, d, "x"),
            P("x", d),
            P(d, None, None, "x"),
            P(d, "x", None),
            P(),
            P(),
            P(),
        ),
        check_vma=False,
    )
```

```python
import functools

import jax
import jax.numpy as jnp
from jax import lax
from jax.experimental import pallas as pl
from jax.experimental.pallas import tpu as pltpu
from jax.sharding import Mesh
from jax.sharding import PartitionSpec as P

HEAD = 128
SEQ = 4096
WINDOW = 1024

EPSILON = 1e-06
ROPE_BASE = 1000000.0
MASKED = -1e30

LINE = 4
GROUP = ("z", "y", "c")
EVERY = ("g", "z", "y", "c", "x")
SWAP = [(0, 1), (1, 0)]
VMEM_LIMIT = 56 * 1024 * 1024

F32 = jnp.float32
BF16 = jnp.bfloat16


def swap(value, axis):
    return lax.ppermute(value, axis, SWAP)


def cross(value, offset):
    return lax.ppermute(value, "z", [(k, k ^ offset) for k in range(LINE)])


def take(value, index, dim):
    return lax.dynamic_index_in_dim(value, index, dim, keepdims=False)


def split(value, index, dim):
    return take(value, index, dim), take(value, 1 - index, dim)


ANYWHERE = pl.BlockSpec(memory_space=pl.ANY)


def without(count, kernel, first=0):
    def run(*refs):
        kernel(*refs[:first], *refs[first + count :])

    return run


def stage(kernel, after, inputs, outputs, name):
    count, _, width = inputs[0].shape
    parts = max(1, 4 // count)

    def spec(rows):
        return pl.BlockSpec((1, rows, width // parts), lambda i, j: (i, 0, j))

    return pl.pallas_call(
        without(len(after), kernel),
        grid=(count, parts),
        in_specs=[ANYWHERE] * len(after) + [spec(v.shape[1]) for v in inputs],
        out_specs=[spec(rows) for rows, _ in outputs],
        out_shape=[jax.ShapeDtypeStruct((count, rows, width), kind) for rows, kind in outputs],
        compiler_params=pltpu.CompilerParams(vmem_limit_bytes=VMEM_LIMIT),
        cost_estimate=pl.CostEstimate(
            flops=0, bytes_accessed=8 * count * width * sum(rows for rows, _ in outputs), transcendentals=0
        ),
        name=name,
    )(*after, *inputs)


def pair_kernel(first, first_x, second, second_y, out_first, out_second):
    half = first.shape[1]
    out_first[0, :half] = first[0]
    out_first[0, half:] = first_x[0]
    out_second[0, :half] = second[0]
    out_second[0, half:] = second_y[0]


def plane_kernel(first, first_y, second, second_x, out):
    rows = first.shape[1]
    half = rows // 2
    for y, source in enumerate((first, first_y)):
        out[0, 2 * y * rows : (2 * y + 1) * rows] = source[0]
    for x, source in enumerate((second, second_x)):
        for y in range(2):
            start = (2 * y + 1) * rows + x * half
            out[0, start : start + half] = source[0, y * half : (y + 1) * half]


def slot_pair(shards, after):
    rows = shards.shape[1]
    half = rows // 2
    first, second = shards[:, :half], shards[:, half:]
    pairs = stage(
        pair_kernel,
        after,
        [first, swap(first, "x"), second, swap(second, "y")],
        [(rows, BF16)] * 2,
        "pair",
    )
    arrived = swap(pairs[0], "y"), swap(pairs[1], "x")

    def plane(after):
        (own,) = stage(
            plane_kernel,
            after,
            [pairs[0], arrived[0], pairs[1], arrived[1]],
            [(4 * rows, BF16)],
            "plane",
        )
        return own, swap(own, "c")

    return pairs, plane, arrived


def slot_gather(shards, after_pair, after_plane):
    pairs, plane, _ = slot_pair(shards, after_pair)
    halves = plane(after_plane)
    return halves, (pairs[0], halves[0])


def core_sum_kernel(keep, arrived, first, first_send, second, second_send):
    rows = first.shape[1]
    half = rows // 2

    def total(start, count):
        here = slice(start, start + count)
        return keep[0, here].astype(F32) + arrived[0, here].astype(F32)

    first[0] = total(0, rows)
    first_send[0] = total(2 * rows, rows).astype(BF16)
    for y in range(2):
        start = (2 * y + 1) * rows
        second[0, y * half : (y + 1) * half] = total(start, half)
        second_send[0, y * half : (y + 1) * half] = total(start + half, half).astype(BF16)


def pair_sum_kernel(first, first_y, second, second_x, first_keep, first_send, second_keep, second_send):
    half = first_keep.shape[1]
    for value, arrived, keep, send in (
        (first, first_y, first_keep, first_send),
        (second, second_x, second_keep, second_send),
    ):
        keep[0] = value[0, :half] + arrived[0, :half].astype(F32)
        send[0] = (value[0, half:] + arrived[0, half:].astype(F32)).astype(BF16)


def last_sum_kernel(first, first_x, second, second_y, out):
    half = first.shape[1]
    out[0, :half] = first[0] + first_x[0].astype(F32)
    out[0, half:] = second[0] + second_y[0].astype(F32)


def scatter_core(keep, send, after):
    rows = keep.shape[1] // 4
    first, first_send, second, second_send = stage(
        core_sum_kernel,
        after,
        [keep, swap(send, "c")],
        [(rows, F32), (rows, BF16)] * 2,
        "core_sum",
    )
    return first, swap(first_send, "y"), second, swap(second_send, "x")


def scatter_pair(steps, after):
    half = steps[0].shape[1] // 2
    first, first_send, second, second_send = stage(
        pair_sum_kernel,
        after,
        list(steps),
        [(half, F32), (half, BF16)] * 2,
        "pair_sum",
    )
    return first, swap(first_send, "x"), second, swap(second_send, "y")


def scatter_last(steps, after):
    (whole,) = stage(
        last_sum_kernel, after, list(steps), [(2 * steps[0].shape[1], F32)], "last_sum"
    )
    return whole


def slot_scatter(keep, send, after_core, after_pair, after_last):
    core = scatter_core(keep, send, after_core)
    pair = scatter_pair(core, after_pair)
    return scatter_last(pair, after_last), (core[0], core[1], pair[0], pair[1])


def tick_kernel(marker_ref, out_ref):
    corner = marker_ref[...].astype(F32)
    out_ref[0, 0] = jnp.where(jnp.max(corner) <= 3.4e38, 0, 1).astype(jnp.int32)


def tick(marker):
    lead = marker.ndim - 2
    block = (1,) * lead + (min(16, marker.shape[-2]), min(HEAD, marker.shape[-1]))
    flag = pl.pallas_call(
        tick_kernel,
        grid=(1,),
        in_specs=[pl.BlockSpec(block, lambda i: (0,) * marker.ndim)],
        out_specs=pl.BlockSpec(memory_space=pltpu.SMEM),
        out_shape=jax.ShapeDtypeStruct((1, 1), jnp.int32),
        name="tick",
    )(marker)
    return flag[0, 0]


def hold(value, flag):
    return jnp.where(flag == 0, value, jnp.zeros_like(value))


def all_sum(value):
    for axis in ("c", "x", "y"):
        value = value + swap(value, axis)
    for offset in (1, 2):
        value = value + cross(value, offset)
    return lax.psum(value, "g") if lax.axis_size("g") > 1 else value


def flip(value, index, dim):
    return jnp.where(index == 0, value, jnp.flip(value, dim))


def gather_line(value, across):
    z = lax.axis_index("z")
    others = cross(jnp.stack([value, across]), 1)
    held = [[value, others[0]], [across, others[1]]]
    placed = []
    for high in range(2):
        for low in range(2):
            rows = [jnp.where(z % 2 == low, held[k][0], held[k][1]) for k in range(2)]
            placed.append(jnp.where(z // 2 == high, rows[0], rows[1]))
    return jnp.concatenate(placed, 0), others


def scatter_line(value):
    z = lax.axis_index("z")
    parts = value.reshape(2, 2, -1, value.shape[-1])
    keep, send = split(parts, z % 2, 1)
    marks = [send, cross(send, 1)]
    keep = keep.astype(F32) + marks[1].astype(F32)
    keep, send = split(keep, z // 2, 0)
    send = send.astype(BF16)
    marks += [cross(send, 2), send]
    return (keep + marks[2].astype(F32)).astype(BF16), marks


def exchange(value, axes):
    return lax.all_to_all(value, axes, split_axis=0, concat_axis=0, tiled=True)


def turn(value, cosine, sine):
    return value * cosine + pltpu.roll(value, HEAD // 2, 1) * sine


def turn_back(value, cosine, sine):
    return value * cosine - pltpu.roll(value, HEAD // 2, 1) * sine


def own_order(target_ref, source_ref, x):
    part = source_ref.shape[0] // 4
    for half in range(2):
        for offset in range(2):
            side = x if offset == 0 else 1 - x
            place = pl.multiple_of((side * 2 + half) * part, part)
            start = (half * 2 + offset) * part
            target_ref[pl.ds(place, part), :] = source_ref[start : start + part, :]


def offset_order(target_ref, source_ref, x):
    part = source_ref.shape[0] // 4
    for half in range(2):
        for offset in range(2):
            side = x if offset == 0 else 1 - x
            place = pl.multiple_of((side * 2 + half) * part, part)
            start = (half * 2 + offset) * part
            target_ref[start : start + part, :] = source_ref[pl.ds(place, part), :]


def place_block(own_ref, halves, half_steps, x):
    for half, source in enumerate(halves):

        @pl.when(pl.program_id(0) // half_steps == half)
        def _():
            own_order(own_ref, source, x)


def project_kernel(heads, half_steps, order_ref, rows_ref, other_ref, weight_ref, bias_ref, cos_ref, sin_ref, own_ref, out_ref):
    place_block(own_ref, (rows_ref, other_ref), half_steps, order_ref[0])
    projected = (
        jnp.dot(own_ref[...], weight_ref[...], preferred_element_type=F32) + bias_ref[...]
    )
    for part in range(3 * heads):
        block = projected[:, part * HEAD : (part + 1) * HEAD]
        if part < 2 * heads:
            block = turn(block, cos_ref[...], sin_ref[...])
        out_ref[:, part * HEAD : (part + 1) * HEAD] = block.astype(BF16)


def plain_kernel(half_steps, order_ref, rows_ref, other_ref, weight_ref, own_ref, out_ref):
    place_block(own_ref, (rows_ref, other_ref), half_steps, order_ref[0])
    out_ref[...] = jnp.dot(
        own_ref[...], weight_ref[...], preferred_element_type=F32
    ).astype(BF16)


def project(after, order, halves, weight, bias=None, cosine=None, sine=None):
    slots, half_rows, model = halves[0].shape
    halves = [half.reshape(slots * half_rows, model) for half in halves]
    count = 2 * slots * half_rows
    width = weight.shape[1]
    step = half_rows // 2
    steps = 2 * slots
    arrived = [
        pl.BlockSpec((step, model), lambda i, order: (jnp.minimum(i, steps - 1), 0)),
        pl.BlockSpec((step, model), lambda i, order: (jnp.maximum(i - steps, 0), 0)),
    ]
    whole = pl.BlockSpec((model, width), lambda i, order: (0, 0))

    def placed(columns):
        return pl.BlockSpec((step, columns), lambda i, order: (order[i + 1], 0))

    if bias is None:
        kernel, specs, extra = functools.partial(plain_kernel, steps), arrived + [whole], ()
    else:
        kernel = functools.partial(project_kernel, width // (3 * HEAD), steps)
        row = pl.BlockSpec((1, width), lambda i, order: (0, 0))
        specs = arrived + [whole, row, placed(HEAD), placed(HEAD)]
        extra = (bias, cosine, sine)
    return pl.pallas_call(
        without(len(after), kernel, 1),
        grid_spec=pltpu.PrefetchScalarGridSpec(
            num_scalar_prefetch=1,
            grid=(2 * steps,),
            in_specs=[ANYWHERE] * len(after) + specs,
            out_specs=[placed(model), placed(width)],
        ),
        out_shape=[
            jax.ShapeDtypeStruct((count, model), BF16),
            jax.ShapeDtypeStruct((count, width), BF16),
        ],
        compiler_params=pltpu.CompilerParams(vmem_limit_bytes=VMEM_LIMIT),
        cost_estimate=pl.CostEstimate(
            flops=3 * (2 * count * model * width),
            bytes_accessed=2 * (2 * count * model + model * width + count * width),
            transcendentals=0,
        ),
        name="project",
    )(order, *after, *halves, weight, *extra)


def spread_kernel(order_ref, act_ref, weight_ref, rows_ref, out_ref, sum_ref, held_ref):
    offset_order(held_ref, act_ref, order_ref[0])
    partial_rows = jnp.dot(held_ref[...], weight_ref[...], preferred_element_type=F32)
    out_ref[...] = partial_rows.astype(BF16)
    products = jnp.sum(partial_rows * rows_ref[...].astype(F32), axis=0, keepdims=True)

    @pl.when(pl.program_id(0) == 0)
    def _():
        sum_ref[...] = products

    @pl.when(pl.program_id(0) > 0)
    def _():
        sum_ref[...] += products


def spread_plain_kernel(order_ref, act_ref, weight_ref, out_ref, held_ref):
    offset_order(held_ref, act_ref, order_ref[0])
    out_ref[...] = jnp.dot(held_ref[...], weight_ref[...], preferred_element_type=F32).astype(BF16)


def spread(after, order, act, weight, core, rows=None):
    count, inner = act.shape
    model = weight.shape[1]
    slots = order.shape[0] // 4
    step = count // (4 * slots)

    first = core * 2 * slots + 1
    specs = [
        pl.BlockSpec((step, inner), lambda i, order: (order[first + i], 0)),
        pl.BlockSpec((inner, model), lambda i, order: (0, 0)),
    ]
    out_specs = [pl.BlockSpec((step, model), lambda i, order: (i, 0))]
    out_shape = [jax.ShapeDtypeStruct((count // 2, model), BF16)]
    operands = (order, *after, act, weight)
    if rows is not None:
        specs.append(pl.BlockSpec((step, model), lambda i, order: (i, 0)))
        out_specs.append(pl.BlockSpec((1, model), lambda i, order: (0, 0)))
        out_shape.append(jax.ShapeDtypeStruct((1, model), F32))
        operands = operands + (rows.reshape(count // 2, model),)
    results = pl.pallas_call(
        without(len(after), spread_plain_kernel if rows is None else spread_kernel, 1),
        grid_spec=pltpu.PrefetchScalarGridSpec(
            num_scalar_prefetch=1,
            grid=(2 * slots,),
            in_specs=[ANYWHERE] * len(after) + specs,
            out_specs=out_specs,
            scratch_shapes=[pltpu.VMEM((step, inner), BF16)],
        ),
        out_shape=out_shape,
        compiler_params=pltpu.CompilerParams(vmem_limit_bytes=VMEM_LIMIT),
        cost_estimate=pl.CostEstimate(
            flops=3 * (count * model * inner),
            bytes_accessed=2 * (count * model + model * inner),
            transcendentals=0,
        ),
        name="spread",
    )(*operands)
    return (results[0].reshape(slots, -1, model),) + tuple(results[1:])


def block_probs(query, keys, seg_q, seg_k, valid_k, first, reach):
    rows, span = query.shape[0], keys.shape[0]
    scores = lax.dot_general(query, keys, (((1,), (1,)), ((), ())), preferred_element_type=F32)
    scores = scores * (HEAD ** (-0.5))
    distance = (
        reach
        + lax.broadcasted_iota(jnp.int32, (rows, span), 0)
        - lax.broadcasted_iota(jnp.int32, (rows, span), 1)
    )
    allowed = (
        (distance >= 0)
        & (distance < WINDOW)
        & (seg_q == seg_k)
        & ((valid_k == 1) | (distance == 0))
    )
    scores = jnp.where(allowed, scores, MASKED)
    powers = jnp.exp(scores - jnp.max(scores, axis=-1, keepdims=True))
    return powers / jnp.sum(powers, axis=-1, keepdims=True)


def attend_kernel(step, reach, q_ref, k_ref, v_ref, segq_ref, segk_ref, valid_ref, out_ref):
    first = pl.multiple_of(pl.program_id(1) * step, step)
    span = pl.ds(first, step + reach)
    probs = block_probs(
        q_ref[...], k_ref[span, :], segq_ref[...], segk_ref[:, span], valid_ref[:, span], first, reach
    )
    out_ref[...] = jnp.dot(
        probs.astype(BF16), v_ref[span, :], preferred_element_type=F32
    ).astype(BF16)


def head_specs(count, step, heads):
    ahead = count // (2 * step)
    return [
        pl.BlockSpec((step, HEAD), lambda h, i: (i + ahead, h)),
        pl.BlockSpec((count, HEAD), lambda h, i: (0, heads + h)),
        pl.BlockSpec((count, HEAD), lambda h, i: (0, 2 * heads + h)),
    ]


def attend(after, projected, seg_q, seg_k, valid_k):
    held, width = projected.shape
    count, width = held // 2, width // 3
    step = count // 4
    heads = width // HEAD
    flops = 4 * count * (step + count) * width
    return pl.pallas_call(
        without(len(after), functools.partial(attend_kernel, step, count)),
        grid=(heads, 4),
        in_specs=[ANYWHERE] * len(after)
        + head_specs(held, step, heads)
        + [
            pl.BlockSpec((step, 1), lambda h, i: (i, 0)),
            pl.BlockSpec((1, held), lambda h, i: (0, 0)),
            pl.BlockSpec((1, held), lambda h, i: (0, 0)),
        ],
        out_specs=pl.BlockSpec((step, HEAD), lambda h, i: (i, h)),
        out_shape=jax.ShapeDtypeStruct((count, width), BF16),
        compiler_params=pltpu.CompilerParams(vmem_limit_bytes=VMEM_LIMIT),
        cost_estimate=pl.CostEstimate(
            flops=9 * (flops), bytes_accessed=8 * held * width, transcendentals=flops // (4 * HEAD)
        ),
        name="attend",
    )(*after, projected, projected, projected, seg_q, seg_k, valid_k)


def attend_back_kernel(
    step, reach, heads, q_ref, k_ref, v_ref, g_ref, segq_ref, segk_ref, valid_ref, cos_ref, sin_ref,
    out_ref, dk_ref, dv_ref,
):
    head, block = pl.program_id(0), pl.program_id(1)
    first = pl.multiple_of(block * step, step)
    span = pl.ds(first, step + reach)
    columns = [pl.ds(pl.multiple_of((part * heads + head) * HEAD, HEAD), HEAD) for part in range(3)]

    @pl.when(block == 0)
    def _():
        dk_ref[...] = jnp.zeros_like(dk_ref)
        dv_ref[...] = jnp.zeros_like(dv_ref)
        out_ref[0:reach, columns[0]] = jnp.zeros((reach, HEAD), BF16)

    query, keys, grad = q_ref[...], k_ref[span, :], g_ref[...]
    probs = block_probs(
        query, keys, segq_ref[...], segk_ref[:, span], valid_ref[:, span], first, reach
    )
    g_probs = lax.dot_general(
        grad, v_ref[span, :], (((1,), (1,)), ((), ())), preferred_element_type=F32
    )
    inner = jnp.sum(probs * g_probs, axis=-1, keepdims=True)
    g_scores = (probs * (g_probs - inner)).astype(BF16)
    scale = HEAD ** (-0.5)
    dq = jnp.dot(g_scores, keys, preferred_element_type=F32) * scale
    here = pl.ds(pl.multiple_of(first + reach, step), step)
    out_ref[here, columns[0]] = turn_back(dq, cos_ref[here, :], sin_ref[here, :]).astype(BF16)
    dk_ref[span, :] += (
        lax.dot_general(g_scores, query, (((0,), (0,)), ((), ())), preferred_element_type=F32)
        * scale
    )
    dv_ref[span, :] += lax.dot_general(
        probs.astype(BF16), grad, (((0,), (0,)), ((), ())), preferred_element_type=F32
    )

    @pl.when(block == pl.num_programs(1) - 1)
    def _():
        out_ref[:, columns[1]] = turn_back(dk_ref[...], cos_ref[...], sin_ref[...]).astype(BF16)
        out_ref[:, columns[2]] = dv_ref[...].astype(BF16)


def attend_back(after, projected, grad, seg_q, seg_k, valid_k, cosine, sine):
    held, width = projected.shape
    count, width = held // 2, width // 3
    step = count // 4
    heads = width // HEAD
    flops = 10 * count * (step + count) * width
    return pl.pallas_call(
        without(len(after), functools.partial(attend_back_kernel, step, count, heads)),
        grid=(heads, 4),
        in_specs=[ANYWHERE] * len(after)
        + head_specs(held, step, heads)
        + [
            pl.BlockSpec((step, HEAD), lambda h, i: (i, h)),
            pl.BlockSpec((step, 1), lambda h, i: (i, 0)),
            pl.BlockSpec((1, held), lambda h, i: (0, 0)),
            pl.BlockSpec((1, held), lambda h, i: (0, 0)),
            pl.BlockSpec((held, HEAD), lambda h, i: (0, 0)),
            pl.BlockSpec((held, HEAD), lambda h, i: (0, 0)),
        ],
        out_specs=pl.BlockSpec((held, 3 * width), lambda h, i: (0, 0)),
        out_shape=jax.ShapeDtypeStruct((held, 3 * width), BF16),
        scratch_shapes=[pltpu.VMEM((held, HEAD), F32)] * 2,
        compiler_params=pltpu.CompilerParams(vmem_limit_bytes=VMEM_LIMIT),
        cost_estimate=pl.CostEstimate(
            flops=6 * (flops), bytes_accessed=12 * held * width, transcendentals=flops // (10 * HEAD)
        ),
        name="attend_back",
    )(*after, projected, projected, projected, grad, seg_q, seg_k, valid_k, cosine, sine)


def one_hot(slot_row, capacity):
    rows = lax.broadcasted_iota(jnp.int32, (capacity, slot_row.shape[1]), 0)
    return slot_row == rows


def moe_in_kernel(
    shape, expert_ref, rows_ref, other_rows_ref, grad_ref, other_grad_ref, win_ref, wdn_ref, slot_ref,
    act_ref, hid_ref, sig_ref, erow_ref, egrad_ref, egate_ref,
):
    experts, own, held, capacity = shape
    here = pl.program_id(0) < pl.num_programs(0) // 2
    rows = jnp.where(here, rows_ref[...], other_rows_ref[...])
    grad = jnp.where(here, grad_ref[...], other_grad_ref[...])
    inputs = dot_nt(rows, win_ref[...])
    gate_in, up_in = inputs[:, :held], inputs[:, held:]
    raw = dot_nt(grad, wdn_ref[...])
    column = lax.broadcasted_iota(jnp.int32, (1, held), 1)
    is_router = (column >= own) & (column < own + experts)
    logits = jnp.where(is_router, up_in, MASKED)
    powers = jnp.exp(logits - jnp.max(logits, axis=-1, keepdims=True))
    picked = jnp.where(column == own + expert_ref[0], powers, 0.0)
    gate = jnp.sum(picked, axis=-1, keepdims=True) / jnp.sum(powers, axis=-1, keepdims=True)
    shared_in = jnp.sum(jnp.where(column == own + experts, up_in, 0.0), axis=-1, keepdims=True)
    shared_gate = 1.0 / (1.0 + jnp.exp(-shared_in))
    sigma = 1.0 / (1.0 + jnp.exp(-gate_in))
    swished = gate_in * sigma
    hidden = swished * up_in
    grad_hidden = shared_gate * raw
    act_ref[:, :held] = (grad_hidden * up_in * sigma * (1.0 + gate_in * (1.0 - sigma))).astype(BF16)
    act_ref[:, held:] = (grad_hidden * swished).astype(BF16)
    hid_ref[...] = (shared_gate * hidden).astype(BF16)
    sig_ref[...] = jnp.sum(hidden * grad_hidden, axis=-1, keepdims=True) * (1.0 - shared_gate)
    place = jnp.where(one_hot(slot_ref[0], capacity), 1.0, 0.0)
    place_low = place.astype(BF16)
    erow_ref[...] = jnp.dot(place_low, rows, preferred_element_type=F32).astype(BF16)
    egrad_ref[...] = jnp.dot(place_low, grad, preferred_element_type=F32).astype(BF16)
    egate_ref[...] = jnp.dot(
        place,
        jnp.broadcast_to(gate, (gate.shape[0], HEAD)),
        precision=lax.Precision.HIGHEST,
        preferred_element_type=F32,
    )


def moe_in(after, expert, rows, grads, w_in, w_dn, slot_rows, experts, own, capacity):
    blocks, _, step = slot_rows.shape
    model = rows[0].shape[1]
    held = w_dn.shape[0]
    count = blocks * step
    half = blocks // 2

    def row_spec(core):
        def block(i):
            return jnp.maximum(i - half, 0) if core else jnp.minimum(i, half - 1)

        return pl.BlockSpec((step, model), lambda i: (block(i), 0))

    return pl.pallas_call(
        without(len(after), functools.partial(moe_in_kernel, (experts, own, held, capacity))),
        grid=(blocks,),
        in_specs=[ANYWHERE] * len(after)
        + [
            pl.BlockSpec(memory_space=pltpu.SMEM),
            row_spec(0),
            row_spec(1),
            row_spec(0),
            row_spec(1),
            pl.BlockSpec((2 * held, model), lambda i: (0, 0)),
            pl.BlockSpec((held, model), lambda i: (0, 0)),
            pl.BlockSpec((1, 1, step), lambda i: (i, 0, 0)),
        ],
        out_specs=[
            pl.BlockSpec((step, 2 * held), lambda i: (i, 0)),
            pl.BlockSpec((step, held), lambda i: (i, 0)),
            pl.BlockSpec((step, 1), lambda i: (i, 0)),
            pl.BlockSpec((capacity, model), lambda i: (i, 0)),
            pl.BlockSpec((capacity, model), lambda i: (i, 0)),
            pl.BlockSpec((capacity, HEAD), lambda i: (i, 0)),
        ],
        out_shape=[
            jax.ShapeDtypeStruct((count, 2 * held), BF16),
            jax.ShapeDtypeStruct((count, held), BF16),
            jax.ShapeDtypeStruct((count, 1), F32),
            jax.ShapeDtypeStruct((blocks * capacity, model), BF16),
            jax.ShapeDtypeStruct((blocks * capacity, model), BF16),
            jax.ShapeDtypeStruct((blocks * capacity, HEAD), F32),
        ],
        compiler_params=pltpu.CompilerParams(vmem_limit_bytes=VMEM_LIMIT),
        cost_estimate=pl.CostEstimate(
            flops=2 * (2 * count * model * (3 * held + 2 * capacity)),
            bytes_accessed=6 * count * model,
            transcendentals=2 * count * held,
        ),
        name="moe_in",
    )(*after, expert, *rows, *grads, w_in, w_dn, slot_rows)


def dot_nt(left, right):
    return lax.dot_general(left, right, (((1,), (1,)), ((), ())), preferred_element_type=F32)


def expert_kernel(
    steps, rows_ref, grad_ref, gate_ref, wgu_ref, wd_ref,
    back_ref, out_ref, dgu_ref, hid_ref, ggate_ref, acc_g, acc_u, acc_r,
):
    step = pl.program_id(0)

    @pl.when(step == 0)
    def _():
        acc_g[...] = dot_nt(rows_ref[...], wgu_ref[0])
        acc_u[...] = dot_nt(rows_ref[...], wgu_ref[1])
        acc_r[...] = dot_nt(grad_ref[...], wd_ref[...])

    @pl.when((step > 0) & (step < steps))
    def _():
        acc_g[...] += dot_nt(rows_ref[...], wgu_ref[0])
        acc_u[...] += dot_nt(rows_ref[...], wgu_ref[1])
        acc_r[...] += dot_nt(grad_ref[...], wd_ref[...])

    @pl.when(step == steps)
    def _():
        gate_in, up_in, raw, gates = acc_g[...], acc_u[...], acc_r[...], gate_ref[:, :1]
        sigma = 1.0 / (1.0 + jnp.exp(-gate_in))
        swished = gate_in * sigma
        hidden = swished * up_in
        ggate_ref[...] = jnp.sum(hidden * raw, axis=-1, keepdims=True)
        hid_ref[...] = (gates * hidden).astype(BF16)
        scaled = gates * raw
        dgu_ref[0] = (scaled * up_in * sigma * (1.0 + gate_in * (1.0 - sigma))).astype(BF16)
        dgu_ref[1] = (scaled * swished).astype(BF16)

    @pl.when(step >= steps)
    def _():
        back = jnp.dot(dgu_ref[0], wgu_ref[0], preferred_element_type=F32)
        back = back + jnp.dot(dgu_ref[1], wgu_ref[1], preferred_element_type=F32)
        back_ref[...] = back.astype(BF16)
        out_ref[...] = jnp.dot(hid_ref[...], wd_ref[...], preferred_element_type=F32).astype(BF16)


def run_expert(after, rows, grad, gates, w_gu, w_down):
    count, model = rows.shape
    cols = w_down.shape[0]
    steps = 4
    chunk = model // steps
    return pl.pallas_call(
        without(len(after), functools.partial(expert_kernel, steps)),
        grid=(2 * steps,),
        in_specs=[ANYWHERE] * len(after)
        + [
            pl.BlockSpec((count, chunk), lambda i: (0, jnp.minimum(i, steps - 1))),
            pl.BlockSpec((count, chunk), lambda i: (0, jnp.minimum(i, steps - 1))),
            pl.BlockSpec((count, HEAD), lambda i: (0, 0)),
            pl.BlockSpec((2, cols, chunk), lambda i: (0, 0, i % steps)),
            pl.BlockSpec((cols, chunk), lambda i: (0, i % steps)),
        ],
        out_specs=[
            pl.BlockSpec((count, chunk), lambda i: (0, jnp.maximum(i - steps, 0))),
            pl.BlockSpec((count, chunk), lambda i: (0, jnp.maximum(i - steps, 0))),
            pl.BlockSpec((2, count, cols), lambda i: (0, 0, 0)),
            pl.BlockSpec((count, cols), lambda i: (0, 0)),
            pl.BlockSpec((count, 1), lambda i: (0, 0)),
        ],
        out_shape=[
            jax.ShapeDtypeStruct((count, model), BF16),
            jax.ShapeDtypeStruct((count, model), BF16),
            jax.ShapeDtypeStruct((2, count, cols), BF16),
            jax.ShapeDtypeStruct((count, cols), BF16),
            jax.ShapeDtypeStruct((count, 1), F32),
        ],
        scratch_shapes=[pltpu.VMEM((count, cols), F32)] * 3,
        compiler_params=pltpu.CompilerParams(vmem_limit_bytes=VMEM_LIMIT),
        cost_estimate=pl.CostEstimate(
            flops=2 * (12 * count * model * cols),
            bytes_accessed=8 * count * model + 12 * model * cols,
            transcendentals=count * cols,
        ),
        name="run_expert",
    )(*after, rows, grad, gates, w_gu, w_down)


def sum_kernel(*refs):
    lefts, rights = refs[: len(refs) // 2 - 1], refs[len(refs) // 2 - 1 : -2]
    out_ref, acc_ref = refs[-2:]
    tile = pl.program_id(2)
    total = None
    for left, right in zip(lefts, rights):
        part = lax.dot_general(
            left[0], right[...], (((0,), (0,)), ((), ())), preferred_element_type=F32
        )
        total = part if total is None else total + part

    @pl.when(tile == 0)
    def _():
        acc_ref[...] = total

    @pl.when(tile > 0)
    def _():
        acc_ref[...] += total

    @pl.when(tile == pl.num_programs(2) - 1)
    def _():
        out_ref[0] = acc_ref[...].astype(out_ref.dtype)


def weight_sum(after, terms, tile, steps_of_tiles, dtype):
    parts, _, inner = terms[0][0].shape
    model = terms[0][2].shape[1]
    steps = 4
    width = model // steps

    def left_spec(first):
        return pl.BlockSpec((1, tile, inner), lambda j, d, t: (j, t + first, 0))

    def right_spec(stride, first):
        return pl.BlockSpec((tile, width), lambda j, d, t: (t * stride + first, d))

    return pl.pallas_call(
        without(len(after), sum_kernel),
        grid=(parts, steps, steps_of_tiles),
        in_specs=[ANYWHERE] * len(after)
        + [left_spec(term[1]) for term in terms]
        + [right_spec(*term[3:]) for term in terms],
        out_specs=pl.BlockSpec((1, inner, width), lambda j, d, t: (j, 0, d)),
        out_shape=jax.ShapeDtypeStruct((parts, inner, model), dtype),
        scratch_shapes=[pltpu.VMEM((inner, width), F32)],
        compiler_params=pltpu.CompilerParams(vmem_limit_bytes=VMEM_LIMIT),
        cost_estimate=pl.CostEstimate(
            flops=2 * (2 * len(terms) * parts * steps_of_tiles * tile * inner * model),
            bytes_accessed=len(terms) * 2 * steps_of_tiles * tile * (parts * inner + model)
            + 4 * parts * inner * model,
            transcendentals=0,
        ),
        name="weight_sum",
    )(*after, *[term[0] for term in terms], *[term[2] for term in terms])


def combine_kernel(capacity, taken, *refs):
    out_ref = refs[-1]

    def write(act_ref, weight_ref, slot_ref, rows_ref):
        place = jnp.where(one_hot(slot_ref[0], capacity), 1.0, 0.0).astype(BF16)
        routed = lax.dot_general(
            place, rows_ref[...], (((0,), (0,)), ((), ())), preferred_element_type=F32
        )
        own = jnp.dot(act_ref[...], weight_ref[...], preferred_element_type=F32)
        out_ref[...] = (own + routed).astype(BF16)

    for term in range(len(refs) // 4):
        pl.when(pl.program_id(0) // taken == term)(
            functools.partial(write, *refs[4 * term : 4 * term + 4])
        )


def combine(after, terms, core):
    blocks, _, step = terms[0][2].shape
    model = terms[0][1].shape[1]
    capacity = terms[0][3].shape[0] // blocks
    taken = blocks // 2
    specs, operands, flops = [], [], 0
    for term, (act, weight, slot_rows, rows) in enumerate(terms):
        inner = weight.shape[0]

        def block(i, term=term):
            return core * taken + jnp.clip(i - term * taken, 0, taken - 1)

        specs += [
            pl.BlockSpec((step, inner), lambda i, block=block: (block(i), 0)),
            pl.BlockSpec((inner, model), lambda i: (0, 0)),
            pl.BlockSpec((1, 1, step), lambda i, block=block: (block(i), 0, 0)),
            pl.BlockSpec((capacity, model), lambda i, block=block: (block(i), 0)),
        ]
        operands += [act, weight, slot_rows, rows]
        flops += 2 * taken * step * model * (inner + capacity)
    count = len(terms) * taken * step
    return pl.pallas_call(
        without(len(after), functools.partial(combine_kernel, capacity, taken)),
        grid=(len(terms) * taken,),
        in_specs=[ANYWHERE] * len(after) + specs,
        out_specs=pl.BlockSpec((step, model), lambda i: (i, 0)),
        out_shape=jax.ShapeDtypeStruct((count, model), BF16),
        compiler_params=pltpu.CompilerParams(vmem_limit_bytes=VMEM_LIMIT),
        cost_estimate=pl.CostEstimate(
            flops=3 * (flops),
            bytes_accessed=2 * count * model * (step + capacity) // step,
            transcendentals=0,
        ),
        name="combine",
    )(*after, *operands)


def finish_kernel(hidden_ref, attn_ref, valid_ref, first, second, third, fourth, out_ref, sum_ref):
    residual, attn, valid = hidden_ref[...].astype(F32), attn_ref[...], valid_ref[...]
    moe = first[...] + second[...].astype(F32) + third[...].astype(F32) + fourth[...].astype(F32)
    out_ref[...] = (residual + attn + moe).astype(BF16)
    for place, value in enumerate((residual, attn, moe)):
        sum_ref[0, place] = jnp.sum(valid * value * value)
    sum_ref[0, 3] = jnp.sum(valid)


def finish(after, hidden_in, attn_rows, valid_rows, moe_parts):
    return pl.pallas_call(
        without(len(after), finish_kernel),
        in_specs=[ANYWHERE] * len(after) + [pl.BlockSpec(memory_space=pltpu.VMEM)] * 7,
        out_specs=[pl.BlockSpec(memory_space=pltpu.VMEM), pl.BlockSpec(memory_space=pltpu.SMEM)],
        out_shape=[
            jax.ShapeDtypeStruct(hidden_in.shape, BF16),
            jax.ShapeDtypeStruct((1, 4), F32),
        ],
        compiler_params=pltpu.CompilerParams(vmem_limit_bytes=VMEM_LIMIT),
        name="finish",
    )(*after, hidden_in, attn_rows, valid_rows, *moe_parts)


def norm_scale(rows_in):
    return lax.rsqrt(jnp.mean(rows_in * rows_in, axis=-1, keepdims=True) + EPSILON)


def norm_back(rows_in, scaling, gain, grad):
    unit_rows = rows_in * scaling
    grad_unit = grad * gain
    return scaling * (
        grad_unit - unit_rows * jnp.mean(grad_unit * unit_rows, axis=-1, keepdims=True)
    )


def swish(gate_in):
    return gate_in * jax.nn.sigmoid(gate_in)


def swish_back(gate_in, up_in, grad):
    sigma = jax.nn.sigmoid(gate_in)
    grad_gate = grad * up_in * sigma * (1.0 + gate_in * (1.0 - sigma))
    return (grad_gate, grad * gate_in * sigma)


def rope_tables(first_row, row_count):
    placing = (first_row + jnp.arange(row_count, dtype=jnp.int32)) % SEQ
    frequency = ROPE_BASE ** (-(jnp.arange(HEAD // 2, dtype=F32) * 2.0 / HEAD))
    angles = placing.astype(F32)[:, None] * frequency[None, :]
    cosine, sine = jnp.cos(angles), jnp.sin(angles)
    return (
        jnp.concatenate([cosine, cosine], 1),
        jnp.concatenate([-sine, sine], 1),
    )


def per_device(
    hidden_in,
    cotangent,
    norm_gains,
    qkv_weight,
    qkv_bias,
    out_weight,
    router_weight,
    shared_gate_vec,
    shared_gate_up,
    shared_down,
    expert_gate_up,
    expert_down,
    segments,
    valid_mask,
    routes,
    slots,
):
    groups = lax.axis_size("g")
    blocks = segments.shape[0]
    rows_here, model = hidden_in.shape
    weight_rows, local_cols = qkv_weight.shape[1:]
    shared_cols = shared_gate_up.shape[2]
    experts, top = router_weight.shape[1], routes.shape[1]
    shares = groups * 4 * LINE
    cols = local_cols // 4
    own = shared_cols // shares
    held = -(-(own + experts + 1) // 128) * 128
    capacity = -(-(blocks * top * 4 // (3 * experts)) // 16) * 16
    plane_rows = 4 * blocks
    everywhere = ("g",) + GROUP
    g, z, y, c, x = (lax.axis_index(axis) for axis in EVERY)
    expert = ((g * LINE + z) * 2 + y) * 2 + c

    ahead = [(k, k + 1) for k in range(LINE - 1)]
    behind = [(k + 1, k) for k in range(LINE - 1)]

    residual = hidden_in.astype(F32)
    gain_attn, gain_moe = norm_gains[0], norm_gains[1]
    scale_attn = norm_scale(residual)
    own_attn = (residual * scale_attn * gain_attn).astype(BF16)
    numbers = jnp.concatenate([segments[None], valid_mask[None], routes.T, slots.T], 0)
    numbers = jnp.stack([numbers, swap(numbers, "y")])
    numbers = jnp.stack([numbers, swap(numbers, "c")])
    numbers_here = flip(flip(numbers[:, :, :2], c, 0), y, 1).transpose(2, 1, 0, 3)
    numbers_here = numbers_here.reshape(2, plane_rows)
    numbers_before = jnp.where(z == 0, -1, lax.ppermute(numbers_here, "z", ahead))

    before = lax.ppermute(own_attn, "z", ahead)
    def cut_heads(value):
        return value.reshape(weight_rows, -1, 4, cols).transpose(2, 0, 1, 3)

    qkv_cut = cut_heads(qkv_weight.transpose(1, 0, 2)).reshape(4, weight_rows, 3 * cols)
    out_cut = cut_heads(out_weight.T).reshape(4, weight_rows, cols)
    w_heads = exchange(jnp.concatenate([qkv_cut, out_cut], 2), ("y", "c"))
    w_heads = w_heads.reshape(4 * weight_rows, 4 * cols)
    qkv_rows = w_heads[:, : 3 * cols]
    qkv_across = cross(qkv_rows, 2)
    later = tick(w_heads)
    attn_pairs, attn_plane, _ = slot_pair(jnp.stack([before, own_attn]), (w_heads, numbers_before))
    rows_attn = attn_plane((qkv_across,))
    grad_late = hold(cotangent, tick(rows_attn[0]))
    grad_crossed = [cross(grad_late, offset) for offset in range(1, LINE)]
    w_qkv, qkv_others = gather_line(qkv_rows, qkv_across)
    if groups > 1:
        w_qkv = lax.all_gather(w_qkv, "g", axis=0, tiled=True)

    late_gu, late_dn = hold(shared_gate_up, later), hold(shared_down, later)
    shared_cut = jnp.concatenate(
        [
            late_gu[0].T.reshape(shares, own, weight_rows),
            late_gu[1].T.reshape(shares, own, weight_rows),
            late_dn.reshape(shares, own, weight_rows),
        ],
        1,
    )

    here = x * local_cols + (y * 2 + c) * cols
    bias = lax.dynamic_slice_in_dim(qkv_bias, here, cols, 1).astype(F32).reshape(1, 3 * cols)
    cosine, sine = rope_tables((z + LINE - 1) * plane_rows + later, 2 * plane_rows)
    order = jnp.stack([(y ^ j) * 2 + (c ^ i) for i in range(2) for j in range(2)])
    order = order.astype(jnp.int32)
    order_one = jnp.concatenate([x[None], order])
    order_two = jnp.concatenate([x[None], order[:2], order[:2] + 4, order[2:], order[2:] + 4])
    own_rows, projected = project((), order_two, rows_attn, w_qkv, bias, cosine, sine)
    w_out_rows = hold(w_heads[:, 3 * cols :], tick(qkv_others))
    w_out, _ = gather_line(w_out_rows, hold(cross(w_out_rows, 2), tick(projected)))
    if groups > 1:
        w_out = lax.all_gather(w_out, "g", axis=0, tiled=True)
    numbers = hold(numbers, tick(projected))
    numbers = jnp.stack([numbers] + [cross(numbers, offset) for offset in range(1, LINE)])
    numbers = numbers.reshape(LINE, 1, 4, 2 + 2 * top, blocks)
    if groups > 1:
        numbers = lax.all_gather(numbers, "g", axis=1, tiled=True)
    slot_here = jnp.max(
        jnp.where(numbers[:, :, :, 2 : 2 + top] == expert, numbers[:, :, :, 2 + top :], -1), 3
    )
    slot_here = slot_here.reshape(LINE * groups * 4, 2, 2, rows_here // 2)
    slot_here = flip(slot_here, x, 1).transpose(0, 2, 1, 3).reshape(2, 2, groups, 2, 2, blocks)
    near = jnp.concatenate([numbers_before, numbers_here], 1)
    seg_k, valid_k = near[:1], near[1:]
    seg_q = numbers_here[0].reshape(plane_rows, 1)
    attended = attend((grad_crossed[1],), projected, seg_q, seg_k, valid_k)
    w_out_t = w_out.T
    (send,) = spread((grad_crossed[0],), order_one, attended, w_out_t, 1)
    (keep,) = spread((send,), order_one, attended, w_out_t, 0)
    attn_rows = slot_scatter(
        keep, send, (slot_here.reshape(-1, blocks),), (), (grad_crossed[2],)
    )[0][0]
    middle = residual + attn_rows
    scale_moe = norm_scale(middle)
    own_moe = (middle * scale_moe * gain_moe).astype(BF16)
    grad_pairs, grad_plane, grad_arrived = slot_pair(
        hold(jnp.stack([cotangent, grad_crossed[0]]), tick(own_moe)), ()
    )
    crossed = [cross(own_moe, offset) for offset in range(1, LINE)]
    near_pairs, near_plane, _ = slot_pair(
        jnp.stack([own_moe, crossed[0]]), tuple(crossed[1:]) + grad_arrived
    )
    w_shared = exchange(hold(shared_cut, tick(near_pairs[0])), everywhere)
    near_rows = near_plane(())
    near_grads = grad_plane((near_pairs[0],))
    far_pairs, far_plane, _ = slot_pair(hold(jnp.stack(crossed[1:]), tick(near_rows[0])), ())
    def whole_slots(halves):
        halves = [half.reshape(-1, model) for half in halves]
        if groups > 1:
            halves = [lax.all_gather(half, "g", axis=0, tiled=True) for half in halves]
        return halves

    chunk_rows, chunk_grads = [whole_slots(near_rows)], [whole_slots(near_grads)]

    w_shared = w_shared.transpose(1, 0, 2).reshape(3 * own, model)

    def padded(*values):
        value = jnp.concatenate(values, 0)
        return jnp.pad(value, ((0, held - value.shape[0]), (0, 0)))

    shared_in = jnp.concatenate(
        [
            padded(w_shared[:own]),
            padded(w_shared[own : 2 * own], router_weight.T, shared_gate_vec[None]),
        ],
        0,
    )
    shared_dn = padded(w_shared[2 * own :])

    w_gu, w_down = expert_gate_up[0].transpose(0, 2, 1), expert_down[0]
    expert_id = expert.reshape(1).astype(jnp.int32)

    def slots_of(table):
        return table.transpose(3, 2, 0, 1, 4, 5).reshape(-1, 1, blocks)

    def core_part(after, terms, core):
        if groups == 1:
            part = combine(after, terms, core)
        else:
            parts = [combine(after, [term], core) for term in terms]
            parts = [lax.psum_scatter(v, "g", scatter_dimension=0, tiled=True) for v in parts]
            part = jnp.concatenate(parts, 0)
        return part.reshape(-1, plane_rows // 2, model)

    tables = [slots_of(slot_here[chunk : chunk + 1]) for chunk in range(2)]
    acts, hiddens, signals, inputs, grads, results = [], [], [], [], [], []
    gate_grads, backs = [], []

    def enter_chunk(chunk, after):
        act, hid, sig, erow, egrad, egate = moe_in(
            after, expert_id,
            chunk_rows[chunk], chunk_grads[chunk], shared_in, shared_dn, tables[chunk],
            experts, own, capacity,
        )
        signals.append(sig.reshape(-1, blocks))
        acts.append(act)
        hiddens.append(hid)
        return erow, egrad, egate

    def run_chunk(chunk, after, erow, egrad, egate):
        back, out, dgu, ehid, ggate = run_expert(after, erow, egrad, egate, w_gu, w_down)
        chosen = tables[chunk] == jnp.arange(capacity, dtype=jnp.int32)[None, :, None]
        ggate = ggate.reshape(-1, capacity, 1)
        gate_grads.append(jnp.sum(jnp.where(chosen, ggate, 0.0), axis=1))
        inputs.append((dgu, erow))
        grads.append((ehid, egrad))
        results.append(out)
        backs.append(back)

    def grad_term(chunk):
        return [(acts[chunk], shared_in, tables[chunk], backs[chunk])]

    def moe_term(chunk):
        return [(hiddens[chunk], shared_dn, tables[chunk], results[chunk])]

    grad_pairs, grad_plane, _ = slot_pair(
        hold(jnp.stack(grad_crossed[1:]), tick(near_rows[0])), (far_pairs[0],)
    )
    entered = enter_chunk(0, (far_pairs[0], grad_pairs[0]))
    far_rows = far_plane((acts[0],))
    chunk_rows.append(whole_slots(far_rows))
    run_chunk(0, (), *entered)
    far_grads = grad_plane((backs[0],))
    chunk_grads.append(whole_slots(far_grads))
    send = core_part((far_rows[0],), grad_term(0), 1)
    keep = core_part((send, far_grads[0]), grad_term(0), 0)
    near_steps = scatter_core(keep, send, ())
    run_chunk(1, (), *enter_chunk(1, (near_steps[0],)))
    near_steps = scatter_pair(near_steps, ())
    send = core_part((near_steps[0],), grad_term(1), 1)
    keep = core_part((send,), grad_term(1), 0)
    near_total = scatter_last(near_steps, ())
    near_cross = cross(near_total[1].astype(BF16), 1)

    far_steps = scatter_core(keep, send, (near_total,))
    moe_terms = moe_term(0) + moe_term(1)
    moe_send = core_part((far_steps[0],), moe_terms, 1)
    moe_keep = core_part((moe_send,), moe_terms, 0)
    signals = jnp.stack([jnp.stack(gate_grads), jnp.stack(signals)])
    signals = signals.reshape(2, 2, 2, groups, 2, 2, 2, 2, rows_here // 2)
    for dim, index in ((1, z // 2), (2, c), (4, z % 2), (5, y), (7, x)):
        signals = flip(signals, index, dim)
    signals = signals.transpose(3, 1, 4, 5, 2, 7, 0, 6, 8).reshape(2 * shares, 2, rows_here)
    far_steps = scatter_pair(far_steps, (moe_keep,))
    moe_steps = scatter_core(moe_keep, moe_send, (far_steps[0],))
    far_total = scatter_last(far_steps, (moe_steps[0],))
    far_cross = [cross(far_total[k].astype(BF16), 2 + k) for k in range(2)]

    tiles = range(2)
    shared_time = (far_total,)
    grad_sgu = weight_sum(
        shared_time,
        [
            (acts[chunk][None], core * groups, chunk_rows[chunk][core], 1, 0)
            for chunk in tiles
            for core in tiles
        ],
        plane_rows,
        groups,
        BF16,
    )[0]
    grad_sdn = weight_sum(
        shared_time,
        [
            (hiddens[chunk][None], core * groups, chunk_grads[chunk][core], 1, 0)
            for chunk in tiles
            for core in tiles
        ],
        plane_rows,
        groups,
        BF16,
    )[0]
    grad_normed = near_total[0] + near_cross.astype(F32)
    grad_normed = grad_normed + far_cross[0].astype(F32) + far_cross[1].astype(F32)
    grad_normed = hold(grad_normed, tick(grad_sgu) + tick(grad_sdn) + tick(moe_steps[1]))
    shared_grad = jnp.concatenate(
        [grad_sgu[:own], grad_sgu[held : held + own], grad_sdn[:own]], 0
    )
    shared_grad = shared_grad.reshape(3 * own, shares, weight_rows).transpose(1, 0, 2)
    shared_grad = exchange(shared_grad, everywhere)
    shared_grad_sent = shared_grad
    shared_grad = shared_grad.reshape(shares, 3, own, weight_rows).transpose(1, 0, 2, 3)
    shared_grad = shared_grad.reshape(3, shared_cols, weight_rows).astype(F32)
    grad_sgu = shared_grad[:2].transpose(0, 2, 1)

    signals = exchange(hold(signals, tick(far_total)), EVERY)
    signals = signals.reshape(experts, 2, 2, rows_here)
    grad_router_probs = jnp.sum(signals[:, :, 0], axis=1).T
    gate_signal = jnp.sum(signals[:, :, 1], axis=(0, 1))

    own_logits = jnp.dot(own_moe, router_weight, preferred_element_type=F32)
    router_probs = jax.nn.softmax(own_logits, axis=-1)
    grad_logits = router_probs * (
        grad_router_probs - jnp.sum(router_probs * grad_router_probs, axis=-1, keepdims=True)
    )
    grad_normed = (
        grad_normed
        + gate_signal[:, None] * shared_gate_vec.astype(F32)[None, :]
        + jnp.einsum("te,de->td", grad_logits, router_weight.astype(F32))
    )
    own_float = own_moe.astype(F32)
    grad_router = jnp.einsum("td,te->ed", own_float, grad_logits)
    grad_gate_vec = jnp.sum(gate_signal[:, None] * own_float, axis=0)
    grad_gain_moe = jnp.sum(grad_normed * (middle * scale_moe), axis=0)
    grad_middle = cotangent.astype(F32) + norm_back(middle, scale_moe, gain_moe, grad_normed)
    grad_attn = grad_middle.astype(BF16)

    pairs, plane, _ = slot_pair(grad_attn[None], ())
    moe_steps = scatter_pair(moe_steps, (pairs[0],))
    plane_grad, grad_attended = project((), order_one, plane((moe_steps[0],)), w_out)
    moe_parts = scatter_last(moe_steps, (grad_attended,))
    moe_cross = [cross(moe_parts[k].astype(BF16), k) for k in range(1, LINE)]

    def weight_grad(left, right):
        return lax.dot_general(left, right, (((0,), (0,)), ((), ())), preferred_element_type=F32)

    def to_weight_owners(value):
        if groups > 1:
            value = lax.psum_scatter(value, "g", scatter_dimension=0, tiled=True)
        value, mark = scatter_line(value)
        return exchange(value.reshape(4, weight_rows, -1), ("y", "c")).astype(F32), mark

    grad_out = weight_grad(plane_grad, attended).astype(BF16)
    grad_projected = attend_back(
        (grad_out, shared_grad_sent, moe_parts),
        projected, grad_attended, seg_q, seg_k, valid_k, cosine, sine,
    )
    grad_qkv = weight_grad(own_rows, grad_projected).astype(BF16)
    grad_out, out_marks = to_weight_owners(grad_out)
    grad_out = grad_out.transpose(1, 0, 2).reshape(weight_rows, local_cols).T
    tile = inputs[0][1].shape[0]
    grad_egu = weight_sum(
        (grad_projected,), [(left, 0, right, 1, 0) for left, right in inputs], tile, 1, F32
    )
    grad_qkv, qkv_marks = to_weight_owners(grad_qkv)
    grad_edown = weight_sum(
        (grad_egu,), [(left[None], 0, right, 1, 0) for left, right in grads], tile, 1, F32
    )
    grad_qkv = grad_qkv.reshape(4, weight_rows, 3, cols).transpose(2, 1, 0, 3)
    grad_qkv = grad_qkv.reshape(3, weight_rows, local_cols)
    w_qkv_t = w_qkv.T
    send, sum_send = spread(
        (qkv_marks[0], out_marks[1]),
        order_two, grad_projected, w_qkv_t, 1, rows_attn[1],
    )
    keep, sum_keep = spread((send, grad_egu, qkv_marks[3]), order_two, grad_projected, w_qkv_t, 0, rows_attn[0])
    gain_sum = (sum_send + sum_keep)[0] / gain_attn
    bias_sum = jnp.sum(grad_projected.astype(F32), axis=0).reshape(3, cols)
    grad_bias = lax.dynamic_update_slice_in_dim(jnp.zeros((3, model), F32), bias_sum, here, 1)

    valid_rows = lax.dynamic_slice_in_dim(valid_mask, x * rows_here, rows_here, 0).astype(F32)
    output, squares = finish(
        (grad_projected,), hidden_in, attn_rows, valid_rows[:, None], [moe_parts[0]] + moe_cross
    )

    sums_of_all = all_sum(
        jnp.concatenate(
            [
                grad_router,
                grad_gate_vec[None],
                grad_gain_moe[None],
                hold(gain_sum[None], tick(grad_edown) + tick(grad_sgu)),
                grad_bias,
                jnp.pad(squares, ((0, 0), (0, model - 4))),
            ],
            0,
        )
    )
    back_both, _ = slot_scatter(
        keep, send, (), (qkv_marks[2], out_marks[2], grad_edown), ()
    )
    back_own = back_both[1] + lax.ppermute(back_both[0].astype(BF16), "z", behind).astype(F32)
    input_grad = grad_middle + norm_back(residual, scale_attn, gain_attn, back_own)
    others = sums_of_all[experts:]
    root_means = jnp.sqrt(others[6, :3] / (jnp.maximum(others[6, 3], 1.0) * model))
    return (
        output,
        input_grad,
        jnp.stack([others[2], others[1]]),
        grad_qkv,
        others[3:6],
        grad_out,
        sums_of_all[:experts].T,
        others[0],
        grad_sgu,
        shared_grad[2],
        grad_egu.transpose(0, 2, 1)[None],
        grad_edown,
        root_means[0],
        root_means[1],
        root_means[2],
    )


def solution(mesh):
    dp, mp = mesh.shape["dp"], mesh.shape["mp"]
    inner = Mesh(mesh.devices.reshape(dp // (4 * LINE), LINE, 2, 2, mp), EVERY)
    d = ("g",) + GROUP
    placed = (
        P(EVERY, None),
        P(EVERY, None),
        P(),
        P(None, d, "x"),
        P(),
        P("x", d),
        P(),
        P(),
        P(None, d, "x"),
        P("x", d),
        P(d, None, None, "x"),
        P(d, "x", None),
        P(d),
        P(d),
        P(d, None),
        P(d, None),
    )
    return jax.shard_map(
        per_device,
        mesh=inner,
        in_specs=placed,
        out_specs=(
            P(EVERY, None),
            P(EVERY, None),
            P(),
            P(None, d, "x"),
            P(),
            P("x", d),
            P(),
            P(),
            P(None, d, "x"),
            P("x", d),
            P(d, None, None, "x"),
            P(d, "x", None),
            P(),
            P(),
            P(),
        ),
        check_vma=False,
    )
```
